32 devices in a mesh: groups: 2 (over y), row: 4 (over x, core), col: 4 (over z).
Axes of the slice: x: 2, y: 2, z: 4, core: 2. Of those that a mesh axis runs over, the one named last changes fastest.
Arguments:
- inputs: bfloat16 [1536, 4096], P(('groups', 'col'), 'row'), parts along dimension 0, may hold values from -6 to 6
- cotangent: bfloat16 [1536, 4096], P(('groups', 'col'), 'row'), parts along dimension 0, may hold values from -6 to 6
- preactivation: bfloat16 [1536, 8192], P(('groups', 'row'), 'col'), parts along dimension 0, may hold values from -8 to 8
- up_weight: bfloat16 [4096, 8192], P('row', 'col'), may hold values from -0.09375 to 0.09375
- down_weight: bfloat16 [8192, 4096], P('col', 'row'), may hold values from -0.0625 to 0.0625
Outputs:
- grad_input: bfloat16 [1536, 4096], P(('groups', 'col'), 'row'), parts along dimension 0
- grad_up: float32 [8192, 8192], P(('groups', 'row'), 'col'), parts along dimension 0
- grad_down: float32 [16384, 4096], P(('groups', 'col'), 'row'), parts along dimension 0
The draws below stay inside these ranges and needn't reach their ends.
There are 2 independent parts, one for each index of `groups`. The reference program is written for one: setup_inputs(seed, part) draws one part's arguments, and reference() takes and returns one part's arrays. A program takes and returns all parts, laid end to end along the dimension named above; an argument that names none is the same for every part. Nothing has to cross between parts.
All inputs are finite; a program needn't handle non-finite values.
Results may differ from the reference program's by a relative error of at most 0.0049.
Values may be sent and summed in bfloat16 or wider, within the bound.
No kernel may reach another device: no remote copies, remote signals or barrier semaphores. Data moves between devices by JAX's collectives and lax.ppermute only.
A program may use at most 128 MiB of HBM per device.

```python
import jax
import jax.numpy as jnp

D = 4096
H = 8192
TOKENS = 768


def block_scale(key, extent, cuts, smallest, top_value):
    level, own = 1.0, jax.random.fold_in(key, 6)
    for axis_at, blocks in cuts:
        draws = jnp.exp(jax.random.uniform(jax.random.fold_in(own, axis_at), (blocks,), jnp.float32, smallest / len(cuts), top_value / len(cuts)))
        level = level * jnp.repeat(draws, extent[axis_at] // blocks).reshape([-1 if axis == axis_at else 1 for axis in range(len(extent))])
    return level


def scatter_about(own_key, shape, deviation, reach, pieces=(), dtype=jnp.bfloat16):
    result = jax.random.normal(own_key, shape, jnp.float32) * deviation
    if len(pieces) > 0:
        result = block_scale(own_key, shape, pieces, -0.22, 0.18) * result
    return jnp.clip(result, min=-reach, max=reach).astype(dtype)


def setup_inputs(seed: int = 0, part: int = 0) -> dict:
    key_list = jax.random.split(jax.random.key(seed), 6)
    part_keys = jax.random.split(jax.random.fold_in(key_list[5], part), 6)
    return {
        "inputs": scatter_about(part_keys[0], (TOKENS, D), 1.0, 6.0, ((0, 4), (1, 4))),
        "cotangent": scatter_about(part_keys[1], (TOKENS, D), 1.0, 6.0, ((0, 4), (1, 4))),
        "preactivation": scatter_about(part_keys[2], (TOKENS, H), 1.5, 8.0, ((0, 4), (1, 4))),
        "up_weight": scatter_about(key_list[3], (D, H), D ** -0.5, 0.09375, ((0, 4), (1, 4))),
        "down_weight": scatter_about(key_list[4], (H, D), H ** -0.5, 0.0625, ((0, 4), (1, 4))),
    }


def gelu_pair(values):
    v = values.astype(jnp.float32)
    tanh_arg = 0.7978845608 * (v + 0.044715 * v * v * v)
    tanh_val = jnp.tanh(tanh_arg)
    gelu_value = 0.5 * v * (1.0 + tanh_val)
    gelu_slope = 0.5 * (1.0 + tanh_val) + 0.5 * v * (1.0 - tanh_val * tanh_val) * 0.7978845608 * (1.0 + 3.0 * 0.044715 * v * v)
    return gelu_value, gelu_slope


def reference(inputs, cotangent, preactivation, up_weight, down_weight):
    hidden_grad = jnp.dot(cotangent, down_weight.T, preferred_element_type=jnp.float32)
    gelu_value, gelu_slope = gelu_pair(preactivation)
    activation = gelu_value.astype(jnp.bfloat16)
    pre_grad = (hidden_grad * gelu_slope).astype(jnp.bfloat16)
    grad_input = jnp.dot(pre_grad, up_weight.T, preferred_element_type=jnp.float32).astype(jnp.bfloat16)
    token_scale = 1.0 / (TOKENS ** 0.5)
    grad_up = jnp.dot(inputs.T, pre_grad, preferred_element_type=jnp.float32) * token_scale
    grad_down = jnp.dot(activation.T, cotangent, preferred_element_type=jnp.float32) * token_scale
    return grad_input, grad_up, grad_down
```

```python
import math

import jax
import jax.numpy as jnp
from jax import lax
from jax.sharding import PartitionSpec as P

LAST = (((1,), (1,)), ((), ()))
FIRST = (((0,), (0,)), ((), ()))


def gelu_parts(values):
    v = values.astype(jnp.float32)
    tanh_val = jnp.tanh(0.7978845608 * (v + 0.044715 * v * v * v))
    return v, tanh_val


def gelu(values):
    v, tanh_val = gelu_parts(values)
    return 0.5 * v * (1.0 + tanh_val)


def gelu_slope(values):
    v, tanh_val = gelu_parts(values)
    return 0.5 * (1.0 + tanh_val) + 0.5 * v * (1.0 - tanh_val * tanh_val) * 0.7978845608 * (
        1.0 + 3.0 * 0.044715 * v * v
    )


def dot(a, b, dims):
    return lax.dot_general(a, b, dims, preferred_element_type=jnp.float32)


def per_device(inputs, cotangent, preactivation, up_weight, down_weight):
    cols, rows = lax.axis_size("col"), lax.axis_size("row")
    z, r = lax.axis_index("col"), lax.axis_index("row")
    core = lax.rem(r, 2)
    tokens, features = cotangent.shape
    hidden = down_weight.shape[0]
    half = hidden // 2
    ring = [(i, (i + 1) % cols) for i in range(cols)]
    pair = [(i, i ^ 1) for i in range(rows)]
    total_tokens = tokens * cols
    token_scale = 1.0 / math.sqrt(total_tokens)

    pre_all = lax.all_gather(preactivation, "row", axis=0, tiled=True)

    down_mine = lax.dynamic_slice(down_weight, (core * half, 0), (half, features))
    down_other = lax.dynamic_slice(down_weight, ((1 - core) * half, 0), (half, features))
    down_pair = lax.ppermute(down_other, "row", pair)
    up_mine = lax.dynamic_slice(up_weight, (0, core * half), (features, half))
    up_other = lax.dynamic_slice(up_weight, (0, (1 - core) * half), (features, half))

    cots = [cotangent]
    for _ in range(cols - 1):
        cots.append(lax.ppermute(cots[-1], "col", ring))
    inputs_all = lax.all_gather(inputs, "col", axis=0, tiled=True)

    order = list(range(1, cols)) + [0]
    sums = None
    pre_grad_all = jnp.zeros((total_tokens, hidden), jnp.bfloat16)
    cot_all = jnp.zeros((total_tokens, features), jnp.bfloat16)
    for s in order:
        at = lax.rem(z - s + cols, cols) * tokens
        cot = cots[s]
        cot_all = lax.dynamic_update_slice(cot_all, cot, (at, 0))
        cot_pair = lax.ppermute(cot, "row", pair)
        part = dot(cot, down_mine, LAST) + dot(cot_pair, down_pair, LAST)
        sent = part.astype(jnp.bfloat16)
        for shift in range(2, rows, 2):
            part = part + lax.ppermute(
                sent, "row", [(i, (i + shift) % rows) for i in range(rows)]
            ).astype(jnp.float32)
        v = lax.dynamic_slice(pre_all, (at, core * half), (tokens, half))
        pre_grad = (part * gelu_slope(v)).astype(jnp.bfloat16)
        pre_grad_pair = lax.ppermute(pre_grad, "row", pair)
        pre_grad_all = lax.dynamic_update_slice(pre_grad_all, pre_grad, (at, core * half))
        pre_grad_all = lax.dynamic_update_slice(
            pre_grad_all, pre_grad_pair, (at, (1 - core) * half)
        )
        share = dot(pre_grad, up_mine, LAST) + dot(pre_grad_pair, up_other, LAST)
        if sums is not None:
            share = share + lax.ppermute(sums, "col", ring).astype(jnp.float32)
        sums = share.astype(jnp.bfloat16)
    activation = gelu(pre_all).astype(jnp.bfloat16)
    grad_down = dot(activation, cot_all, FIRST) * token_scale
    grad_up = dot(inputs_all, pre_grad_all, FIRST) * token_scale
    return (sums, grad_up, grad_down)


def solution(mesh):
    placed = (
        P(("groups", "col"), "row"),
        P(("groups", "col"), "row"),
        P(("groups", "row"), "col"),
        P("row", "col"),
        P("col", "row"),
    )
    return jax.shard_map(
        per_device,
        mesh=mesh,
        in_specs=placed,
        out_specs=(
            P(("groups", "col"), "row"),
            P(("groups", "row"), "col"),
            P(("groups", "col"), "row"),
        ),
        check_vma=False,
    )
```

```python
import functools
import math

import jax
import jax.numpy as jnp
from jax import lax
from jax.experimental import pallas as pl
from jax.experimental.pallas import tpu as pltpu
from jax.sharding import PartitionSpec as P

LAST = (((1,), (1,)), ((), ()))
FIRST = (((0,), (0,)), ((), ()))
MIB = 1024 * 1024


def gelu_parts(values):
    v = values.astype(jnp.float32)
    tanh_val = jnp.tanh(0.7978845608 * (v + 0.044715 * v * v * v))
    return v, tanh_val


def gelu(values):
    v, tanh_val = gelu_parts(values)
    return 0.5 * v * (1.0 + tanh_val)


def gelu_slope(values):
    v, tanh_val = gelu_parts(values)
    return 0.5 * (1.0 + tanh_val) + 0.5 * v * (1.0 - tanh_val * tanh_val) * 0.7978845608 * (
        1.0 + 3.0 * 0.044715 * v * v
    )


def dot(a, b, dims):
    return lax.dot_general(a, b, dims, preferred_element_type=jnp.float32)


def tile_of(extent):
    return next(t for t in (256, 128, extent) if extent % t == 0)


def in_vmem():
    return pl.BlockSpec(memory_space=pltpu.VMEM)


def grad_down_kernel(blocks, scale, at_ref, pre_ref, *refs):
    cot_refs, out_ref, cots = refs[:blocks], refs[blocks], refs[blocks + 1]
    tokens = cot_refs[0].shape[0]

    @pl.when(pl.program_id(0) == 0)
    def _():
        for s in range(blocks):
            cots[pl.ds(pl.multiple_of(at_ref[s] * tokens, tokens), tokens), :] = cot_refs[s][...]

    activation = gelu(pre_ref[...]).astype(jnp.bfloat16)
    out_ref[...] = dot(activation, cots[...], FIRST) * scale


def grad_down_call(at, pre_all, cots, scale):
    total, hidden = pre_all.shape
    features = cots[0].shape[1]
    tile = tile_of(hidden)
    return pl.pallas_call(
        functools.partial(grad_down_kernel, len(cots), scale),
        out_shape=jax.ShapeDtypeStruct((hidden, features), jnp.float32),
        grid_spec=pltpu.PrefetchScalarGridSpec(
            num_scalar_prefetch=1,
            grid=(hidden // tile,),
            in_specs=[pl.BlockSpec((total, tile), lambda i, at: (0, i))]
            + [in_vmem() for _ in cots],
            out_specs=pl.BlockSpec((tile, features), lambda i, at: (i, 0)),
            scratch_shapes=[pltpu.VMEM((total, features), jnp.bfloat16)],
        ),
        compiler_params=pltpu.CompilerParams(vmem_limit_bytes=24 * MIB),
        cost_estimate=pl.CostEstimate(
            flops=2 * total * hidden * features,
            bytes_accessed=4 * hidden * features + 2 * total * (hidden + features),
            transcendentals=total * hidden,
        ),
    )(at, pre_all, *cots)


def grad_up_kernel(blocks, scale, at_ref, in_ref, *refs):
    mine, pair = refs[:blocks], refs[blocks : 2 * blocks]
    out_ref, grads = refs[2 * blocks], refs[2 * blocks + 1]
    tokens, half = mine[0].shape

    @pl.when(pl.program_id(0) == 0)
    def _():
        core = at_ref[blocks]
        left = pl.ds(pl.multiple_of(core * half, half), half)
        right = pl.ds(pl.multiple_of((1 - core) * half, half), half)
        for s in range(blocks):
            here = pl.ds(pl.multiple_of(at_ref[s] * tokens, tokens), tokens)
            grads[here, left] = mine[s][...]
            grads[here, right] = pair[s][...]

    out_ref[...] = dot(in_ref[...], grads[...], FIRST) * scale


def grad_up_call(at, inputs_all, mine, pair, scale):
    total, features = inputs_all.shape
    hidden = 2 * mine[0].shape[1]
    tile = tile_of(features)
    return pl.pallas_call(
        functools.partial(grad_up_kernel, len(mine), scale),
        out_shape=jax.ShapeDtypeStruct((features, hidden), jnp.float32),
        grid_spec=pltpu.PrefetchScalarGridSpec(
            num_scalar_prefetch=1,
            grid=(features // tile,),
            in_specs=[pl.BlockSpec((total, tile), lambda i, at: (0, i))]
            + [in_vmem() for _ in mine + pair],
            out_specs=pl.BlockSpec((tile, hidden), lambda i, at: (i, 0)),
            scratch_shapes=[pltpu.VMEM((total, hidden), jnp.bfloat16)],
        ),
        compiler_params=pltpu.CompilerParams(vmem_limit_bytes=24 * MIB),
        cost_estimate=pl.CostEstimate(
            flops=2 * total * hidden * features,
            bytes_accessed=4 * hidden * features + 2 * total * (hidden + features),
            transcendentals=0,
        ),
    )(at, inputs_all, *mine, *pair)


def pre_grad_kernel(at_ref, pre_ref, part_ref, *refs):
    out_ref = refs[-1]
    rows = 64
    for first in range(0, part_ref.shape[0], rows):
        here = pl.ds(first, rows)
        total = part_ref[here, :]
        for other in refs[:-1]:
            total = total + other[here, :].astype(jnp.float32)
        out_ref[here, :] = (total * gelu_slope(pre_ref[here, :])).astype(jnp.bfloat16)


def pre_grad_call(at, core, pre_all, part, others):
    tokens, half = part.shape
    return pl.pallas_call(
        pre_grad_kernel,
        out_shape=jax.ShapeDtypeStruct((tokens, half), jnp.bfloat16),
        grid_spec=pltpu.PrefetchScalarGridSpec(
            num_scalar_prefetch=1,
            grid=(1,),
            in_specs=[pl.BlockSpec((tokens, half), lambda i, at: (at[0], at[1]))]
            + [in_vmem() for _ in [part] + others],
            out_specs=in_vmem(),
        ),
        compiler_params=pltpu.CompilerParams(vmem_limit_bytes=8 * MIB),
        cost_estimate=pl.CostEstimate(
            flops=20 * tokens * half,
            bytes_accessed=10 * tokens * half,
            transcendentals=tokens * half,
        ),
    )(jnp.stack([at, core]).astype(jnp.int32), pre_all, part, *others)


def per_device(inputs, cotangent, preactivation, up_weight, down_weight):
    cols, rows = lax.axis_size("col"), lax.axis_size("row")
    z, r = lax.axis_index("col"), lax.axis_index("row")
    core = lax.rem(r, 2)
    tokens, features = cotangent.shape
    hidden = down_weight.shape[0]
    half = hidden // 2
    ring = [(i, (i + 1) % cols) for i in range(cols)]
    pair = [(i, i ^ 1) for i in range(rows)]
    scale = 1.0 / math.sqrt(tokens * cols)
    at = jnp.stack([lax.rem(z - s + cols, cols) for s in range(cols)] + [core]).astype(jnp.int32)

    pre_all = lax.all_gather(preactivation, "row", axis=0, tiled=True)

    down_mine = lax.dynamic_slice(down_weight, (core * half, 0), (half, features))
    down_other = lax.dynamic_slice(down_weight, ((1 - core) * half, 0), (half, features))
    up_mine = lax.dynamic_slice(up_weight, (0, core * half), (features, half))
    up_other = lax.dynamic_slice(up_weight, (0, (1 - core) * half), (features, half))

    cots, parts, sent = [cotangent], [None] * cols, [None] * cols

    def hidden_part(s):
        cot_pair = lax.ppermute(cots[s], "row", pair)
        parts[s] = dot(cots[s], down_mine, LAST) + dot(cot_pair, down_pair, LAST)
        sent[s] = parts[s].astype(jnp.bfloat16)

    arriving = lax.ppermute(cotangent, "col", ring)
    down_pair = lax.ppermute(down_other, "row", pair)
    for s in range(cols):
        hidden_part(s)
        if s < cols - 1:
            arriving, _ = lax.optimization_barrier((arriving, sent[s]))
            cots.append(arriving)
        if s < cols - 2:
            arriving = lax.ppermute(arriving, "col", ring)
    inputs_all = lax.all_gather(inputs, "col", axis=0, tiled=True)

    sums, mine, theirs = None, [None] * cols, [None] * cols
    for s in list(range(1, cols)) + [0]:
        others = [
            lax.ppermute(sent[s], "row", [(i, (i + shift) % rows) for i in range(rows)])
            for shift in range(2, rows, 2)
        ]
        mine[s] = pre_grad_call(at[s], core, pre_all, parts[s], others)
        theirs[s] = lax.ppermute(mine[s], "row", pair)
        share = dot(mine[s], up_mine, LAST) + dot(theirs[s], up_other, LAST)
        if sums is not None:
            share = share + lax.ppermute(sums, "col", ring).astype(jnp.float32)
        sums = share.astype(jnp.bfloat16)
    grad_down = grad_down_call(at, pre_all, cots, scale)
    grad_up = grad_up_call(at, inputs_all, mine, theirs, scale)
    return (sums, grad_up, grad_down)


def solution(mesh):
    placed = (
        P(("groups", "col"), "row"),
        P(("groups", "col"), "row"),
        P(("groups", "row"), "col"),
        P("row", "col"),
        P("col", "row"),
    )
    return jax.shard_map(
        per_device,
        mesh=mesh,
        in_specs=placed,
        out_specs=(
            P(("groups", "col"), "row"),
            P(("groups", "row"), "col"),
            P(("groups", "col"), "row"),
        ),
        check_vma=False,
    )
```

```python
import functools
import math

import jax
import jax.numpy as jnp
from jax import lax
from jax.experimental import pallas as pl
from jax.experimental.pallas import tpu as pltpu
from jax.sharding import PartitionSpec as P

LAST = (((1,), (1,)), ((), ()))
FIRST = (((0,), (0,)), ((), ()))
MIB = 1024 * 1024


def gelu_parts(values):
    v = values.astype(jnp.float32)
    tanh_val = jnp.tanh(0.7978845608 * (v + 0.044715 * v * v * v))
    return v, tanh_val


def gelu(values):
    v, tanh_val = gelu_parts(values)
    return 0.5 * v * (1.0 + tanh_val)


def gelu_slope(values):
    v, tanh_val = gelu_parts(values)
    return 0.5 * (1.0 + tanh_val) + 0.5 * v * (1.0 - tanh_val * tanh_val) * 0.7978845608 * (
        1.0 + 3.0 * 0.044715 * v * v
    )


def dot(a, b, dims):
    return lax.dot_general(a, b, dims, preferred_element_type=jnp.float32)


def after(value, *first):
    return lax.optimization_barrier((value, *first))[0]


def tile_of(extent):
    return next(t for t in (256, 128, extent) if extent % t == 0)


def in_vmem():
    return pl.BlockSpec(memory_space=pltpu.VMEM)


def grad_down_kernel(blocks, scale, at_ref, pre_ref, *refs):
    cot_refs, out_ref, cots = refs[:blocks], refs[blocks], refs[blocks + 1]
    tokens = cot_refs[0].shape[0]

    @pl.when(pl.program_id(0) == 0)
    def _():
        for s in range(blocks):
            cots[pl.ds(pl.multiple_of(at_ref[s] * tokens, tokens), tokens), :] = cot_refs[s][...]

    activation = gelu(pre_ref[...]).astype(jnp.bfloat16)
    out_ref[...] = dot(activation, cots[...], FIRST) * scale


def grad_down_call(at, pre_all, cots, scale):
    total, hidden = pre_all.shape
    features = cots[0].shape[1]
    tile = tile_of(hidden)
    return pl.pallas_call(
        functools.partial(grad_down_kernel, len(cots), scale),
        out_shape=jax.ShapeDtypeStruct((hidden, features), jnp.float32),
        grid_spec=pltpu.PrefetchScalarGridSpec(
            num_scalar_prefetch=1,
            grid=(hidden // tile,),
            in_specs=[pl.BlockSpec((total, tile), lambda i, at: (0, i))]
            + [in_vmem() for _ in cots],
            out_specs=pl.BlockSpec((tile, features), lambda i, at: (i, 0)),
            scratch_shapes=[pltpu.VMEM((total, features), jnp.bfloat16)],
        ),
        compiler_params=pltpu.CompilerParams(vmem_limit_bytes=24 * MIB),
        cost_estimate=pl.CostEstimate(
            flops=2 * total * hidden * features,
            bytes_accessed=4 * hidden * features + 2 * total * (hidden + features),
            transcendentals=total * hidden,
        ),
    )(at, pre_all, *cots)


def grad_up_kernel(blocks, scale, at_ref, in_ref, *refs):
    mine, pair = refs[:blocks], refs[blocks : 2 * blocks]
    out_ref, grads = refs[2 * blocks], refs[2 * blocks + 1]
    tokens, half = mine[0].shape

    @pl.when(pl.program_id(0) == 0)
    def _():
        core = at_ref[blocks]
        left = pl.ds(pl.multiple_of(core * half, half), half)
        right = pl.ds(pl.multiple_of((1 - core) * half, half), half)
        for s in range(blocks):
            here = pl.ds(pl.multiple_of(at_ref[s] * tokens, tokens), tokens)
            grads[here, left] = mine[s][...]
            grads[here, right] = pair[s][...]

    out_ref[...] = dot(in_ref[...], grads[...], FIRST) * scale


def grad_up_call(at, inputs_all, mine, pair, scale):
    total, features = inputs_all.shape
    hidden = 2 * mine[0].shape[1]
    tile = tile_of(features)
    return pl.pallas_call(
        functools.partial(grad_up_kernel, len(mine), scale),
        out_shape=jax.ShapeDtypeStruct((features, hidden), jnp.float32),
        grid_spec=pltpu.PrefetchScalarGridSpec(
            num_scalar_prefetch=1,
            grid=(features // tile,),
            in_specs=[pl.BlockSpec((total, tile), lambda i, at: (0, i))]
            + [in_vmem() for _ in mine + pair],
            out_specs=pl.BlockSpec((tile, hidden), lambda i, at: (i, 0)),
            scratch_shapes=[pltpu.VMEM((total, hidden), jnp.bfloat16)],
        ),
        compiler_params=pltpu.CompilerParams(vmem_limit_bytes=24 * MIB),
        cost_estimate=pl.CostEstimate(
            flops=2 * total * hidden * features,
            bytes_accessed=4 * hidden * features + 2 * total * (hidden + features),
            transcendentals=0,
        ),
    )(at, inputs_all, *mine, *pair)


def pre_grad_kernel(at_ref, pre_ref, part_ref, *refs):
    out_ref = refs[-1]
    rows = 64
    for first in range(0, part_ref.shape[0], rows):
        here = pl.ds(first, rows)
        total = part_ref[here, :]
        for other in refs[:-1]:
            total = total + other[here, :].astype(jnp.float32)
        out_ref[here, :] = (total * gelu_slope(pre_ref[here, :])).astype(jnp.bfloat16)


def pre_grad_call(at, core, pre_all, part, others):
    tokens, half = part.shape
    return pl.pallas_call(
        pre_grad_kernel,
        out_shape=jax.ShapeDtypeStruct((tokens, half), jnp.bfloat16),
        grid_spec=pltpu.PrefetchScalarGridSpec(
            num_scalar_prefetch=1,
            grid=(1,),
            in_specs=[pl.BlockSpec((tokens, half), lambda i, at: (at[0], at[1]))]
            + [in_vmem() for _ in [part] + others],
            out_specs=in_vmem(),
        ),
        compiler_params=pltpu.CompilerParams(vmem_limit_bytes=8 * MIB),
        cost_estimate=pl.CostEstimate(
            flops=20 * tokens * half,
            bytes_accessed=10 * tokens * half,
            transcendentals=tokens * half,
        ),
    )(jnp.stack([at, core]).astype(jnp.int32), pre_all, part, *others)


def per_device(inputs, cotangent, preactivation, up_weight, down_weight):
    cols, rows = lax.axis_size("col"), lax.axis_size("row")
    z, r = lax.axis_index("col"), lax.axis_index("row")
    core = lax.rem(r, 2)
    tokens, features = cotangent.shape
    hidden = down_weight.shape[0]
    half = hidden // 2
    ring = [(i, (i + 1) % cols) for i in range(cols)]
    pair = [(i, i ^ 1) for i in range(rows)]
    scale = 1.0 / math.sqrt(tokens * cols)
    at = jnp.stack([lax.rem(z - s + cols, cols) for s in range(cols)] + [core]).astype(jnp.int32)

    pre_all = lax.all_gather(preactivation, "row", axis=0, tiled=True)

    down_pair = lax.ppermute(down_weight, "row", pair)
    down_mine = lax.dynamic_slice(down_weight, (core * half, 0), (half, features))
    down_pair = lax.dynamic_slice(down_pair, (core * half, 0), (half, features))
    up_mine = lax.dynamic_slice(up_weight, (0, core * half), (features, half))
    up_other = lax.dynamic_slice(up_weight, (0, (1 - core) * half), (features, half))

    parts, others, mine, theirs = ([None] * cols for _ in range(4))

    def hidden_part(s, cot, first):
        cot_pair = lax.ppermute(after(cot, *first), "row", pair)
        parts[s] = dot(cot, down_mine, LAST) + dot(cot_pair, down_pair, LAST)
        sent = parts[s].astype(jnp.bfloat16)
        others[s] = [
            lax.ppermute(sent, "row", [(i, (i + shift) % rows) for i in range(rows)])
            for shift in range(2, rows, 2)
        ]
        return sent

    def pre_grad(s, first):
        others[s][0] = after(others[s][0], *first)
        mine[s] = pre_grad_call(at[s], core, pre_all, parts[s], others[s])
        theirs[s] = lax.ppermute(mine[s], "row", pair)

    def share(s, first):
        return dot(after(mine[s], *first), up_mine, LAST) + dot(theirs[s], up_other, LAST)

    cots = [cotangent]
    sent = hidden_part(0, cotangent, [])
    arriving = lax.ppermute(cotangent, "col", ring)
    for s in range(1, cols):
        first = [sent]
        if s == cols - 1:
            pre_grad(1, [sent])
            first = [sent, mine[1]]
        cots.append(after(arriving, *first))
        if s < cols - 1:
            arriving = lax.ppermute(cots[s], "col", ring)
        sent = hidden_part(s, cots[s], others[s - 2] if s >= 2 else [])
    inputs_all = lax.all_gather(inputs, "col", axis=0, tiled=True)

    sums = share(1, []).astype(jnp.bfloat16)
    grad_down = grad_down_call(after(at, sums), pre_all, cots, scale)
    for s in range(2, cols):
        pre_grad(s, [sums, sent])
        if s == cols - 1:
            pre_grad(0, [mine[s]])
        arrived = lax.ppermute(sums, "col", ring)
        first = [grad_down] if s == 2 else []
        sums = (share(s, first) + arrived.astype(jnp.float32)).astype(jnp.bfloat16)
    arrived = lax.ppermute(sums, "col", ring)
    grad_up = grad_up_call(after(at, sums), inputs_all, mine, theirs, scale)
    sums = (share(0, [grad_up]) + arrived.astype(jnp.float32)).astype(jnp.bfloat16)
    return (sums, grad_up, grad_down)


def solution(mesh):
    placed = (
        P(("groups", "col"), "row"),
        P(("groups", "col"), "row"),
        P(("groups", "row"), "col"),
        P("row", "col"),
        P("col", "row"),
    )
    return jax.shard_map(
        per_device,
        mesh=mesh,
        in_specs=placed,
        out_specs=(
            P(("groups", "col"), "row"),
            P(("groups", "row"), "col"),
            P(("groups", "col"), "row"),
        ),
        check_vma=False,
    )
```

```python
import functools
import math

import jax
import jax.numpy as jnp
from jax import lax
from jax.experimental import pallas as pl
from jax.experimental.pallas import tpu as pltpu
from jax.sharding import PartitionSpec as P

LAST = (((1,), (1,)), ((), ()))
FIRST = (((0,), (0,)), ((), ()))
MIB = 1024 * 1024
LITTLE = pl.CostEstimate(flops=1024, bytes_accessed=1024, transcendentals=0)


def gelu_parts(values):
    v = values.astype(jnp.float32)
    tanh_val = jnp.tanh(0.7978845608 * (v + 0.044715 * v * v * v))
    return v, tanh_val


def gelu(values):
    v, tanh_val = gelu_parts(values)
    return 0.5 * v * (1.0 + tanh_val)


def gelu_slope(values):
    v, tanh_val = gelu_parts(values)
    return 0.5 * (1.0 + tanh_val) + 0.5 * v * (1.0 - tanh_val * tanh_val) * 0.7978845608 * (
        1.0 + 3.0 * 0.044715 * v * v
    )


def dot(a, b, dims):
    return lax.dot_general(a, b, dims, preferred_element_type=jnp.float32)


def after(value, *first):
    return lax.optimization_barrier((value, *first))[0]


def tile_of(extent):
    return next(t for t in (256, 128, extent) if extent % t == 0)


def in_vmem():
    return pl.BlockSpec(memory_space=pltpu.VMEM)


def grad_down_kernel(blocks, scale, at_ref, pre_ref, *refs):
    cot_refs, out_ref, cots = refs[:blocks], refs[-2], refs[-1]
    tokens = cot_refs[0].shape[0]

    @pl.when(pl.program_id(0) == 0)
    def _():
        for s in range(blocks):
            cots[pl.ds(pl.multiple_of(at_ref[s] * tokens, tokens), tokens), :] = cot_refs[s][...]

    activation = gelu(pre_ref[...]).astype(jnp.bfloat16)
    out_ref[...] = dot(activation, cots[...], FIRST) * scale


def grad_down_call(at, pre_all, cots, scale, second=None):
    total, hidden = pre_all.shape
    features = cots[0].shape[1]
    tile = tile_of(hidden // 2)
    steps = hidden // 2 // tile
    skip = 0 if second is None else steps
    rest = [] if second is None else [second]
    return pl.pallas_call(
        functools.partial(grad_down_kernel, len(cots), scale),
        out_shape=jax.ShapeDtypeStruct((hidden, features), jnp.float32),
        grid_spec=pltpu.PrefetchScalarGridSpec(
            num_scalar_prefetch=1,
            grid=(steps,),
            in_specs=[pl.BlockSpec((total, tile), lambda i, at: (0, i + skip))]
            + [in_vmem() for _ in cots]
            + [pl.BlockSpec(memory_space=pl.ANY) for _ in rest],
            out_specs=pl.BlockSpec((tile, features), lambda i, at: (i + skip, 0)),
            scratch_shapes=[pltpu.VMEM((total, features), jnp.bfloat16)],
        ),
        input_output_aliases={2 + len(cots): 0} if rest else {},
        compiler_params=pltpu.CompilerParams(vmem_limit_bytes=16 * MIB),
        cost_estimate=LITTLE,
    )(at, pre_all, *cots, *rest)


def grad_up_kernel(blocks, scale, at_ref, *refs):
    ins, mine, pair = (refs[i * blocks : (i + 1) * blocks] for i in range(3))
    out_ref, inputs, grads = refs[3 * blocks :]
    tokens, half = mine[0].shape
    tile = out_ref.shape[0]

    @pl.when(pl.program_id(0) == 0)
    def _():
        core = at_ref[blocks]
        left = pl.ds(pl.multiple_of(core * half, half), half)
        right = pl.ds(pl.multiple_of((1 - core) * half, half), half)
        for s in range(blocks):
            here = pl.ds(s * tokens, tokens)
            inputs[here, :] = ins[s][...]
            grads[here, left] = mine[s][...]
            grads[here, right] = pair[s][...]

    columns = pl.ds(pl.multiple_of(pl.program_id(0) * tile, tile), tile)
    out_ref[...] = dot(inputs[:, columns], grads[...], FIRST) * scale


def grad_up_call(at, ins, mine, pair, scale):
    tokens, features = ins[0].shape
    total = tokens * len(ins)
    hidden = 2 * mine[0].shape[1]
    tile = tile_of(features)
    return pl.pallas_call(
        functools.partial(grad_up_kernel, len(mine), scale),
        out_shape=jax.ShapeDtypeStruct((features, hidden), jnp.float32),
        grid_spec=pltpu.PrefetchScalarGridSpec(
            num_scalar_prefetch=1,
            grid=(features // tile,),
            in_specs=[in_vmem() for _ in ins + mine + pair],
            out_specs=pl.BlockSpec((tile, hidden), lambda i, at: (i, 0)),
            scratch_shapes=[
                pltpu.VMEM((total, features), jnp.bfloat16),
                pltpu.VMEM((total, hidden), jnp.bfloat16),
            ],
        ),
        compiler_params=pltpu.CompilerParams(vmem_limit_bytes=20 * MIB),
        cost_estimate=LITTLE,
    )(at, *ins, *mine, *pair)


def lay_out_kernel(at_ref, *refs):
    out_ref = refs[-1]
    tokens = refs[0].shape[0]
    for i, ref in enumerate(refs[:-1]):
        out_ref[pl.ds(pl.multiple_of(at_ref[i] * tokens, tokens), tokens), :] = ref[...]


def lay_out_call(places, blocks):
    tokens, hidden = blocks[0].shape
    return pl.pallas_call(
        lay_out_kernel,
        out_shape=jax.ShapeDtypeStruct((tokens * len(blocks), hidden), jnp.bfloat16),
        grid_spec=pltpu.PrefetchScalarGridSpec(
            num_scalar_prefetch=1,
            grid=(1,),
            in_specs=[in_vmem() for _ in blocks],
            out_specs=in_vmem(),
        ),
        compiler_params=pltpu.CompilerParams(vmem_limit_bytes=8 * MIB),
        cost_estimate=LITTLE,
    )(places, *blocks)


def pre_grad_kernel(at_ref, pre_ref, part_ref, *refs):
    out_ref = refs[-1]
    tokens, half = part_ref.shape
    rows = 64
    columns = pl.ds(pl.multiple_of(at_ref[1] * half, half), half)
    for first in range(0, tokens, rows):
        here = pl.ds(first, rows)
        total = part_ref[here, :]
        for other in refs[:-1]:
            total = total + other[here, :].astype(jnp.float32)
        place = pl.ds(pl.multiple_of(at_ref[0] * tokens + first, rows), rows)
        out_ref[here, :] = (total * gelu_slope(pre_ref[place, columns])).astype(jnp.bfloat16)


def pre_grad_call(at, core, pre_all, part, others):
    tokens, half = part.shape
    return pl.pallas_call(
        pre_grad_kernel,
        out_shape=jax.ShapeDtypeStruct((tokens, half), jnp.bfloat16),
        grid_spec=pltpu.PrefetchScalarGridSpec(
            num_scalar_prefetch=1,
            grid=(1,),
            in_specs=[in_vmem() for _ in [pre_all, part] + others],
            out_specs=in_vmem(),
        ),
        compiler_params=pltpu.CompilerParams(vmem_limit_bytes=8 * MIB),
        cost_estimate=LITTLE,
    )(jnp.stack([at, core]).astype(jnp.int32), pre_all, part, *others)


def hidden_kernel(core_ref, cot_ref, pair_ref, mine_ref, theirs_ref, part_ref, sent_ref):
    half = part_ref.shape[1]
    tile = tile_of(half)
    for first in range(0, half, tile):
        rows = pl.ds(pl.multiple_of(core_ref[0] * half + first, tile), tile)
        part = dot(cot_ref[...], mine_ref[rows, :], LAST)
        part = part + dot(pair_ref[...], theirs_ref[rows, :], LAST)
        part_ref[:, pl.ds(first, tile)] = part
        sent_ref[:, pl.ds(first, tile)] = part.astype(jnp.bfloat16)


def hidden_call(core, cot, cot_pair, down_mine, down_pair):
    shape = (cot.shape[0], down_mine.shape[0] // 2)
    return pl.pallas_call(
        hidden_kernel,
        out_shape=[
            jax.ShapeDtypeStruct(shape, jnp.float32),
            jax.ShapeDtypeStruct(shape, jnp.bfloat16),
        ],
        grid_spec=pltpu.PrefetchScalarGridSpec(
            num_scalar_prefetch=1,
            grid=(1,),
            in_specs=[in_vmem() for _ in range(4)],
            out_specs=[in_vmem(), in_vmem()],
        ),
        compiler_params=pltpu.CompilerParams(vmem_limit_bytes=20 * MIB),
        cost_estimate=LITTLE,
    )(core, cot, cot_pair, down_mine, down_pair)


def share_kernel(core_ref, mine_ref, theirs_ref, up_ref, *refs):
    out_ref = refs[-1]
    features, half = up_ref.shape[0], mine_ref.shape[1]
    tile = tile_of(features)
    left = pl.ds(pl.multiple_of(core_ref[0] * half, half), half)
    right = pl.ds(pl.multiple_of((1 - core_ref[0]) * half, half), half)
    for first in range(0, features, tile):
        here = pl.ds(first, tile)
        total = dot(mine_ref[...], up_ref[here, left], LAST)
        total = total + dot(theirs_ref[...], up_ref[here, right], LAST)
        for arrived in refs[:-1]:
            total = total + arrived[:, here].astype(jnp.float32)
        out_ref[:, here] = total.astype(jnp.bfloat16)


def share_call(core, mine, theirs, up_weight, arrived):
    return pl.pallas_call(
        share_kernel,
        out_shape=jax.ShapeDtypeStruct((mine.shape[0], up_weight.shape[0]), jnp.bfloat16),
        grid_spec=pltpu.PrefetchScalarGridSpec(
            num_scalar_prefetch=1,
            grid=(1,),
            in_specs=[in_vmem() for _ in [mine, theirs, up_weight] + arrived],
            out_specs=in_vmem(),
        ),
        compiler_params=pltpu.CompilerParams(vmem_limit_bytes=16 * MIB),
        cost_estimate=LITTLE,
    )(core, mine, theirs, up_weight, *arrived)


def per_device(inputs, cotangent, preactivation, up_weight, down_weight):
    cols, rows = lax.axis_size("col"), lax.axis_size("row")
    z, r = lax.axis_index("col"), lax.axis_index("row")
    core = lax.rem(r, 2)
    tokens, features = cotangent.shape
    hidden = down_weight.shape[0]
    half = hidden // 2
    ring = [(i, (i + 1) % cols) for i in range(cols)]
    pair = [(i, i ^ 1) for i in range(rows)]
    scale = 1.0 / math.sqrt(tokens * cols)
    at = jnp.stack([lax.rem(z - s + cols, cols) for s in range(cols)] + [core]).astype(jnp.int32)

    shifts = range(2, rows, 2)
    over_x = [[(i, (i + shift) % rows) for i in range(rows)] for shift in shifts]
    places = [r] + [lax.rem(r - shift + rows, rows) for shift in shifts]
    places = jnp.stack(places + [p + 1 - 2 * lax.rem(p, 2) for p in places]).astype(jnp.int32)
    pres = [preactivation] + [lax.ppermute(preactivation, "row", to) for to in over_x]

    down_pair = lax.ppermute(down_weight, "row", pair)
    parts, others, mine, theirs = ([None] * cols for _ in range(4))

    def hidden_part(s, cot, first):
        cot_pair = after(lax.ppermute(cot, "row", pair), *first)
        parts[s], sent = hidden_call(at[cols:], cot, cot_pair, down_weight, down_pair)
        if s != 0:
            exchange(s, sent)
        return sent

    def exchange(s, sent):
        others[s] = [lax.ppermute(sent, "row", to) for to in over_x]

    def pre_grad(s, first):
        others[s][0] = after(others[s][0], *first)
        mine[s] = pre_grad_call(at[s], core, pre_all, parts[s], others[s])
        theirs[s] = lax.ppermute(mine[s], "row", pair)

    def share(s, first, arrived):
        return share_call(at[cols:], after(mine[s], *first), theirs[s], up_weight, arrived)

    cots, ins = [cotangent], [inputs]
    sent = own = hidden_part(0, cotangent, [])
    arriving = lax.ppermute(cotangent, "col", ring)
    for s in range(1, cols):
        first = [sent]
        if s == cols - 1:
            pre_all = lay_out_call(after(places, sent), pres)
            pre_grad(1, [sent])
            first = [sent, mine[1]]
        cots.append(after(arriving, *first))
        sent = hidden_part(s, cots[s], pres[1:] if s == 1 else [])
        if s == 1:
            pres = pres + [lax.ppermute(after(p, cots[1]), "row", pair) for p in pres]
        if s < cols - 1:
            arriving = lax.ppermute(cots[s], "col", ring)
        else:
            ins.append(lax.ppermute(after(inputs, cots[cols - 2]), "col", ring))
    exchange(0, after(own, sent))

    sums = share(1, [ins[1]], [])
    grad_down = grad_down_call(after(at, sums, sent), pre_all, cots, scale)
    for s in range(2, cols):
        pre_grad(s, [sums, grad_down])
        if s == 2:
            grad_down = grad_down_call(after(at, mine[s]), pre_all, cots, scale, grad_down)
        if s == cols - 1:
            pre_grad(0, [mine[s]])
        arrived = lax.ppermute(sums, "col", ring)
        ins.append(lax.ppermute(ins[-1], "col", ring))
        first = [ins[-1]] + ([grad_down] if s == 2 else [])
        sums = share(s, first, [arrived])
    arrived = lax.ppermute(sums, "col", ring)
    grad_up = grad_up_call(after(at, sums), ins, mine, theirs, scale)
    sums = share(0, [grad_up], [arrived])
    return (sums, grad_up, grad_down)


def solution(mesh):
    placed = (
        P(("groups", "col"), "row"),
        P(("groups", "col"), "row"),
        P(("groups", "row"), "col"),
        P("row", "col"),
        P("col", "row"),
    )
    return jax.shard_map(
        per_device,
        mesh=mesh,
        in_specs=placed,
        out_specs=(
            P(("groups", "col"), "row"),
            P(("groups", "row"), "col"),
            P(("groups", "col"), "row"),
        ),
        check_vma=False,
    )
```

```python
import functools
import math

import jax
import jax.numpy as jnp
from jax import lax
from jax.experimental import pallas as pl
from jax.experimental.pallas import tpu as pltpu
from jax.sharding import PartitionSpec as P

LAST = (((1,), (1,)), ((), ()))
FIRST = (((0,), (0,)), ((), ()))
MIB = 1024 * 1024
LITTLE = pl.CostEstimate(flops=1024, bytes_accessed=1024, transcendentals=0)


def gelu_parts(values):
    v = values.astype(jnp.float32)
    tanh_val = jnp.tanh(0.7978845608 * (v + 0.044715 * v * v * v))
    return v, tanh_val


def gelu(values):
    v, tanh_val = gelu_parts(values)
    return 0.5 * v * (1.0 + tanh_val)


def gelu_slope(values):
    v, tanh_val = gelu_parts(values)
    return 0.5 * (1.0 + tanh_val) + 0.5 * v * (1.0 - tanh_val * tanh_val) * 0.7978845608 * (
        1.0 + 3.0 * 0.044715 * v * v
    )


def dot(a, b, dims):
    return lax.dot_general(a, b, dims, preferred_element_type=jnp.float32)


def after(value, *first):
    return lax.optimization_barrier((value, *first))[0]


def tile_of(extent):
    return next(t for t in (256, 128, extent) if extent % t == 0)


def in_vmem():
    return pl.BlockSpec(memory_space=pltpu.VMEM)


def grad_down_kernel(blocks, scale, at_ref, pre_ref, *refs):
    cot_refs, out_ref, cots = refs[:blocks], refs[-2], refs[-1]
    tokens = cot_refs[0].shape[0]

    @pl.when(pl.program_id(0) == 0)
    def _():
        for s in range(blocks):
            cots[pl.ds(pl.multiple_of(at_ref[s] * tokens, tokens), tokens), :] = cot_refs[s][...]

    activation = gelu(pre_ref[...]).astype(jnp.bfloat16)
    out_ref[...] = dot(activation, cots[...], FIRST) * scale


def grad_down_call(at, pre_all, cots, scale):
    total, hidden = pre_all.shape
    features = cots[0].shape[1]
    tile = tile_of(hidden)
    return pl.pallas_call(
        functools.partial(grad_down_kernel, len(cots), scale),
        out_shape=jax.ShapeDtypeStruct((hidden, features), jnp.float32),
        grid_spec=pltpu.PrefetchScalarGridSpec(
            num_scalar_prefetch=1,
            grid=(hidden // tile,),
            in_specs=[pl.BlockSpec((total, tile), lambda i, at: (0, i))]
            + [in_vmem() for _ in cots],
            out_specs=pl.BlockSpec((tile, features), lambda i, at: (i, 0)),
            scratch_shapes=[pltpu.VMEM((total, features), jnp.bfloat16)],
        ),
        compiler_params=pltpu.CompilerParams(vmem_limit_bytes=16 * MIB),
        cost_estimate=LITTLE,
    )(at, pre_all, *cots)


def grad_up_kernel(blocks, scale, at_ref, *refs):
    ins, mine, pair = (refs[i * blocks : (i + 1) * blocks] for i in range(3))
    out_ref, inputs, grads = refs[3 * blocks :]
    tokens, half = mine[0].shape
    tile = out_ref.shape[0]

    @pl.when(pl.program_id(0) == 0)
    def _():
        core = at_ref[blocks]
        left = pl.ds(pl.multiple_of(core * half, half), half)
        right = pl.ds(pl.multiple_of((1 - core) * half, half), half)
        for s in range(blocks):
            here = pl.ds(s * tokens, tokens)
            inputs[here, :] = ins[s][...]
            grads[here, left] = mine[s][...]
            grads[here, right] = pair[s][...]

    columns = pl.ds(pl.multiple_of(pl.program_id(0) * tile, tile), tile)
    out_ref[...] = dot(inputs[:, columns], grads[...], FIRST) * scale


def grad_up_call(at, ins, mine, pair, scale):
    tokens, features = ins[0].shape
    total = tokens * len(ins)
    hidden = 2 * mine[0].shape[1]
    tile = tile_of(features)
    return pl.pallas_call(
        functools.partial(grad_up_kernel, len(mine), scale),
        out_shape=jax.ShapeDtypeStruct((features, hidden), jnp.float32),
        grid_spec=pltpu.PrefetchScalarGridSpec(
            num_scalar_prefetch=1,
            grid=(features // tile,),
            in_specs=[in_vmem() for _ in ins + mine + pair],
            out_specs=pl.BlockSpec((tile, hidden), lambda i, at: (i, 0)),
            scratch_shapes=[
                pltpu.VMEM((total, features), jnp.bfloat16),
                pltpu.VMEM((total, hidden), jnp.bfloat16),
            ],
        ),
        compiler_params=pltpu.CompilerParams(vmem_limit_bytes=20 * MIB),
        cost_estimate=LITTLE,
    )(at, *ins, *mine, *pair)


def lay_out_kernel(at_ref, *refs):
    out_ref = refs[-1]
    tokens = refs[0].shape[0]
    for i, ref in enumerate(refs[:-1]):
        out_ref[pl.ds(pl.multiple_of(at_ref[i] * tokens, tokens), tokens), :] = ref[...]


def lay_out_call(places, blocks):
    tokens, hidden = blocks[0].shape
    return pl.pallas_call(
        lay_out_kernel,
        out_shape=jax.ShapeDtypeStruct((tokens * len(blocks), hidden), jnp.bfloat16),
        grid_spec=pltpu.PrefetchScalarGridSpec(
            num_scalar_prefetch=1,
            grid=(1,),
            in_specs=[in_vmem() for _ in blocks],
            out_specs=in_vmem(),
        ),
        compiler_params=pltpu.CompilerParams(vmem_limit_bytes=8 * MIB),
        cost_estimate=LITTLE,
    )(places, *blocks)


def pre_grad_kernel(at_ref, pre_ref, part_ref, *refs):
    out_ref = refs[-1]
    tokens, half = part_ref.shape
    rows = 64
    columns = pl.ds(pl.multiple_of(at_ref[1] * half, half), half)
    for first in range(0, tokens, rows):
        here = pl.ds(first, rows)
        total = part_ref[here, :]
        for other in refs[:-1]:
            total = total + other[here, :].astype(jnp.float32)
        place = pl.ds(pl.multiple_of(at_ref[0] * tokens + first, rows), rows)
        out_ref[here, :] = (total * gelu_slope(pre_ref[place, columns])).astype(jnp.bfloat16)


def pre_grad_call(at, core, pre_all, part, others):
    tokens, half = part.shape
    return pl.pallas_call(
        pre_grad_kernel,
        out_shape=jax.ShapeDtypeStruct((tokens, half), jnp.bfloat16),
        grid_spec=pltpu.PrefetchScalarGridSpec(
            num_scalar_prefetch=1,
            grid=(1,),
            in_specs=[in_vmem() for _ in [pre_all, part] + others],
            out_specs=in_vmem(),
        ),
        compiler_params=pltpu.CompilerParams(vmem_limit_bytes=8 * MIB),
        cost_estimate=LITTLE,
    )(jnp.stack([at, core]).astype(jnp.int32), pre_all, part, *others)


def hidden_kernel(core_ref, cot_ref, pair_ref, mine_ref, theirs_ref, part_ref, sent_ref):
    tile = mine_ref.shape[0]
    part = dot(cot_ref[...], mine_ref[...], LAST) + dot(pair_ref[...], theirs_ref[...], LAST)
    here = pl.ds(pl.multiple_of(pl.program_id(0) * tile, tile), tile)
    part_ref[:, here] = part
    sent_ref[:, here] = part.astype(jnp.bfloat16)


def hidden_call(core, cot, cot_pair, down_mine, down_pair):
    (tokens, features), half = cot.shape, down_mine.shape[0] // 2
    tile = tile_of(half)
    weight = pl.BlockSpec((tile, features), lambda i, core: (core[0] * (half // tile) + i, 0))
    return pl.pallas_call(
        hidden_kernel,
        out_shape=[
            jax.ShapeDtypeStruct((tokens, half), jnp.float32),
            jax.ShapeDtypeStruct((tokens, half), jnp.bfloat16),
        ],
        grid_spec=pltpu.PrefetchScalarGridSpec(
            num_scalar_prefetch=1,
            grid=(half // tile,),
            in_specs=[in_vmem(), in_vmem(), weight, weight],
            out_specs=[in_vmem(), in_vmem()],
        ),
        compiler_params=pltpu.CompilerParams(vmem_limit_bytes=10 * MIB),
        cost_estimate=LITTLE,
    )(core, cot, cot_pair, down_mine, down_pair)


def share_kernel(core_ref, mine_ref, theirs_ref, up_ref, *refs):
    out_ref = refs[-1]
    tile, half = up_ref.shape[0], mine_ref.shape[1]
    left = pl.ds(pl.multiple_of(core_ref[0] * half, half), half)
    right = pl.ds(pl.multiple_of((1 - core_ref[0]) * half, half), half)
    here = pl.ds(pl.multiple_of(pl.program_id(0) * tile, tile), tile)
    total = dot(mine_ref[...], up_ref[:, left], LAST)
    total = total + dot(theirs_ref[...], up_ref[:, right], LAST)
    for arrived in refs[:-1]:
        total = total + arrived[:, here].astype(jnp.float32)
    out_ref[:, here] = total.astype(jnp.bfloat16)


def share_call(core, mine, theirs, up_weight, arrived):
    features, hidden = up_weight.shape
    tile = tile_of(features)
    return pl.pallas_call(
        share_kernel,
        out_shape=jax.ShapeDtypeStruct((mine.shape[0], features), jnp.bfloat16),
        grid_spec=pltpu.PrefetchScalarGridSpec(
            num_scalar_prefetch=1,
            grid=(features // tile,),
            in_specs=[
                in_vmem(),
                in_vmem(),
                pl.BlockSpec((tile, hidden), lambda i, core: (i, 0)),
                *[in_vmem() for _ in arrived],
            ],
            out_specs=in_vmem(),
        ),
        compiler_params=pltpu.CompilerParams(vmem_limit_bytes=10 * MIB),
        cost_estimate=LITTLE,
    )(core, mine, theirs, up_weight, *arrived)


def per_device(inputs, cotangent, preactivation, up_weight, down_weight):
    cols, rows = lax.axis_size("col"), lax.axis_size("row")
    z, r = lax.axis_index("col"), lax.axis_index("row")
    core = lax.rem(r, 2)
    tokens, features = cotangent.shape
    hidden = down_weight.shape[0]
    half = hidden // 2
    ring = [(i, (i + 1) % cols) for i in range(cols)]
    pair = [(i, i ^ 1) for i in range(rows)]
    scale = 1.0 / math.sqrt(tokens * cols)
    at = jnp.stack([lax.rem(z - s + cols, cols) for s in range(cols)] + [core]).astype(jnp.int32)

    shifts = range(2, rows, 2)
    over_x = [[(i, (i + shift) % rows) for i in range(rows)] for shift in shifts]
    places = [r] + [lax.rem(r - shift + rows, rows) for shift in shifts]
    places = jnp.stack(places + [p + 1 - 2 * lax.rem(p, 2) for p in places]).astype(jnp.int32)
    pres = [preactivation] + [lax.ppermute(preactivation, "row", to) for to in over_x]

    down_pair = lax.ppermute(down_weight, "row", pair)
    parts, others, mine, theirs = ([None] * cols for _ in range(4))

    def hidden_part(s, cot, first):
        cot_pair = after(lax.ppermute(cot, "row", pair), *first)
        parts[s], sent = hidden_call(at[cols:], cot, cot_pair, down_weight, down_pair)
        if s != 0:
            exchange(s, sent)
        return sent

    def exchange(s, sent):
        others[s] = [lax.ppermute(sent, "row", to) for to in over_x]

    def pre_grad(s, first):
        others[s][0] = after(others[s][0], *first)
        mine[s] = pre_grad_call(at[s], core, pre_all, parts[s], others[s])
        theirs[s] = lax.ppermute(mine[s], "row", pair)

    def share(s, first, arrived):
        return share_call(at[cols:], after(mine[s], *first), theirs[s], up_weight, arrived)

    cots, ins = [cotangent], [inputs]
    arriving = lax.ppermute(cotangent, "col", ring)
    for s in range(1, cols):
        first = [sent] if s > 1 else []
        if s > 1 and s == cols - 1:
            pre_all = lay_out_call(after(places, sent), pres)
            pre_grad(1, [sent])
            first = [sent, mine[1]]
        cots.append(after(arriving, *first))
        if s < cols - 1:
            arriving = lax.ppermute(cots[s], "col", ring)
        if s == 1:
            own = hidden_part(0, cotangent, [cots[1]])
            sent = hidden_part(1, cots[1], pres[1:] + [own])
            pres = pres + [lax.ppermute(after(p, cots[1]), "row", pair) for p in pres]
        else:
            sent = hidden_part(s, cots[s], [])
    exchange(0, after(own, sent))
    ins.append(lax.ppermute(after(inputs, cots[cols - 2]), "col", ring))

    late = []
    for s in range(1, cols):
        following = (s + 1) % cols
        pre_grad(following, [sent, *late])
        arrived = [lax.ppermute(sums, "col", ring)] if s > 1 else []
        if s > 1:
            ins.append(lax.ppermute(ins[-1], "col", ring))
        sums = share(s, [mine[following], ins[s]], arrived)
        late = [sums]
        if s == 1:
            grad_down = grad_down_call(after(at, sums), pre_all, cots, scale)
            late = [grad_down]
    arrived = lax.ppermute(sums, "col", ring)
    grad_up = grad_up_call(after(at, sums), ins, mine, theirs, scale)
    sums = share(0, [grad_up], [arrived])
    return (sums, grad_up, grad_down)


def solution(mesh):
    placed = (
        P(("groups", "col"), "row"),
        P(("groups", "col"), "row"),
        P(("groups", "row"), "col"),
        P("row", "col"),
        P("col", "row"),
    )
    return jax.shard_map(
        per_device,
        mesh=mesh,
        in_specs=placed,
        out_specs=(
            P(("groups", "col"), "row"),
            P(("groups", "row"), "col"),
            P(("groups", "col"), "row"),
        ),
        check_vma=False,
    )
```

```python
import functools
import math

import jax
import jax.numpy as jnp
from jax import lax
from jax.experimental import pallas as pl
from jax.experimental.pallas import tpu as pltpu
from jax.sharding import PartitionSpec as P

LAST = (((1,), (1,)), ((), ()))
FIRST = (((0,), (0,)), ((), ()))
MIB = 1024 * 1024
LITTLE = pl.CostEstimate(flops=1024, bytes_accessed=1024, transcendentals=0)


def gelu_parts(values):
    v = values.astype(jnp.float32)
    tanh_val = jnp.tanh(0.7978845608 * (v + 0.044715 * v * v * v))
    return v, tanh_val


def gelu(values):
    v, tanh_val = gelu_parts(values)
    return 0.5 * v * (1.0 + tanh_val)


def gelu_slope(values):
    v, tanh_val = gelu_parts(values)
    return 0.5 * (1.0 + tanh_val) + 0.5 * v * (1.0 - tanh_val * tanh_val) * 0.7978845608 * (
        1.0 + 3.0 * 0.044715 * v * v
    )


def dot(a, b, dims):
    return lax.dot_general(a, b, dims, preferred_element_type=jnp.float32)


def after(value, *first):
    return lax.optimization_barrier((value, *first))[0] if first else value


def tile_of(extent):
    return next(t for t in (256, 128, extent) if extent % t == 0)


def in_vmem():
    return pl.BlockSpec(memory_space=pltpu.VMEM)


def block(index, size, first=0):
    return pl.ds(pl.multiple_of(index * size + first, math.gcd(size, first)), size - first)


def block_at(place_ref, step, cols):
    return lax.rem(place_ref[0] - step + cols, cols)


def core_of(place_ref):
    return lax.rem(place_ref[1], 2)


def call(kernel, place, operands, outs, mib, grid=(1,), in_specs=None, out_specs=None, scratch=()):
    return pl.pallas_call(
        kernel,
        out_shape=outs,
        grid_spec=pltpu.PrefetchScalarGridSpec(
            num_scalar_prefetch=1,
            grid=grid,
            in_specs=in_specs or [in_vmem() for _ in operands],
            out_specs=out_specs or jax.tree.map(lambda _: in_vmem(), outs),
            scratch_shapes=scratch,
        ),
        compiler_params=pltpu.CompilerParams(vmem_limit_bytes=mib * MIB),
        cost_estimate=LITTLE,
    )(place, *operands)


def lay_out_kernel(shifts, rows, place_ref, *refs):
    out_ref = refs[-1]
    tokens = refs[0].shape[0]
    for i, ref in enumerate(refs[:-1]):
        owner = lax.rem(place_ref[1] - shifts[i % len(shifts)] + rows, rows)
        if i >= len(shifts):
            owner = owner + 1 - 2 * lax.rem(owner, 2)
        out_ref[block(owner, tokens), :] = ref[...]


def lay_out_call(place, blocks, shifts, rows):
    tokens, hidden = blocks[0].shape
    out = jax.ShapeDtypeStruct((tokens * len(blocks), hidden), jnp.bfloat16)
    return call(functools.partial(lay_out_kernel, shifts, rows), place, blocks, out, 8)


def hidden_kernel(place_ref, cot_ref, pair_ref, mine_ref, theirs_ref, part_ref, sent_ref):
    half = part_ref.shape[1]
    tile = tile_of(half)
    for first in range(0, half, tile):
        rows = pl.ds(pl.multiple_of(core_of(place_ref) * half + first, tile), tile)
        part = dot(cot_ref[...], mine_ref[rows, :], LAST)
        part = part + dot(pair_ref[...], theirs_ref[rows, :], LAST)
        part_ref[:, pl.ds(first, tile)] = part
        sent_ref[:, pl.ds(first, tile)] = part.astype(jnp.bfloat16)


def hidden_call(place, cot, cot_pair, down_mine, down_pair):
    shape = (cot.shape[0], down_mine.shape[0] // 2)
    outs = [jax.ShapeDtypeStruct(shape, jnp.float32), jax.ShapeDtypeStruct(shape, jnp.bfloat16)]
    return call(hidden_kernel, place, [cot, cot_pair, down_mine, down_pair], outs, 12)


def pre_grad_kernel(step, cols, place_ref, pre_ref, part_ref, *refs):
    out_ref = refs[-1]
    tokens, half = part_ref.shape
    rows = 64 if tokens % 64 == 0 else tokens
    columns = block(core_of(place_ref), half)
    start = block_at(place_ref, step, cols) * tokens
    for first in range(0, tokens, rows):
        here = pl.ds(first, rows)
        total = part_ref[here, :]
        for other in refs[:-1]:
            total = total + other[here, :].astype(jnp.float32)
        v = pre_ref[pl.ds(pl.multiple_of(start + first, rows), rows), columns]
        out_ref[here, :] = (total * gelu_slope(v)).astype(jnp.bfloat16)


def pre_grad_call(place, step, cols, pre_all, part, others):
    out = jax.ShapeDtypeStruct(part.shape, jnp.bfloat16)
    kernel = functools.partial(pre_grad_kernel, step, cols)
    return call(kernel, place, [pre_all, part, *others], out, 8)


def share_kernel(place_ref, mine_ref, theirs_ref, up_ref, *refs):
    out_ref = refs[-1]
    features, half = up_ref.shape[0], mine_ref.shape[1]
    tile = tile_of(features)
    left, right = block(core_of(place_ref), half), block(1 - core_of(place_ref), half)
    for first in range(0, features, tile):
        here = pl.ds(first, tile)
        total = dot(mine_ref[...], up_ref[here, left], LAST)
        total = total + dot(theirs_ref[...], up_ref[here, right], LAST)
        for arrived in refs[:-1]:
            total = total + arrived[:, here].astype(jnp.float32)
        out_ref[:, here] = total.astype(jnp.bfloat16)


def share_call(place, mine, theirs, up_weight, arrived):
    out = jax.ShapeDtypeStruct((mine.shape[0], up_weight.shape[0]), jnp.bfloat16)
    return call(share_kernel, place, [mine, theirs, up_weight, *arrived], out, 12)


def grad_down_kernel(blocks, scale, place_ref, pre_ref, *refs):
    cot_refs, out_ref, cots = refs[:blocks], refs[-2], refs[-1]
    tokens = cot_refs[0].shape[0]

    @pl.when(pl.program_id(0) == 0)
    def _():
        for s in range(blocks):
            cots[block(block_at(place_ref, s, blocks), tokens), :] = cot_refs[s][...]

    activation = gelu(pre_ref[...]).astype(jnp.bfloat16)
    out_ref[...] = dot(activation, cots[...], FIRST) * scale


def grad_down_call(place, pre_all, cots, scale):
    total, hidden = pre_all.shape
    features = cots[0].shape[1]
    tile = tile_of(hidden)
    return call(
        functools.partial(grad_down_kernel, len(cots), scale),
        place,
        [pre_all, *cots],
        jax.ShapeDtypeStruct((hidden, features), jnp.float32),
        14,
        grid=(hidden // tile,),
        in_specs=[pl.BlockSpec((total, tile), lambda i, place: (0, i))]
        + [in_vmem() for _ in cots],
        out_specs=pl.BlockSpec((tile, features), lambda i, place: (i, 0)),
        scratch=[pltpu.VMEM((total, features), jnp.bfloat16)],
    )


def grad_up_kernel(blocks, scale, place_ref, *refs):
    ins, mine, pair = (refs[i * blocks : (i + 1) * blocks] for i in range(3))
    out_ref, inputs, grads = refs[3 * blocks :]
    tokens, half = mine[0].shape
    tile = out_ref.shape[0]

    @pl.when(pl.program_id(0) == 0)
    def _():
        left, right = block(core_of(place_ref), half), block(1 - core_of(place_ref), half)
        for s in range(blocks):
            here = pl.ds(s * tokens, tokens)
            inputs[here, :] = ins[s][...]
            grads[here, left] = mine[s][...]
            grads[here, right] = pair[s][...]

    out_ref[...] = dot(inputs[:, block(pl.program_id(0), tile)], grads[...], FIRST) * scale


def grad_up_call(place, ins, mine, pair, scale):
    tokens, features = ins[0].shape
    total = tokens * len(ins)
    hidden = 2 * mine[0].shape[1]
    tile = tile_of(features)
    return call(
        functools.partial(grad_up_kernel, len(mine), scale),
        place,
        [*ins, *mine, *pair],
        jax.ShapeDtypeStruct((features, hidden), jnp.float32),
        18,
        grid=(features // tile,),
        out_specs=pl.BlockSpec((tile, hidden), lambda i, place: (i, 0)),
        scratch=[
            pltpu.VMEM((total, features), jnp.bfloat16),
            pltpu.VMEM((total, hidden), jnp.bfloat16),
        ],
    )


def per_device(inputs, cotangent, preactivation, up_weight, down_weight):
    cols, rows = lax.axis_size("col"), lax.axis_size("row")
    place = jnp.stack([lax.axis_index("col"), lax.axis_index("row")]).astype(jnp.int32)
    cotangent, preactivation, down_weight = (
        after(x, place) for x in (cotangent, preactivation, down_weight)
    )
    ring = [(i, (i + 1) % cols) for i in range(cols)]
    pair = [(i, i ^ 1) for i in range(rows)]
    shifts = range(0, rows, 2)
    over_x = [[(i, (i + shift) % rows) for i in range(rows)] for shift in shifts[1:]]
    scale = 1.0 / math.sqrt(cotangent.shape[0] * cols)

    pres = [preactivation] + [lax.ppermute(preactivation, "row", to) for to in over_x]
    down_pair = lax.ppermute(down_weight, "row", pair)
    parts, sent, others, mine, theirs = ([None] * cols for _ in range(5))

    def hidden_part(s, *first):
        cot_pair = after(lax.ppermute(cots[s], "row", pair), *first)
        parts[s], sent[s] = hidden_call(place, cots[s], cot_pair, down_weight, down_pair)

    def exchange(s, *first):
        values = after(sent[s], *first)
        others[s] = [lax.ppermute(values, "row", to) for to in over_x]

    def pre_grad(s, *first):
        mine[s] = pre_grad_call(after(place, *first), s, cols, pre_all, parts[s], others[s])
        theirs[s] = lax.ppermute(mine[s], "row", pair)

    def share(s, arrived, *first):
        return share_call(after(place, *first), mine[s], theirs[s], up_weight, arrived)

    cots, ins = [cotangent], [inputs]
    arriving = lax.ppermute(cotangent, "col", ring)
    for s in range(1, cols):
        if s == 2:
            arriving = after(arriving, sent[0])
        elif s > 2:
            arriving = after(arriving, sent[s - 1])
        cots.append(arriving)
        if s < cols - 1:
            arriving = lax.ppermute(arriving, "col", ring)
            hidden_part(s)
            exchange(s)
        if s == 1:
            hidden_part(0, sent[1], *pres[1:])
            pres = pres + [lax.ppermute(after(p, sent[1]), "row", pair) for p in pres]

    last = cols - 1
    pre_all = lay_out_call(after(place, sent[last - 1]), pres, shifts, rows)
    pre_grad(1, sent[last - 1])
    ins.append(lax.ppermute(after(inputs, cots[last - 1]), "col", ring))
    sums = share(1, [], mine[1])
    pre_grad(2, sums)
    hidden_part(last, mine[2], ins[1])
    exchange(last)
    exchange(0, sent[last])
    grad_down = grad_down_call(after(place, sums, sent[last]), pre_all, cots, scale)
    late = grad_down
    for s in range(2, cols):
        following = (s + 1) % cols
        pre_grad(following, late)
        arrived = lax.ppermute(sums, "col", ring)
        ins.append(lax.ppermute(ins[-1], "col", ring))
        sums = late = share(s, [arrived], mine[following], ins[s])
    arrived = lax.ppermute(sums, "col", ring)
    grad_up = grad_up_call(after(place, sums), ins, mine, theirs, scale)
    sums = share(0, [arrived], grad_up)
    return (sums, grad_up, grad_down)


def solution(mesh):
    placed = (
        P(("groups", "col"), "row"),
        P(("groups", "col"), "row"),
        P(("groups", "row"), "col"),
        P("row", "col"),
        P("col", "row"),
    )
    return jax.shard_map(
        per_device,
        mesh=mesh,
        in_specs=placed,
        out_specs=(
            P(("groups", "col"), "row"),
            P(("groups", "row"), "col"),
            P(("groups", "col"), "row"),
        ),
        check_vma=False,
    )
```

```python
import functools
import math

import jax
import jax.numpy as jnp
from jax import lax
from jax.experimental import pallas as pl
from jax.experimental.pallas import tpu as pltpu
from jax.sharding import PartitionSpec as P

LAST = (((1,), (1,)), ((), ()))
FIRST = (((0,), (0,)), ((), ()))
MIB = 1024 * 1024
PART = 16
EARLY = 9 * 10**9


def gelu_parts(values):
    v = values.astype(jnp.float32)
    tanh_val = jnp.tanh(0.7978845608 * (v + 0.044715 * v * v * v))
    return v, tanh_val


def gelu(values):
    v, tanh_val = gelu_parts(values)
    return 0.5 * v * (1.0 + tanh_val)


def gelu_slope(values):
    v, tanh_val = gelu_parts(values)
    return 0.5 * (1.0 + tanh_val) + 0.5 * v * (1.0 - tanh_val * tanh_val) * 0.7978845608 * (
        1.0 + 3.0 * 0.044715 * v * v
    )


def dot(a, b, dims):
    return lax.dot_general(a, b, dims, preferred_element_type=jnp.float32)


def after(value, *first):
    return lax.optimization_barrier((value, *first))[0] if first else value


def tile_of(extent):
    return next(t for t in (256, 128, extent) if extent % t == 0)


def in_vmem():
    return pl.BlockSpec(memory_space=pltpu.VMEM)


def block(index, size, first=0):
    return pl.ds(pl.multiple_of(index * size + first, math.gcd(size, first)), size - first)


def block_at(place_ref, step, cols):
    return lax.rem(place_ref[0] - step + cols, cols)


def core_of(place_ref):
    return lax.rem(place_ref[1], 2)


def call(kernel, place, operands, outs, mib, flops, grid=(1,), in_specs=None, out_specs=None, scratch=()):
    return pl.pallas_call(
        kernel,
        out_shape=outs,
        grid_spec=pltpu.PrefetchScalarGridSpec(
            num_scalar_prefetch=1,
            grid=grid,
            in_specs=in_specs or [in_vmem() for _ in operands],
            out_specs=out_specs or jax.tree.map(lambda _: in_vmem(), outs),
            scratch_shapes=scratch,
        ),
        compiler_params=pltpu.CompilerParams(vmem_limit_bytes=mib * MIB),
        cost_estimate=pl.CostEstimate(flops=flops // PART, bytes_accessed=1024, transcendentals=0),
    )(place, *operands)


def go_on_kernel(place_ref, out_ref):
    for i in range(2):
        out_ref[i] = place_ref[i]


def go_on_call(place, declared):
    return pl.pallas_call(
        go_on_kernel,
        out_shape=jax.ShapeDtypeStruct(place.shape, place.dtype),
        in_specs=[pl.BlockSpec(memory_space=pltpu.SMEM)],
        out_specs=pl.BlockSpec(memory_space=pltpu.SMEM),
        compiler_params=pltpu.CompilerParams(vmem_limit_bytes=MIB // 2),
        cost_estimate=pl.CostEstimate(flops=declared, bytes_accessed=1024, transcendentals=0),
    )(place)


def take_half_kernel(place_ref, mine_ref, theirs_ref, out_ref):
    tokens, half = mine_ref.shape[0], out_ref.shape[1]
    core = core_of(place_ref)
    out_ref[block(core, tokens), :] = mine_ref[:, block(core, half)]
    out_ref[block(1 - core, tokens), :] = theirs_ref[:, block(core, half)]


def take_half_call(place, mine, theirs):
    tokens, hidden = mine.shape
    out = jax.ShapeDtypeStruct((2 * tokens, hidden // 2), jnp.bfloat16)
    return call(take_half_kernel, place, [mine, theirs], out, 8, MIB)


def lay_out_kernel(place_ref, *refs):
    blocks, out_ref = refs[:-1], refs[-1]
    tokens = blocks[0].shape[0]
    for i, ref in enumerate(blocks):
        owner = lax.rem(lax.div(place_ref[1], 2) - i + len(blocks), len(blocks))
        out_ref[block(owner, tokens), :] = ref[...]


def lay_out_call(place, blocks):
    tokens, half = blocks[0].shape
    out = jax.ShapeDtypeStruct((tokens * len(blocks), half), jnp.bfloat16)
    return call(lay_out_kernel, place, blocks, out, 8, 5000 * MIB)


def hidden_kernel(place_ref, cot_ref, pair_ref, mine_ref, theirs_ref, part_ref, sent_ref):
    half = part_ref.shape[1]
    tile = tile_of(half)
    for first in range(0, half, tile):
        rows = pl.ds(pl.multiple_of(core_of(place_ref) * half + first, tile), tile)
        part = dot(cot_ref[...], mine_ref[rows, :], LAST)
        part = part + dot(pair_ref[...], theirs_ref[rows, :], LAST)
        part_ref[:, pl.ds(first, tile)] = part
        sent_ref[:, pl.ds(first, tile)] = part.astype(jnp.bfloat16)


def hidden_call(place, cot, cot_pair, down_mine, down_pair):
    shape = (cot.shape[0], down_mine.shape[0] // 2)
    outs = [jax.ShapeDtypeStruct(shape, jnp.float32), jax.ShapeDtypeStruct(shape, jnp.bfloat16)]
    return call(hidden_kernel, place, [cot, cot_pair, down_mine, down_pair], outs, 12, 4 * cot.size * shape[1])


def pre_grad_kernel(step, cols, place_ref, pre_ref, part_ref, *refs):
    out_ref = refs[-1]
    tokens, half = part_ref.shape
    rows = 64 if tokens % 64 == 0 else tokens
    start = block_at(place_ref, step, cols) * tokens
    for first in range(0, tokens, rows):
        here = pl.ds(first, rows)
        total = part_ref[here, :]
        for other in refs[:-1]:
            total = total + other[here, :].astype(jnp.float32)
        v = pre_ref[pl.ds(pl.multiple_of(start + first, rows), rows), :]
        out_ref[here, :] = (total * gelu_slope(v)).astype(jnp.bfloat16)


def pre_grad_call(place, step, cols, pre_all, part, others):
    out = jax.ShapeDtypeStruct(part.shape, jnp.bfloat16)
    kernel = functools.partial(pre_grad_kernel, step, cols)
    return call(kernel, place, [pre_all, part, *others], out, 8, 8192 * part.size)


def share_kernel(place_ref, mine_ref, theirs_ref, up_ref, *refs):
    out_ref = refs[-1]
    features, half = up_ref.shape[0], mine_ref.shape[1]
    tile = tile_of(features)
    left, right = block(core_of(place_ref), half), block(1 - core_of(place_ref), half)
    for first in range(0, features, tile):
        here = pl.ds(first, tile)
        total = dot(mine_ref[...], up_ref[here, left], LAST)
        total = total + dot(theirs_ref[...], up_ref[here, right], LAST)
        for arrived in refs[:-1]:
            total = total + arrived[:, here].astype(jnp.float32)
        out_ref[:, here] = total.astype(jnp.bfloat16)


def share_call(place, mine, theirs, up_weight, arrived):
    out = jax.ShapeDtypeStruct((mine.shape[0], up_weight.shape[0]), jnp.bfloat16)
    return call(share_kernel, place, [mine, theirs, up_weight, *arrived], out, 12, 2 * mine.shape[0] * up_weight.size)


def grad_down_kernel(blocks, scale, place_ref, mine_ref, theirs_ref, *refs):
    cot_refs, out_ref, cots = refs[:blocks], refs[-2], refs[-1]
    tokens, tile = cot_refs[0].shape[0], out_ref.shape[0]
    i, steps = pl.program_id(0), mine_ref.shape[1] // tile

    @pl.when(i == 0)
    def _():
        for s in range(blocks):
            cots[block(block_at(place_ref, s, blocks), tokens), :] = cot_refs[s][...]

    def product(pre_ref, at):
        activation = gelu(pre_ref[:, block(at, tile)]).astype(jnp.bfloat16)
        out_ref[...] = dot(activation, cots[...], FIRST) * scale

    pl.when(i < steps)(lambda: product(mine_ref, i))
    pl.when(i >= steps)(lambda: product(theirs_ref, i - steps))


def grad_down_call(place, pre_mine, pre_theirs, cots, scale):
    (total, half), features = pre_mine.shape, cots[0].shape[1]
    tile = tile_of(half)
    steps = half // tile

    def rows(i, place):
        core = lax.rem(place[1], 2)
        return jnp.where(i < steps, core * steps + i, (1 - core) * steps + i - steps), 0

    return call(
        functools.partial(grad_down_kernel, len(cots), scale),
        place,
        [pre_mine, pre_theirs, *cots],
        jax.ShapeDtypeStruct((2 * half, features), jnp.float32),
        14,
        4 * pre_mine.size * features,
        grid=(2 * steps,),
        out_specs=pl.BlockSpec((tile, features), rows),
        scratch=[pltpu.VMEM((total, features), jnp.bfloat16)],
    )


def grad_up_kernel(blocks, scale, place_ref, *refs):
    ins, mine, pair = (refs[i * blocks : (i + 1) * blocks] for i in range(3))
    out_ref, inputs, grads = refs[3 * blocks :]
    tokens, half = mine[0].shape
    tile = out_ref.shape[0]

    @pl.when(pl.program_id(0) == 0)
    def _():
        left, right = block(core_of(place_ref), half), block(1 - core_of(place_ref), half)
        for s in range(blocks):
            here = pl.ds(s * tokens, tokens)
            inputs[here, :] = ins[s][...]
            grads[here, left] = mine[s][...]
            grads[here, right] = pair[s][...]

    out_ref[...] = dot(inputs[:, block(pl.program_id(0), tile)], grads[...], FIRST) * scale


def grad_up_call(place, ins, mine, pair, scale):
    tokens, features = ins[0].shape
    total = tokens * len(ins)
    hidden = 2 * mine[0].shape[1]
    tile = tile_of(features)
    return call(
        functools.partial(grad_up_kernel, len(mine), scale),
        place,
        [*ins, *mine, *pair],
        jax.ShapeDtypeStruct((features, hidden), jnp.float32),
        18,
        2 * total * hidden * features,
        grid=(features // tile,),
        out_specs=pl.BlockSpec((tile, hidden), lambda i, place: (i, 0)),
        scratch=[
            pltpu.VMEM((total, features), jnp.bfloat16),
            pltpu.VMEM((total, hidden), jnp.bfloat16),
        ],
    )


def per_device(inputs, cotangent, preactivation, up_weight, down_weight):
    cols, rows = lax.axis_size("col"), lax.axis_size("row")
    place = jnp.stack([lax.axis_index("col"), lax.axis_index("row")]).astype(jnp.int32)
    cotangent, preactivation, down_weight = (
        after(x, place) for x in (cotangent, preactivation, down_weight)
    )
    ring = [(i, (i + 1) % cols) for i in range(cols)]
    pair = [(i, i ^ 1) for i in range(rows)]
    over_x = [[(i, (i + shift) % rows) for i in range(rows)] for shift in range(2, rows, 2)]
    scale = 1.0 / math.sqrt(cotangent.shape[0] * cols)

    pre = take_half_call(place, preactivation, lax.ppermute(preactivation, "row", pair))
    pres = [pre] + [lax.ppermute(pre, "row", to) for to in over_x]
    down_pair = lax.ppermute(down_weight, "row", pair)
    parts, sent, others, mine, theirs = ([None] * cols for _ in range(5))

    def hidden_part(s, *first):
        cot_pair = after(lax.ppermute(cots[s], "row", pair), *first)
        parts[s], sent[s] = hidden_call(place, cots[s], cot_pair, down_weight, down_pair)

    def exchange(s, *first):
        values = after(sent[s], *first)
        others[s] = [lax.ppermute(values, "row", to) for to in over_x]

    def pre_grad(s, *first):
        mine[s] = pre_grad_call(after(place, *first), s, cols, pre_all, parts[s], others[s])
        theirs[s] = lax.ppermute(mine[s], "row", pair)

    def share(s, arrived, *first):
        here = after(place, *arrived, *first)
        here = go_on_call(here, EARLY) if arrived else here
        return share_call(here, mine[s], theirs[s], up_weight, arrived)

    cots, ins, last = [cotangent], [inputs], cols - 1
    for s in range(1, cols):
        cots.append(lax.ppermute(cots[s - 1], "col", ring))
        if s == 1:
            cots[1] = after(cots[1], pre)
            ins.append(lax.ppermute(after(inputs, cots[1]), "col", ring))
        if s == 2:
            cots[2] = after(cots[2], ins[1])

    hidden_part(1)
    exchange(1)
    pre_all = lay_out_call(place, pres)
    pre_grad(1)
    for s in range(2, last):
        hidden_part(s, mine[1])
        exchange(s)
    hidden_part(0, sent[last - 1])
    sums = share(1, [], sent[0])
    pre_grad(2, sums)
    cots[last] = after(cots[last], mine[2])
    hidden_part(last)
    exchange(last)
    exchange(0, sent[last])
    pre_theirs = lax.ppermute(after(pre_all, sums), "row", pair)
    for s in range(2, cols):
        arrived = lax.ppermute(sums, "col", ring)
        ins.append(lax.ppermute(after(ins[-1], sums, cots[last]), "col", ring))
        if s > 2:
            pre_grad(s, sums)
        if s == last:
            grad_down = grad_down_call(after(place, mine[s]), pre_all, pre_theirs, cots, scale)
            pre_grad(0, grad_down)
        sums = share(s, [arrived], ins[s], *([mine[0]] if s == last else []))
    arrived = lax.ppermute(sums, "col", ring)
    grad_up = grad_up_call(after(place, sums), ins, mine, theirs, scale)
    sums = share(0, [arrived], grad_up)
    return (sums, grad_up, grad_down)


def solution(mesh):
    placed = (
        P(("groups", "col"), "row"),
        P(("groups", "col"), "row"),
        P(("groups", "row"), "col"),
        P("row", "col"),
        P("col", "row"),
    )
    return jax.shard_map(
        per_device,
        mesh=mesh,
        in_specs=placed,
        out_specs=(
            P(("groups", "col"), "row"),
            P(("groups", "row"), "col"),
            P(("groups", "col"), "row"),
        ),
        check_vma=False,
    )
```

```python
import functools
import math

import jax
import jax.numpy as jnp
from jax import lax
from jax.experimental import pallas as pl
from jax.experimental.pallas import tpu as pltpu
from jax.sharding import PartitionSpec as P

LAST = (((1,), (1,)), ((), ()))
FIRST = (((0,), (0,)), ((), ()))
MIB = 1024 * 1024
LITTLE, SOME, MORE, MUCH, MOST = 10**7, 10**8, 10**9, 4 * 10**9, 8 * 10**9


def gelu_parts(values):
    v = values.astype(jnp.float32)
    tanh_val = jnp.tanh(0.7978845608 * (v + 0.044715 * v * v * v))
    return v, tanh_val


def gelu(values):
    v, tanh_val = gelu_parts(values)
    return 0.5 * v * (1.0 + tanh_val)


def gelu_slope(values):
    v, tanh_val = gelu_parts(values)
    return 0.5 * (1.0 + tanh_val) + 0.5 * v * (1.0 - tanh_val * tanh_val) * 0.7978845608 * (
        1.0 + 3.0 * 0.044715 * v * v
    )


def dot(a, b, dims):
    return lax.dot_general(a, b, dims, preferred_element_type=jnp.float32)


def after(value, *first):
    return lax.optimization_barrier((value, *first))[0] if first else value


def tile_of(extent):
    return next(t for t in (256, 128, extent) if extent % t == 0)


def in_vmem():
    return pl.BlockSpec(memory_space=pltpu.VMEM)


def block(index, size, first=0):
    return pl.ds(pl.multiple_of(index * size + first, math.gcd(size, first)), size - first)


def block_at(place_ref, step, cols):
    return lax.rem(place_ref[0] - step + cols, cols)


def core_of(place_ref):
    return lax.rem(place_ref[1], 2)


def call(kernel, place, operands, outs, mib, cost, grid=(1,), in_specs=None, out_specs=None, scratch=()):
    return pl.pallas_call(
        kernel,
        out_shape=outs,
        grid_spec=pltpu.PrefetchScalarGridSpec(
            num_scalar_prefetch=1,
            grid=grid,
            in_specs=in_specs or [in_vmem() for _ in operands],
            out_specs=out_specs or jax.tree.map(lambda _: in_vmem(), outs),
            scratch_shapes=scratch,
        ),
        compiler_params=pltpu.CompilerParams(vmem_limit_bytes=mib * MIB),
        cost_estimate=pl.CostEstimate(flops=cost, bytes_accessed=1024, transcendentals=0),
    )(place, *operands)


def lay_out_kernel(shifts, rows, place_ref, *refs):
    out_ref = refs[-1]
    tokens = refs[0].shape[0]
    for i, ref in enumerate(refs[:-1]):
        owner = lax.rem(place_ref[1] - shifts[i % len(shifts)] + rows, rows)
        if i >= len(shifts):
            owner = owner + 1 - 2 * lax.rem(owner, 2)
        out_ref[block(owner, tokens), :] = ref[...]


def lay_out_call(place, blocks, shifts, rows):
    tokens, hidden = blocks[0].shape
    out = jax.ShapeDtypeStruct((tokens * len(blocks), hidden), jnp.bfloat16)
    return call(functools.partial(lay_out_kernel, shifts, rows), place, blocks, out, 8, SOME)


def take_rows_kernel(place_ref, rows_ref, out_ref):
    out_ref[...] = rows_ref[block(core_of(place_ref), out_ref.shape[0]), :]


def take_rows_call(place, weight):
    out = jax.ShapeDtypeStruct((weight.shape[0] // 2, weight.shape[1]), weight.dtype)
    return call(take_rows_kernel, place, [weight], out, 12, LITTLE)


def hidden_kernel(place_ref, cot_ref, pair_ref, mine_ref, theirs_ref, part_ref, sent_ref):
    half = part_ref.shape[1]
    tile = tile_of(half)
    for first in range(0, half, tile):
        here = pl.ds(first, tile)
        rows = pl.ds(pl.multiple_of(core_of(place_ref) * half + first, tile), tile)
        part = dot(cot_ref[...], mine_ref[here, :], LAST)
        part = part + dot(pair_ref[...], theirs_ref[rows, :], LAST)
        part_ref[:, here] = part
        sent_ref[:, here] = part.astype(jnp.bfloat16)


def hidden_call(place, cot, cot_pair, down_mine, down_pair):
    shape = (cot.shape[0], down_mine.shape[0])
    outs = [jax.ShapeDtypeStruct(shape, jnp.float32), jax.ShapeDtypeStruct(shape, jnp.bfloat16)]
    return call(hidden_kernel, place, [cot, cot_pair, down_mine, down_pair], outs, 12, LITTLE)


def pre_grad_kernel(step, cols, place_ref, pre_ref, part_ref, *refs):
    out_ref = refs[-1]
    tokens, half = part_ref.shape
    rows = 64 if tokens % 64 == 0 else tokens
    columns = block(core_of(place_ref), half)
    start = block_at(place_ref, step, cols) * tokens
    for first in range(0, tokens, rows):
        here = pl.ds(first, rows)
        total = part_ref[here, :]
        for other in refs[:-1]:
            total = total + other[here, :].astype(jnp.float32)
        v = pre_ref[pl.ds(pl.multiple_of(start + first, rows), rows), columns]
        out_ref[here, :] = (total * gelu_slope(v)).astype(jnp.bfloat16)


def pre_grad_call(place, step, cols, pre_all, part, others):
    out = jax.ShapeDtypeStruct(part.shape, jnp.bfloat16)
    kernel = functools.partial(pre_grad_kernel, step, cols)
    return call(kernel, place, [pre_all, part, *others], out, 8, SOME)


def share_kernel(place_ref, mine_ref, theirs_ref, up_ref, out_ref, *sent_refs):
    features, half = up_ref.shape[0], mine_ref.shape[1]
    tile = tile_of(features)
    left, right = block(core_of(place_ref), half), block(1 - core_of(place_ref), half)
    for first in range(0, features, tile):
        here = pl.ds(first, tile)
        total = dot(mine_ref[...], up_ref[here, left], LAST)
        total = total + dot(theirs_ref[...], up_ref[here, right], LAST)
        out_ref[:, here] = total
        for sent in sent_refs:
            sent[:, here] = total.astype(jnp.bfloat16)


def share_call(place, mine, theirs, up_weight, first):
    shape = (mine.shape[0], up_weight.shape[0])
    outs = [jax.ShapeDtypeStruct(shape, jnp.float32)]
    outs += [jax.ShapeDtypeStruct(shape, jnp.bfloat16)] * first
    return call(share_kernel, place, [mine, theirs, up_weight], outs, 12, LITTLE)


def add_kernel(place_ref, part_ref, *refs):
    out_ref = refs[-1]
    rows = 64 if part_ref.shape[0] % 64 == 0 else part_ref.shape[0]
    for first in range(0, part_ref.shape[0], rows):
        here = pl.ds(first, rows)
        total = part_ref[here, :].astype(jnp.float32)
        for arrived in refs[:-1]:
            total = total + arrived[here, :].astype(jnp.float32)
        out_ref[here, :] = total.astype(out_ref.dtype)


def add_call(place, part, arrived, dtype, cost):
    out = jax.ShapeDtypeStruct(part.shape, dtype)
    return call(add_kernel, place, [part, *arrived], out, 4, cost)


def grad_down_kernel(blocks, scale, place_ref, pre_ref, *refs):
    cot_refs, out_ref, cots = refs[:blocks], refs[-2], refs[-1]
    tokens = cot_refs[0].shape[0]

    @pl.when(pl.program_id(0) == 0)
    def _():
        for s in range(blocks):
            cots[block(block_at(place_ref, s, blocks), tokens), :] = cot_refs[s][...]

    activation = gelu(pre_ref[...]).astype(jnp.bfloat16)
    out_ref[...] = dot(activation, cots[...], FIRST) * scale


def grad_down_call(place, pre_all, cots, scale):
    total, hidden = pre_all.shape
    features = cots[0].shape[1]
    tile = tile_of(hidden)
    return call(
        functools.partial(grad_down_kernel, len(cots), scale),
        place,
        [pre_all, *cots],
        jax.ShapeDtypeStruct((hidden, features), jnp.float32),
        14,
        SOME,
        grid=(hidden // tile,),
        in_specs=[pl.BlockSpec((total, tile), lambda i, place: (0, i))]
        + [in_vmem() for _ in cots],
        out_specs=pl.BlockSpec((tile, features), lambda i, place: (i, 0)),
        scratch=[pltpu.VMEM((total, features), jnp.bfloat16)],
    )


def grad_up_kernel(blocks, scale, place_ref, *refs):
    ins, mine, pair = (refs[i * blocks : (i + 1) * blocks] for i in range(3))
    out_ref, inputs, grads = refs[3 * blocks :]
    tokens, half = mine[0].shape
    tile = out_ref.shape[0]

    @pl.when(pl.program_id(0) == 0)
    def _():
        left, right = block(core_of(place_ref), half), block(1 - core_of(place_ref), half)
        for s in range(blocks):
            here = pl.ds(s * tokens, tokens)
            inputs[here, :] = ins[s][...]
            grads[here, left] = mine[s][...]
            grads[here, right] = pair[s][...]

    out_ref[...] = dot(inputs[:, block(pl.program_id(0), tile)], grads[...], FIRST) * scale


def grad_up_call(place, ins, mine, pair, scale):
    tokens, features = ins[0].shape
    total = tokens * len(ins)
    hidden = 2 * mine[0].shape[1]
    tile = tile_of(features)
    return call(
        functools.partial(grad_up_kernel, len(mine), scale),
        place,
        [*ins, *mine, *pair],
        jax.ShapeDtypeStruct((features, hidden), jnp.float32),
        18,
        MORE,
        grid=(features // tile,),
        out_specs=pl.BlockSpec((tile, hidden), lambda i, place: (i, 0)),
        scratch=[
            pltpu.VMEM((total, features), jnp.bfloat16),
            pltpu.VMEM((total, hidden), jnp.bfloat16),
        ],
    )


def per_device(inputs, cotangent, preactivation, up_weight, down_weight):
    cols, rows = lax.axis_size("col"), lax.axis_size("row")
    place = jnp.stack([lax.axis_index("col"), lax.axis_index("row")]).astype(jnp.int32)
    cotangent, preactivation, down_weight = (
        after(x, place) for x in (cotangent, preactivation, down_weight)
    )
    ring = [(i, (i + 1) % cols) for i in range(cols)]
    back = [(i, (i - 1) % cols) for i in range(cols)]
    pair = [(i, i ^ 1) for i in range(rows)]
    shifts = range(0, rows, 2)
    over_x = [[(i, (i + shift) % rows) for i in range(rows)] for shift in shifts[1:]]
    scale = 1.0 / math.sqrt(cotangent.shape[0] * cols)

    pres = [preactivation] + [lax.ppermute(preactivation, "row", to) for to in over_x]
    down_pair = lax.ppermute(down_weight, "row", pair)
    down_mine = take_rows_call(place, down_weight)
    parts, sent, others, mine, theirs = ([None] * cols for _ in range(5))

    def hidden_part(s, *first):
        cot_pair = after(lax.ppermute(cots[s], "row", pair), *first)
        parts[s], sent[s] = hidden_call(place, cots[s], cot_pair, down_mine, down_pair)

    def exchange(s, *first):
        values = after(sent[s], *first)
        others[s] = [lax.ppermute(values, "row", to) for to in over_x]

    def pre_grad(s, *first):
        mine[s] = pre_grad_call(after(place, *first), s, cols, pre_all, parts[s], others[s])
        theirs[s] = lax.ppermute(mine[s], "row", pair)

    def share(s, *first):
        sends = s in (1, cols - 1)
        return share_call(after(place, *first), mine[s], theirs[s], up_weight, sends)

    cots, middle = [cotangent] + [None] * (cols - 1), cols // 2
    order = []
    for s in range(1, middle + 1):
        cots[s] = lax.ppermute(cots[s - 1], "col", ring)
        order.append(s)
        if cols - s > middle:
            cots[cols - s] = lax.ppermute(cots[(cols - s + 1) % cols], "col", back)
            order.append(cols - s)
    arrived = list(cots)

    def hidden_next(i):
        s = order[i]
        arrived[s] = after(cots[s], sent[order[i - 1]] if i else down_mine)
        cot_pair = lax.ppermute(arrived[s], "row", pair)
        parts[s], sent[s] = hidden_call(place, cots[s], cot_pair, down_mine, down_pair)
        exchange(s)

    for i in range(len(order)):
        hidden_next(i)
    pres = pres + [lax.ppermute(after(p, sent[1]), "row", pair) for p in pres]
    pre_all = lay_out_call(place, pres, shifts, rows)
    hidden_part(0, sent[order[-1]])
    exchange(0)
    parts[1], others[1] = add_call(after(place, sent[order[1]]), parts[1], others[1], jnp.float32, MOST), []
    shares = {}
    for s in order:
        pre_grad(s, *(shares[t][0] for t in shares), *([sent[order[2]]] if s == order[1] else []))
        if s in (1, cols - 1):
            shares[s] = share(s)
    for s in order:
        if s not in shares:
            shares[s] = share(s)

    ins = [inputs]
    for s in range(1, cols):
        ins.append(lax.ppermute(ins[-1], "col", ring))

    right = left = None
    for j in range(1, cols):
        forth, mirror = shares[j], shares[cols - j]
        if j == 1:
            right, left = forth[1], mirror[1]
        elif 2 * j == cols:
            both = add_call(place, right, [left], jnp.float32, MUCH)
            right = left = add_call(place, both, [forth[0]], jnp.bfloat16, LITTLE)
        else:
            right, left = (
                add_call(place, forth[0], [right], jnp.bfloat16, LITTLE),
                add_call(place, mirror[0], [left], jnp.bfloat16, LITTLE),
            )
        if j == cols - 2:
            grad_down = grad_down_call(after(place, right, left), pre_all, cots, scale)
            pre_grad(0, grad_down, ins[-1])
        if j == cols - 1:
            late = after(place, right, left, mine[0])
        right = lax.ppermute(right, "col", [(z, z + 1) for z in range(j)])
        left = lax.ppermute(left, "col", [(z, z - 1) for z in range(cols - j, cols)])
    own = share(0)[0]
    grad_up = grad_up_call(after(late, own), ins, mine, theirs, scale)
    sums = add_call(after(place, grad_up), own, [right, left], jnp.bfloat16, LITTLE)
    return (sums, grad_up, grad_down)


def solution(mesh):
    placed = (
        P(("groups", "col"), "row"),
        P(("groups", "col"), "row"),
        P(("groups", "row"), "col"),
        P("row", "col"),
        P("col", "row"),
    )
    return jax.shard_map(
        per_device,
        mesh=mesh,
        in_specs=placed,
        out_specs=(
            P(("groups", "col"), "row"),
            P(("groups", "row"), "col"),
            P(("groups", "col"), "row"),
        ),
        check_vma=False,
    )
```

```python
import functools
import math

import jax
import jax.numpy as jnp
from jax import lax
from jax.experimental import pallas as pl
from jax.experimental.pallas import tpu as pltpu
from jax.sharding import PartitionSpec as P

LAST = (((1,), (1,)), ((), ()))
FIRST = (((0,), (0,)), ((), ()))
MIB = 1024 * 1024
LITTLE, SOME, MORE, MUCH, MOST = 10**7, 10**8, 10**9, 3 * 10**9, 3 * 10**9


def gelu_parts(values):
    v = values.astype(jnp.float32)
    tanh_val = jnp.tanh(0.7978845608 * (v + 0.044715 * v * v * v))
    return v, tanh_val


def gelu(values):
    v, tanh_val = gelu_parts(values)
    return 0.5 * v * (1.0 + tanh_val)


def gelu_slope(values):
    v, tanh_val = gelu_parts(values)
    return 0.5 * (1.0 + tanh_val) + 0.5 * v * (1.0 - tanh_val * tanh_val) * 0.7978845608 * (
        1.0 + 3.0 * 0.044715 * v * v
    )


def dot(a, b, dims):
    return lax.dot_general(a, b, dims, preferred_element_type=jnp.float32)


def after(value, *first):
    return lax.optimization_barrier((value, *first))[0] if first else value


def tile_of(extent):
    return next(t for t in (256, 128, extent) if extent % t == 0)


def in_vmem():
    return pl.BlockSpec(memory_space=pltpu.VMEM)


def block(index, size, first=0):
    return pl.ds(pl.multiple_of(index * size + first, math.gcd(size, first)), size - first)


def block_at(place_ref, step, cols):
    return lax.rem(place_ref[0] - step + cols, cols)


def core_of(place_ref):
    return lax.rem(place_ref[1], 2)


def call(kernel, place, operands, outs, mib, cost, grid=(1,), in_specs=None, out_specs=None, scratch=()):
    return pl.pallas_call(
        kernel,
        out_shape=outs,
        grid_spec=pltpu.PrefetchScalarGridSpec(
            num_scalar_prefetch=1,
            grid=grid,
            in_specs=in_specs or [in_vmem() for _ in operands],
            out_specs=out_specs or jax.tree.map(lambda _: in_vmem(), outs),
            scratch_shapes=scratch,
        ),
        compiler_params=pltpu.CompilerParams(vmem_limit_bytes=mib * MIB),
        cost_estimate=pl.CostEstimate(flops=cost, bytes_accessed=1024, transcendentals=0),
    )(place, *operands)


def lay_out_kernel(shifts, rows, place_ref, *refs):
    out_ref = refs[-1]
    tokens = refs[0].shape[0]
    for i, ref in enumerate(refs[:-1]):
        owner = lax.rem(place_ref[1] - shifts[i % len(shifts)] + rows, rows)
        if i >= len(shifts):
            owner = owner + 1 - 2 * lax.rem(owner, 2)
        out_ref[block(owner, tokens), :] = ref[...]


def lay_out_call(place, blocks, shifts, rows):
    tokens, hidden = blocks[0].shape
    out = jax.ShapeDtypeStruct((tokens * len(blocks), hidden), jnp.bfloat16)
    return call(functools.partial(lay_out_kernel, shifts, rows), place, blocks, out, 8, SOME)


def take_rows_kernel(place_ref, rows_ref, out_ref):
    out_ref[...] = rows_ref[block(core_of(place_ref), out_ref.shape[0]), :]


def take_rows_call(place, weight):
    out = jax.ShapeDtypeStruct((weight.shape[0] // 2, weight.shape[1]), weight.dtype)
    return call(take_rows_kernel, place, [weight], out, 12, LITTLE)


def hidden_kernel(place_ref, cot_ref, pair_ref, mine_ref, theirs_ref, part_ref, sent_ref):
    half = part_ref.shape[1]
    tile = tile_of(half)
    for first in range(0, half, tile):
        here = pl.ds(first, tile)
        rows = pl.ds(pl.multiple_of(core_of(place_ref) * half + first, tile), tile)
        part = dot(cot_ref[...], mine_ref[here, :], LAST)
        part = part + dot(pair_ref[...], theirs_ref[rows, :], LAST)
        part_ref[:, here] = part
        sent_ref[:, here] = part.astype(jnp.bfloat16)


def hidden_call(place, cot, cot_pair, down_mine, down_pair):
    shape = (cot.shape[0], down_mine.shape[0])
    outs = [jax.ShapeDtypeStruct(shape, jnp.float32), jax.ShapeDtypeStruct(shape, jnp.bfloat16)]
    return call(hidden_kernel, place, [cot, cot_pair, down_mine, down_pair], outs, 12, LITTLE)


def pre_grad_kernel(step, cols, place_ref, pre_ref, part_ref, *refs):
    out_ref = refs[-1]
    tokens, half = part_ref.shape
    rows = 64 if tokens % 64 == 0 else tokens
    columns = block(core_of(place_ref), half)
    start = block_at(place_ref, step, cols) * tokens
    for first in range(0, tokens, rows):
        here = pl.ds(first, rows)
        total = part_ref[here, :]
        for other in refs[:-1]:
            total = total + other[here, :].astype(jnp.float32)
        v = pre_ref[pl.ds(pl.multiple_of(start + first, rows), rows), columns]
        out_ref[here, :] = (total * gelu_slope(v)).astype(jnp.bfloat16)


def pre_grad_call(place, step, cols, pre_all, part, others):
    out = jax.ShapeDtypeStruct(part.shape, jnp.bfloat16)
    kernel = functools.partial(pre_grad_kernel, step, cols)
    return call(kernel, place, [pre_all, part, *others], out, 8, SOME)


def share_kernel(place_ref, mine_ref, theirs_ref, up_ref, out_ref, *sent_refs):
    features, half = up_ref.shape[0], mine_ref.shape[1]
    tile = tile_of(features)
    left, right = block(core_of(place_ref), half), block(1 - core_of(place_ref), half)
    for first in range(0, features, tile):
        here = pl.ds(first, tile)
        total = dot(mine_ref[...], up_ref[here, left], LAST)
        total = total + dot(theirs_ref[...], up_ref[here, right], LAST)
        out_ref[:, here] = total
        for sent in sent_refs:
            sent[:, here] = total.astype(jnp.bfloat16)


def share_call(place, mine, theirs, up_weight, first):
    shape = (mine.shape[0], up_weight.shape[0])
    outs = [jax.ShapeDtypeStruct(shape, jnp.float32)]
    outs += [jax.ShapeDtypeStruct(shape, jnp.bfloat16)] * first
    return call(share_kernel, place, [mine, theirs, up_weight], outs, 12, LITTLE)


def add_kernel(place_ref, part_ref, *refs):
    out_ref = refs[-1]
    rows = 64 if part_ref.shape[0] % 64 == 0 else part_ref.shape[0]
    for first in range(0, part_ref.shape[0], rows):
        here = pl.ds(first, rows)
        total = part_ref[here, :].astype(jnp.float32)
        for arrived in refs[:-1]:
            total = total + arrived[here, :].astype(jnp.float32)
        out_ref[here, :] = total.astype(out_ref.dtype)


def add_call(place, part, arrived, dtype, cost):
    out = jax.ShapeDtypeStruct(part.shape, dtype)
    return call(add_kernel, place, [part, *arrived], out, 4, cost)


def grad_down_kernel(blocks, scale, place_ref, pre_ref, *refs):
    cot_refs, out_ref, cots = refs[:blocks], refs[-2], refs[-1]
    tokens = cot_refs[0].shape[0]

    @pl.when(pl.program_id(0) == 0)
    def _():
        for s in range(blocks):
            cots[block(block_at(place_ref, s, blocks), tokens), :] = cot_refs[s][...]

    activation = gelu(pre_ref[...]).astype(jnp.bfloat16)
    out_ref[...] = dot(activation, cots[...], FIRST) * scale


def grad_down_call(place, pre_all, cots, scale):
    total, hidden = pre_all.shape
    features = cots[0].shape[1]
    tile = tile_of(hidden)
    return call(
        functools.partial(grad_down_kernel, len(cots), scale),
        place,
        [pre_all, *cots],
        jax.ShapeDtypeStruct((hidden, features), jnp.float32),
        14,
        SOME,
        grid=(hidden // tile,),
        in_specs=[pl.BlockSpec((total, tile), lambda i, place: (0, i))]
        + [in_vmem() for _ in cots],
        out_specs=pl.BlockSpec((tile, features), lambda i, place: (i, 0)),
        scratch=[pltpu.VMEM((total, features), jnp.bfloat16)],
    )


def grad_up_kernel(blocks, scale, place_ref, *refs):
    ins, mine, pair = (refs[i * blocks : (i + 1) * blocks] for i in range(3))
    out_ref, inputs, grads = refs[3 * blocks :]
    tokens, half = mine[0].shape
    tile = out_ref.shape[0]

    @pl.when(pl.program_id(0) == 0)
    def _():
        left, right = block(core_of(place_ref), half), block(1 - core_of(place_ref), half)
        for s in range(blocks):
            here = pl.ds(s * tokens, tokens)
            inputs[here, :] = ins[s][...]
            grads[here, left] = mine[s][...]
            grads[here, right] = pair[s][...]

    out_ref[...] = dot(inputs[:, block(pl.program_id(0), tile)], grads[...], FIRST) * scale


def grad_up_call(place, ins, mine, pair, scale):
    tokens, features = ins[0].shape
    total = tokens * len(ins)
    hidden = 2 * mine[0].shape[1]
    tile = tile_of(features)
    return call(
        functools.partial(grad_up_kernel, len(mine), scale),
        place,
        [*ins, *mine, *pair],
        jax.ShapeDtypeStruct((features, hidden), jnp.float32),
        18,
        MORE,
        grid=(features // tile,),
        out_specs=pl.BlockSpec((tile, hidden), lambda i, place: (i, 0)),
        scratch=[
            pltpu.VMEM((total, features), jnp.bfloat16),
            pltpu.VMEM((total, hidden), jnp.bfloat16),
        ],
    )


def per_device(inputs, cotangent, preactivation, up_weight, down_weight):
    cols, rows = lax.axis_size("col"), lax.axis_size("row")
    place = jnp.stack([lax.axis_index("col"), lax.axis_index("row")]).astype(jnp.int32)
    cotangent, preactivation, down_weight = (
        after(x, place) for x in (cotangent, preactivation, down_weight)
    )
    ring = [(i, (i + 1) % cols) for i in range(cols)]
    back = [(i, (i - 1) % cols) for i in range(cols)]
    pair = [(i, i ^ 1) for i in range(rows)]
    shifts = range(0, rows, 2)
    over_x = [[(i, (i + shift) % rows) for i in range(rows)] for shift in shifts[1:]]
    scale = 1.0 / math.sqrt(cotangent.shape[0] * cols)

    pres = [preactivation] + [lax.ppermute(preactivation, "row", to) for to in over_x]
    down_pair = lax.ppermute(down_weight, "row", pair)
    down_mine = take_rows_call(place, down_weight)
    parts, sent, others, mine, theirs = ([None] * cols for _ in range(5))

    def hidden_part(s, *first):
        cot_pair = after(lax.ppermute(cots[s], "row", pair), *first)
        parts[s], sent[s] = hidden_call(place, cots[s], cot_pair, down_mine, down_pair)

    def exchange(s, *first):
        values = after(sent[s], *first)
        others[s] = [lax.ppermute(values, "row", to) for to in over_x]

    def pre_grad(s, *first):
        mine[s] = pre_grad_call(after(place, *first), s, cols, pre_all, parts[s], others[s])
        theirs[s] = lax.ppermute(mine[s], "row", pair)

    def share(s, *first):
        sends = s in (1, cols - 1)
        return share_call(after(place, *first), mine[s], theirs[s], up_weight, sends)

    cots, middle = [cotangent] + [None] * (cols - 1), cols // 2
    order = []
    for s in range(1, middle + 1):
        cots[s] = lax.ppermute(cots[s - 1], "col", ring)
        order.append(s)
        if cols - s > middle:
            cots[cols - s] = lax.ppermute(cots[(cols - s + 1) % cols], "col", back)
            order.append(cols - s)
    arrived = list(cots)

    def hidden_next(i):
        s = order[i]
        arrived[s] = after(cots[s], sent[order[i - 1]] if i else down_mine)
        cot_pair = lax.ppermute(arrived[s], "row", pair)
        if i == 1:
            cot_pair = after(cot_pair, parts[order[0]])
        parts[s], sent[s] = hidden_call(place, cots[s], cot_pair, down_mine, down_pair)
        exchange(s)
        cost = MUCH if i else MOST
        parts[s], others[s] = add_call(place, parts[s], others[s], jnp.float32, cost), []

    for i in range(len(order)):
        hidden_next(i)
    pres = pres + [lax.ppermute(after(p, sent[1]), "row", pair) for p in pres]
    pre_all = lay_out_call(after(place, sent[order[1]]), pres, shifts, rows)
    hidden_part(0, sent[order[-1]])
    exchange(0)
    shares = {}
    for s in order:
        pre_grad(s, *(shares[t][0] for t in shares), *([sent[order[2]]] if s == order[1] else []))
        if s in (1, cols - 1):
            shares[s] = share(s, *([parts[order[2]]] if s == order[1] else []))
    for s in order:
        if s not in shares:
            shares[s] = share(s)

    ins = [inputs]
    for s in range(1, cols):
        ins.append(lax.ppermute(ins[-1], "col", ring))

    right = left = None
    for j in range(1, cols):
        forth, mirror = shares[j], shares[cols - j]
        if j == 1:
            right, left = forth[1], mirror[1]
        elif 2 * j == cols:
            both = add_call(place, right, [left], jnp.float32, MUCH)
            right = left = add_call(place, both, [forth[0]], jnp.bfloat16, LITTLE)
        else:
            right, left = (
                add_call(place, forth[0], [right], jnp.bfloat16, LITTLE),
                add_call(place, mirror[0], [left], jnp.bfloat16, LITTLE),
            )
        if j == cols - 2:
            grad_down = grad_down_call(after(place, right, left), pre_all, cots, scale)
            pre_grad(0, grad_down, ins[-1])
        if j == cols - 1:
            late = after(place, right, left, mine[0])
        right = lax.ppermute(right, "col", [(z, z + 1) for z in range(j)])
        left = lax.ppermute(left, "col", [(z, z - 1) for z in range(cols - j, cols)])
    own = share(0)[0]
    grad_up = grad_up_call(after(late, own), ins, mine, theirs, scale)
    sums = add_call(after(place, grad_up), own, [right, left], jnp.bfloat16, LITTLE)
    return (sums, grad_up, grad_down)


def solution(mesh):
    placed = (
        P(("groups", "col"), "row"),
        P(("groups", "col"), "row"),
        P(("groups", "row"), "col"),
        P("row", "col"),
        P("col", "row"),
    )
    return jax.shard_map(
        per_device,
        mesh=mesh,
        in_specs=placed,
        out_specs=(
            P(("groups", "col"), "row"),
            P(("groups", "row"), "col"),
            P(("groups", "col"), "row"),
        ),
        check_vma=False,
    )
```

```python
import functools
import math

import jax
import jax.numpy as jnp
from jax import lax
from jax.experimental import pallas as pl
from jax.experimental.pallas import tpu as pltpu
from jax.sharding import PartitionSpec as P

LAST = (((1,), (1,)), ((), ()))
FIRST = (((0,), (0,)), ((), ()))
MIB = 1024 * 1024
LITTLE, SOME, MORE, MUCH, MOST = 10**7, 10**8, 10**9, 3 * 10**9, 8 * 10**9


def gelu_parts(values):
    v = values.astype(jnp.float32)
    tanh_val = jnp.tanh(0.7978845608 * (v + 0.044715 * v * v * v))
    return v, tanh_val


def gelu(values):
    v, tanh_val = gelu_parts(values)
    return 0.5 * v * (1.0 + tanh_val)


def gelu_slope(values):
    v, tanh_val = gelu_parts(values)
    return 0.5 * (1.0 + tanh_val) + 0.5 * v * (1.0 - tanh_val * tanh_val) * 0.7978845608 * (
        1.0 + 3.0 * 0.044715 * v * v
    )


def dot(a, b, dims):
    return lax.dot_general(a, b, dims, preferred_element_type=jnp.float32)


def after(value, *first):
    return lax.optimization_barrier((value, *first))[0] if first else value


def tile_of(extent):
    return next(t for t in (256, 128, extent) if extent % t == 0)


def in_vmem():
    return pl.BlockSpec(memory_space=pltpu.VMEM)


def block(index, size, first=0):
    return pl.ds(pl.multiple_of(index * size + first, math.gcd(size, first)), size - first)


def block_at(place_ref, step, cols):
    return lax.rem(place_ref[0] - step + cols, cols)


def core_of(place_ref):
    return lax.rem(place_ref[1], 2)


ADD_COST = {1: MUCH, 2: MOST}


def call(kernel, place, operands, outs, mib, cost, grid=(1,), in_specs=None, out_specs=None, scratch=()):
    return pl.pallas_call(
        kernel,
        out_shape=outs,
        grid_spec=pltpu.PrefetchScalarGridSpec(
            num_scalar_prefetch=1,
            grid=grid,
            in_specs=in_specs or [in_vmem() for _ in operands],
            out_specs=out_specs or jax.tree.map(lambda _: in_vmem(), outs),
            scratch_shapes=scratch,
        ),
        compiler_params=pltpu.CompilerParams(vmem_limit_bytes=mib * MIB),
        cost_estimate=pl.CostEstimate(flops=cost, bytes_accessed=1024, transcendentals=0),
    )(place, *operands)


def take_half_kernel(place_ref, mine_ref, theirs_ref, out_ref):
    tokens, half = mine_ref.shape[0], out_ref.shape[1]
    core = core_of(place_ref)
    out_ref[block(core, tokens), :] = mine_ref[:, block(core, half)]
    out_ref[block(1 - core, tokens), :] = theirs_ref[:, block(core, half)]


def take_half_call(place, mine, theirs):
    tokens, hidden = mine.shape
    out = jax.ShapeDtypeStruct((2 * tokens, hidden // 2), jnp.bfloat16)
    return call(take_half_kernel, place, [mine, theirs], out, 8, LITTLE)


def lay_out_kernel(chips, place_ref, *refs):
    blocks, (pre_ref, act_ref) = refs[:chips], refs[chips:]
    tokens = blocks[0].shape[0]
    rows = 64 if tokens % 64 == 0 else tokens
    for i, ref in enumerate(blocks):
        owner = lax.rem(lax.div(place_ref[1], 2) - i + chips, chips)
        pre_ref[block(owner, tokens), :] = ref[...]
        for first in range(0, tokens, rows):
            here = pl.ds(pl.multiple_of(owner * tokens + first, rows), rows)
            act_ref[here, :] = gelu(ref[pl.ds(first, rows), :]).astype(jnp.bfloat16)


def lay_out_call(place, blocks):
    tokens, half = blocks[0].shape
    out = jax.ShapeDtypeStruct((tokens * len(blocks), half), jnp.bfloat16)
    kernel = functools.partial(lay_out_kernel, len(blocks))
    return call(kernel, place, blocks, [out, out], 12, 2 * MUCH)


def hidden_kernel(place_ref, cot_ref, down_ref, own_ref, other_ref):
    half = own_ref.shape[1]
    tile = tile_of(half)
    for first in range(0, half, tile):
        here = pl.ds(first, tile)
        for core, out_ref in ((1 - core_of(place_ref), other_ref), (core_of(place_ref), own_ref)):
            rows = pl.ds(pl.multiple_of(core * half + first, tile), tile)
            part = dot(cot_ref[...], down_ref[rows, :], LAST)
            out_ref[:, here] = part.astype(out_ref.dtype)


def hidden_call(place, cot, down_weight):
    shape = (cot.shape[0], down_weight.shape[0] // 2)
    outs = [jax.ShapeDtypeStruct(shape, jnp.float32), jax.ShapeDtypeStruct(shape, jnp.bfloat16)]
    return call(hidden_kernel, place, [cot, down_weight], outs, 10, LITTLE)


def pre_grad_kernel(step, cols, place_ref, pre_ref, part_ref, *refs):
    out_ref = refs[-1]
    tokens, half = part_ref.shape
    rows = 64 if tokens % 64 == 0 else tokens
    start = block_at(place_ref, step, cols) * tokens
    for first in range(0, tokens, rows):
        here = pl.ds(first, rows)
        total = part_ref[here, :]
        for other in refs[:-1]:
            total = total + other[here, :].astype(jnp.float32)
        v = pre_ref[pl.ds(pl.multiple_of(start + first, rows), rows), :]
        out_ref[here, :] = (total * gelu_slope(v)).astype(jnp.bfloat16)


def pre_grad_call(place, step, cols, pre_all, part, others):
    out = jax.ShapeDtypeStruct(part.shape, jnp.bfloat16)
    kernel = functools.partial(pre_grad_kernel, step, cols)
    return call(kernel, place, [pre_all, part, *others], out, 8, SOME)


def share_kernel(place_ref, mine_ref, theirs_ref, up_ref, out_ref, *sent_refs):
    features, half = up_ref.shape[0], mine_ref.shape[1]
    tile = tile_of(features)
    left, right = block(core_of(place_ref), half), block(1 - core_of(place_ref), half)
    for first in range(0, features, tile):
        here = pl.ds(first, tile)
        total = dot(mine_ref[...], up_ref[here, left], LAST)
        total = total + dot(theirs_ref[...], up_ref[here, right], LAST)
        out_ref[:, here] = total
        for sent in sent_refs:
            sent[:, here] = total.astype(jnp.bfloat16)


def share_call(place, mine, theirs, up_weight, first):
    shape = (mine.shape[0], up_weight.shape[0])
    outs = [jax.ShapeDtypeStruct(shape, jnp.float32)]
    outs += [jax.ShapeDtypeStruct(shape, jnp.bfloat16)] * first
    return call(share_kernel, place, [mine, theirs, up_weight], outs, 12, LITTLE)


def add_kernel(place_ref, part_ref, *refs):
    out_ref = refs[-1]
    rows = 64 if part_ref.shape[0] % 64 == 0 else part_ref.shape[0]
    for first in range(0, part_ref.shape[0], rows):
        here = pl.ds(first, rows)
        total = part_ref[here, :].astype(jnp.float32)
        for arrived in refs[:-1]:
            total = total + arrived[here, :].astype(jnp.float32)
        out_ref[here, :] = total.astype(out_ref.dtype)


def add_call(place, part, arrived, dtype, cost):
    out = jax.ShapeDtypeStruct(part.shape, dtype)
    return call(add_kernel, place, [part, *arrived], out, 4, cost)


def grad_down_kernel(blocks, scale, place_ref, mine_ref, theirs_ref, *refs):
    cot_refs, out_ref, cots = refs[:blocks], refs[-2], refs[-1]
    tokens, tile = cot_refs[0].shape[0], out_ref.shape[0]
    i, steps = pl.program_id(0), mine_ref.shape[1] // tile

    @pl.when(i == 0)
    def _():
        for s in range(blocks):
            cots[block(block_at(place_ref, s, blocks), tokens), :] = cot_refs[s][...]

    def product(act_ref, at):
        out_ref[...] = dot(act_ref[:, block(at, tile)], cots[...], FIRST) * scale

    pl.when(i < steps)(lambda: product(mine_ref, i))
    pl.when(i >= steps)(lambda: product(theirs_ref, i - steps))


def grad_down_call(place, act_mine, act_theirs, cots, scale):
    (total, half), features = act_mine.shape, cots[0].shape[1]
    tile = tile_of(half)
    steps = half // tile

    def rows(i, place):
        core = lax.rem(place[1], 2)
        return jnp.where(i < steps, core * steps + i, (1 - core) * steps + i - steps), 0

    return call(
        functools.partial(grad_down_kernel, len(cots), scale),
        place,
        [act_mine, act_theirs, *cots],
        jax.ShapeDtypeStruct((2 * half, features), jnp.float32),
        14,
        SOME,
        grid=(2 * steps,),
        out_specs=pl.BlockSpec((tile, features), rows),
        scratch=[pltpu.VMEM((total, features), jnp.bfloat16)],
    )


def grad_up_kernel(blocks, scale, place_ref, *refs):
    ins, mine, pair = (refs[i * blocks : (i + 1) * blocks] for i in range(3))
    out_ref, inputs, grads = refs[3 * blocks :]
    tokens, half = mine[0].shape
    tile = out_ref.shape[0]

    @pl.when(pl.program_id(0) == 0)
    def _():
        left, right = block(core_of(place_ref), half), block(1 - core_of(place_ref), half)
        for s in range(blocks):
            here = pl.ds(s * tokens, tokens)
            inputs[here, :] = ins[s][...]
            grads[here, left] = mine[s][...]
            grads[here, right] = pair[s][...]

    out_ref[...] = dot(inputs[:, block(pl.program_id(0), tile)], grads[...], FIRST) * scale


def grad_up_call(place, ins, mine, pair, scale):
    tokens, features = ins[0].shape
    total = tokens * len(ins)
    hidden = 2 * mine[0].shape[1]
    tile = tile_of(features)
    return call(
        functools.partial(grad_up_kernel, len(mine), scale),
        place,
        [*ins, *mine, *pair],
        jax.ShapeDtypeStruct((features, hidden), jnp.float32),
        18,
        MUCH,
        grid=(features // tile,),
        out_specs=pl.BlockSpec((tile, hidden), lambda i, place: (i, 0)),
        scratch=[
            pltpu.VMEM((total, features), jnp.bfloat16),
            pltpu.VMEM((total, hidden), jnp.bfloat16),
        ],
    )


def per_device(inputs, cotangent, preactivation, up_weight, down_weight):
    cols, rows = lax.axis_size("col"), lax.axis_size("row")
    place = jnp.stack([lax.axis_index("col"), lax.axis_index("row")]).astype(jnp.int32)
    cotangent, preactivation = after(cotangent, place), after(preactivation, place)
    ring = [(i, (i + 1) % cols) for i in range(cols)]
    pair = [(i, i ^ 1) for i in range(rows)]
    over_x = [[(i, (i + shift) % rows) for i in range(rows)] for shift in range(2, rows, 2)]
    scale = 1.0 / math.sqrt(cotangent.shape[0] * cols)
    last = cols - 1

    pre = take_half_call(place, preactivation, lax.ppermute(preactivation, "row", pair))
    pres = [pre] + [lax.ppermute(pre, "row", to) for to in over_x]
    parts, sent, others, mine, theirs = ([None] * cols for _ in range(5))

    def hidden_part(s, *first):
        own, other = hidden_call(after(place, *first), cots[s], down_weight)
        arrived = lax.ppermute(other, "row", pair)
        sent[s] = add_call(place, own, [arrived], jnp.bfloat16, LITTLE)
        parts[s] = own, arrived

    def exchange(s, *first):
        values = after(sent[s], *first)
        others[s] = [lax.ppermute(values, "row", to) for to in over_x]

    def pre_grad(s, *first):
        own, arrived = parts[s]
        total = add_call(after(place, *first), own, [arrived, *others[s]], jnp.float32, ADD_COST.get(s, MUCH))
        mine[s] = pre_grad_call(place, s, cols, pre_all, total, [])
        theirs[s] = lax.ppermute(mine[s], "row", pair)

    def share(s, *first):
        return share_call(after(place, *first), mine[s], theirs[s], up_weight, s == 1)

    cots = [cotangent]
    hidden_part(0)
    for s in range(1, cols):
        arriving = lax.ppermute(cots[s - 1], "col", ring)
        cots.append(after(arriving, sent[s - 1]) if s > 1 else after(arriving, pre, parts[0][0]))
        if s < last:
            hidden_part(s)
            exchange(s)
    ins = [inputs, lax.ppermute(after(inputs, cots[1]), "col", ring)]
    pre_all, act = lay_out_call(place, pres)
    act_theirs = lax.ppermute(act, "row", pair)

    pre_grad(1, pre_all)
    sums = share(1)[1]
    cots[last] = after(cots[last], sums)
    hidden_part(last, sums)
    exchange(last)
    exchange(0, sent[last])
    for s in range(2, cols):
        arrived = lax.ppermute(sums, "col", ring)
        ins.append(lax.ppermute(after(ins[-1], sums), "col", ring))
        pre_grad(s, *([late] if s > 2 else [ins[1]]))
        first = []
        if s == last:
            grad_down = grad_down_call(
                after(place, mine[s], *ins[2:s]), act, act_theirs, cots, scale
            )
            pre_grad(0, grad_down)
            first = [grad_down]
        if s == 2:
            arrived = add_call(place, arrived, [], jnp.float32, MUCH)
        part = share(s, *first)[0]
        sums = late = add_call(place, part, [arrived], jnp.bfloat16, LITTLE)
    arrived = lax.ppermute(sums, "col", ring)
    part = share(0, sums)[0]
    grad_up = grad_up_call(after(place, part), ins, mine, theirs, scale)
    sums = add_call(after(place, grad_up), part, [arrived], jnp.bfloat16, LITTLE)
    return (sums, grad_up, grad_down)


def solution(mesh):
    placed = (
        P(("groups", "col"), "row"),
        P(("groups", "col"), "row"),
        P(("groups", "row"), "col"),
        P("row", "col"),
        P("col", "row"),
    )
    return jax.shard_map(
        per_device,
        mesh=mesh,
        in_specs=placed,
        out_specs=(
            P(("groups", "col"), "row"),
            P(("groups", "row"), "col"),
            P(("groups", "col"), "row"),
        ),
        check_vma=False,
    )
```

```python
import functools
import math

import jax
import jax.numpy as jnp
from jax import lax
from jax.experimental import pallas as pl
from jax.experimental.pallas import tpu as pltpu
from jax.sharding import PartitionSpec as P

LAST = (((1,), (1,)), ((), ()))
FIRST = (((0,), (0,)), ((), ()))
MIB = 1024 * 1024
LITTLE, SOME, MORE, MUCH, MOST = 10**7, 10**8, 10**9, 3 * 10**9, 8 * 10**9


def gelu_parts(values):
    v = values.astype(jnp.float32)
    tanh_val = jnp.tanh(0.7978845608 * (v + 0.044715 * v * v * v))
    return v, tanh_val


def gelu(values):
    v, tanh_val = gelu_parts(values)
    return 0.5 * v * (1.0 + tanh_val)


def gelu_slope(values):
    v, tanh_val = gelu_parts(values)
    return 0.5 * (1.0 + tanh_val) + 0.5 * v * (1.0 - tanh_val * tanh_val) * 0.7978845608 * (
        1.0 + 3.0 * 0.044715 * v * v
    )


def dot(a, b, dims):
    return lax.dot_general(a, b, dims, preferred_element_type=jnp.float32)


def after(value, *first):
    return lax.optimization_barrier((value, *first))[0] if first else value


def tile_of(extent, most=512):
    return next(t for t in (most, 256, 128, extent) if extent % t == 0)


def in_vmem():
    return pl.BlockSpec(memory_space=pltpu.VMEM)


def block(index, size, first=0):
    return pl.ds(pl.multiple_of(index * size + first, math.gcd(size, first)), size - first)


def block_at(place_ref, step, cols):
    return lax.rem(place_ref[0] - step + cols, cols)


def core_of(place_ref):
    return lax.rem(place_ref[1], 2)


ADD_COST = {1: MUCH, 2: MOST}


def call(kernel, place, operands, outs, mib, cost, grid=(1,), in_specs=None, out_specs=None, scratch=()):
    return pl.pallas_call(
        kernel,
        out_shape=outs,
        grid_spec=pltpu.PrefetchScalarGridSpec(
            num_scalar_prefetch=1,
            grid=grid,
            in_specs=in_specs or [in_vmem() for _ in operands],
            out_specs=out_specs or jax.tree.map(lambda _: in_vmem(), outs),
            scratch_shapes=scratch,
        ),
        compiler_params=pltpu.CompilerParams(vmem_limit_bytes=mib * MIB),
        cost_estimate=pl.CostEstimate(flops=cost, bytes_accessed=1024, transcendentals=0),
    )(place, *operands)


def take_half_kernel(place_ref, mine_ref, theirs_ref, out_ref):
    tokens, half = mine_ref.shape[0], out_ref.shape[1]
    core = core_of(place_ref)
    out_ref[block(core, tokens), :] = mine_ref[:, block(core, half)]
    out_ref[block(1 - core, tokens), :] = theirs_ref[:, block(core, half)]


def take_half_call(place, mine, theirs):
    tokens, hidden = mine.shape
    out = jax.ShapeDtypeStruct((2 * tokens, hidden // 2), jnp.bfloat16)
    return call(take_half_kernel, place, [mine, theirs], out, 8, LITTLE)


def lay_out_kernel(chips, place_ref, *refs):
    blocks, (pre_ref, act_ref) = refs[:chips], refs[chips:]
    tokens = blocks[0].shape[0]
    rows = 64 if tokens % 64 == 0 else tokens
    for i, ref in enumerate(blocks):
        owner = lax.rem(lax.div(place_ref[1], 2) - i + chips, chips)
        pre_ref[block(owner, tokens), :] = ref[...]
        for first in range(0, tokens, rows):
            here = pl.ds(pl.multiple_of(owner * tokens + first, rows), rows)
            act_ref[here, :] = gelu(ref[pl.ds(first, rows), :]).astype(jnp.bfloat16)


def lay_out_call(place, blocks):
    tokens, half = blocks[0].shape
    out = jax.ShapeDtypeStruct((tokens * len(blocks), half), jnp.bfloat16)
    kernel = functools.partial(lay_out_kernel, len(blocks))
    return call(kernel, place, blocks, [out, out], 12, 2 * MUCH)


def hidden_kernel(place_ref, cot_ref, down_ref, own_ref, other_ref):
    half = own_ref.shape[1]
    tile = tile_of(half)
    for first in range(0, half, tile):
        here = pl.ds(first, tile)
        for core, out_ref in ((1 - core_of(place_ref), other_ref), (core_of(place_ref), own_ref)):
            rows = pl.ds(pl.multiple_of(core * half + first, tile), tile)
            part = dot(cot_ref[...], down_ref[rows, :], LAST)
            out_ref[:, here] = part.astype(out_ref.dtype)


def hidden_call(place, cot, down_weight):
    shape = (cot.shape[0], down_weight.shape[0] // 2)
    outs = [jax.ShapeDtypeStruct(shape, jnp.float32), jax.ShapeDtypeStruct(shape, jnp.bfloat16)]
    return call(hidden_kernel, place, [cot, down_weight], outs, 10, LITTLE)


def pre_grad_kernel(step, cols, place_ref, pre_ref, part_ref, *refs):
    out_ref = refs[-1]
    tokens, half = part_ref.shape
    rows = 64 if tokens % 64 == 0 else tokens
    start = block_at(place_ref, step, cols) * tokens
    for first in range(0, tokens, rows):
        here = pl.ds(first, rows)
        total = part_ref[here, :]
        for other in refs[:-1]:
            total = total + other[here, :].astype(jnp.float32)
        v = pre_ref[pl.ds(pl.multiple_of(start + first, rows), rows), :]
        out_ref[here, :] = (total * gelu_slope(v)).astype(jnp.bfloat16)


def pre_grad_call(place, step, cols, pre_all, part, others):
    out = jax.ShapeDtypeStruct(part.shape, jnp.bfloat16)
    kernel = functools.partial(pre_grad_kernel, step, cols)
    return call(kernel, place, [pre_all, part, *others], out, 8, SOME)


def share_kernel(place_ref, mine_ref, theirs_ref, up_ref, out_ref, *sent_refs):
    features, half = up_ref.shape[0], mine_ref.shape[1]
    tile = tile_of(features)
    left, right = block(core_of(place_ref), half), block(1 - core_of(place_ref), half)
    for first in range(0, features, tile):
        here = pl.ds(first, tile)
        total = dot(mine_ref[...], up_ref[here, left], LAST)
        total = total + dot(theirs_ref[...], up_ref[here, right], LAST)
        out_ref[:, here] = total
        for sent in sent_refs:
            sent[:, here] = total.astype(jnp.bfloat16)


def share_call(place, mine, theirs, up_weight, first):
    shape = (mine.shape[0], up_weight.shape[0])
    outs = [jax.ShapeDtypeStruct(shape, jnp.float32)]
    outs += [jax.ShapeDtypeStruct(shape, jnp.bfloat16)] * first
    return call(share_kernel, place, [mine, theirs, up_weight], outs, 12, LITTLE)


def add_kernel(place_ref, part_ref, *refs):
    out_ref = refs[-1]
    rows = 64 if part_ref.shape[0] % 64 == 0 else part_ref.shape[0]
    for first in range(0, part_ref.shape[0], rows):
        here = pl.ds(first, rows)
        total = part_ref[here, :].astype(jnp.float32)
        for arrived in refs[:-1]:
            total = total + arrived[here, :].astype(jnp.float32)
        out_ref[here, :] = total.astype(out_ref.dtype)


def add_call(place, part, arrived, dtype, cost):
    out = jax.ShapeDtypeStruct(part.shape, dtype)
    return call(add_kernel, place, [part, *arrived], out, 4, cost)


def grad_down_kernel(blocks, scale, place_ref, mine_ref, theirs_ref, *refs):
    cot_refs, out_ref, cots = refs[:blocks], refs[-2], refs[-1]
    tokens, tile = cot_refs[0].shape[0], out_ref.shape[0]
    i, steps = pl.program_id(0), mine_ref.shape[1] // tile

    @pl.when(i == 0)
    def _():
        for s in range(blocks):
            cots[block(block_at(place_ref, s, blocks), tokens), :] = cot_refs[s][...]

    def product(act_ref, at):
        out_ref[...] = dot(act_ref[:, block(at, tile)], cots[...], FIRST) * scale

    pl.when(i < steps)(lambda: product(mine_ref, i))
    pl.when(i >= steps)(lambda: product(theirs_ref, i - steps))


def grad_down_call(place, act_mine, act_theirs, cots, scale):
    (total, half), features = act_mine.shape, cots[0].shape[1]
    tile = tile_of(half)
    steps = half // tile

    def rows(i, place):
        core = lax.rem(place[1], 2)
        return jnp.where(i < steps, core * steps + i, (1 - core) * steps + i - steps), 0

    return call(
        functools.partial(grad_down_kernel, len(cots), scale),
        place,
        [act_mine, act_theirs, *cots],
        jax.ShapeDtypeStruct((2 * half, features), jnp.float32),
        14,
        SOME,
        grid=(2 * steps,),
        out_specs=pl.BlockSpec((tile, features), rows),
        scratch=[pltpu.VMEM((total, features), jnp.bfloat16)],
    )


def join_kernel(place_ref, *refs):
    tokens = refs[0].shape[0]
    for s, ref in enumerate(refs[:-1]):
        refs[-1][pl.ds(s * tokens, tokens), :] = ref[...]


def join_call(place, blocks):
    tokens, features = blocks[0].shape
    out = jax.ShapeDtypeStruct((tokens * len(blocks), features), blocks[0].dtype)
    return call(join_kernel, place, blocks, out, 8, MOST)


def grad_up_kernel(blocks, scale, place_ref, inputs, *refs):
    mine, pair = refs[:blocks], refs[blocks : 2 * blocks]
    out_ref, grads = refs[2 * blocks :]
    tokens, half = mine[0].shape
    tile = out_ref.shape[0]

    @pl.when(pl.program_id(0) == 0)
    def _():
        left, right = block(core_of(place_ref), half), block(1 - core_of(place_ref), half)
        for s in range(blocks):
            here = pl.ds(s * tokens, tokens)
            grads[here, left] = mine[s][...]
            grads[here, right] = pair[s][...]

    out_ref[...] = dot(inputs[:, block(pl.program_id(0), tile)], grads[...], FIRST) * scale


def grad_up_call(place, inputs, mine, pair, scale):
    total, features = inputs.shape
    hidden = 2 * mine[0].shape[1]
    tile = tile_of(features, 256)
    return call(
        functools.partial(grad_up_kernel, len(mine), scale),
        place,
        [inputs, *mine, *pair],
        jax.ShapeDtypeStruct((features, hidden), jnp.float32),
        18,
        MUCH,
        grid=(features // tile,),
        out_specs=pl.BlockSpec((tile, hidden), lambda i, place: (i, 0)),
        scratch=[
            pltpu.VMEM((total, hidden), jnp.bfloat16),
        ],
    )


def per_device(inputs, cotangent, preactivation, up_weight, down_weight):
    cols, rows = lax.axis_size("col"), lax.axis_size("row")
    place = jnp.stack([lax.axis_index("col"), lax.axis_index("row")]).astype(jnp.int32)
    cotangent, preactivation = after(cotangent, place), after(preactivation, place)
    ring = [(i, (i + 1) % cols) for i in range(cols)]
    pair = [(i, i ^ 1) for i in range(rows)]
    over_x = [[(i, (i + shift) % rows) for i in range(rows)] for shift in range(2, rows, 2)]
    scale = 1.0 / math.sqrt(cotangent.shape[0] * cols)
    last = cols - 1

    pre = take_half_call(place, preactivation, lax.ppermute(preactivation, "row", pair))
    pres = [pre] + [lax.ppermute(pre, "row", to) for to in over_x]
    parts, sent, others, mine, theirs = ([None] * cols for _ in range(5))

    def hidden_part(s, *first):
        own, other = hidden_call(after(place, *first), cots[s], down_weight)
        arrived = lax.ppermute(other, "row", pair)
        sent[s] = add_call(place, own, [arrived], jnp.bfloat16, LITTLE)
        parts[s] = own, arrived

    def exchange(s, *first):
        values = after(sent[s], *first)
        others[s] = [lax.ppermute(values, "row", to) for to in over_x]

    def pre_grad(s, *first):
        own, arrived = parts[s]
        total = add_call(after(place, *first), own, [arrived, *others[s]], jnp.float32, ADD_COST.get(s, MUCH))
        mine[s] = pre_grad_call(place, s, cols, pre_all, total, [])
        theirs[s] = lax.ppermute(mine[s], "row", pair)

    def share(s, *first):
        return share_call(after(place, *first), mine[s], theirs[s], up_weight, s == 1)

    cots = [cotangent]
    hidden_part(0)
    for s in range(1, cols):
        arriving = lax.ppermute(cots[s - 1], "col", ring)
        cots.append(after(arriving, sent[s - 1]) if s > 1 else after(arriving, pre, parts[0][0]))
        if s < last:
            hidden_part(s)
            exchange(s)
    ins = [inputs, lax.ppermute(after(inputs, cots[last - 1]), "col", ring)]
    pre_all, act = lay_out_call(place, pres)
    act_theirs = lax.ppermute(act, "row", pair)

    pre_grad(1, pre_all)
    sums = share(1)[1]
    cots[last] = after(cots[last], sums)
    hidden_part(last, sums)
    exchange(last)
    exchange(0, sent[last])
    for s in range(2, cols):
        arrived = lax.ppermute(sums, "col", ring)
        pre_grad(s, *([late] if s > 2 else []))
        ins.append(lax.ppermute(after(ins[-1], sums, mine[s]), "col", ring))
        first = []
        if s == last:
            grad_down = grad_down_call(
                after(place, mine[s]), act, act_theirs, cots, scale
            )
            pre_grad(0, grad_down)
            first = [grad_down]
        if s == 2:
            arrived = add_call(place, arrived, [], jnp.float32, MOST)
        part = share(s, *first)[0]
        sums = late = add_call(place, part, [arrived], jnp.bfloat16, LITTLE)
    arrived = lax.ppermute(sums, "col", ring)
    part = share(0, sums)[0]
    grad_up = grad_up_call(after(place, part), join_call(place, ins), mine, theirs, scale)
    sums = add_call(after(place, grad_up), part, [arrived], jnp.bfloat16, LITTLE)
    return (sums, grad_up, grad_down)


def solution(mesh):
    placed = (
        P(("groups", "col"), "row"),
        P(("groups", "col"), "row"),
        P(("groups", "row"), "col"),
        P("row", "col"),
        P("col", "row"),
    )
    return jax.shard_map(
        per_device,
        mesh=mesh,
        in_specs=placed,
        out_specs=(
            P(("groups", "col"), "row"),
            P(("groups", "row"), "col"),
            P(("groups", "col"), "row"),
        ),
        check_vma=False,
    )
```

```python
import functools
import math

import jax
import jax.numpy as jnp
from jax import lax
from jax.experimental import pallas as pl
from jax.experimental.pallas import tpu as pltpu
from jax.sharding import PartitionSpec as P

LAST = (((1,), (1,)), ((), ()))
FIRST = (((0,), (0,)), ((), ()))
MIB = 1024 * 1024
LITTLE, SOME, MORE, MUCH, MOST = 10**7, 10**8, 10**9, 3 * 10**9, 8 * 10**9


def gelu_parts(values):
    v = values.astype(jnp.float32)
    tanh_val = jnp.tanh(0.7978845608 * (v + 0.044715 * v * v * v))
    return v, tanh_val


def gelu(values):
    v, tanh_val = gelu_parts(values)
    return 0.5 * v * (1.0 + tanh_val)


def gelu_slope(values):
    v, tanh_val = gelu_parts(values)
    return 0.5 * (1.0 + tanh_val) + 0.5 * v * (1.0 - tanh_val * tanh_val) * 0.7978845608 * (
        1.0 + 3.0 * 0.044715 * v * v
    )


def dot(a, b, dims):
    return lax.dot_general(a, b, dims, preferred_element_type=jnp.float32)


def after(value, *first):
    return lax.optimization_barrier((value, *first))[0] if first else value


def tile_of(extent, most=512):
    return next(t for t in (most, 256, 128, extent) if extent % t == 0)


def in_vmem():
    return pl.BlockSpec(memory_space=pltpu.VMEM)


def block(index, size, first=0):
    return pl.ds(pl.multiple_of(index * size + first, math.gcd(size, first)), size - first)


def block_at(place_ref, step, cols):
    return lax.rem(place_ref[0] - step + cols, cols)


def core_of(place_ref):
    return lax.rem(place_ref[1], 2)


ADD_COST = {1: MUCH, 2: MOST}


def call(kernel, place, operands, outs, mib, cost, grid=(1,), in_specs=None, out_specs=None, scratch=()):
    return pl.pallas_call(
        kernel,
        out_shape=outs,
        grid_spec=pltpu.PrefetchScalarGridSpec(
            num_scalar_prefetch=1,
            grid=grid,
            in_specs=in_specs or [in_vmem() for _ in operands],
            out_specs=out_specs or jax.tree.map(lambda _: in_vmem(), outs),
            scratch_shapes=scratch,
        ),
        compiler_params=pltpu.CompilerParams(vmem_limit_bytes=mib * MIB),
        cost_estimate=pl.CostEstimate(flops=cost, bytes_accessed=1024, transcendentals=0),
    )(place, *operands)


def take_half_kernel(place_ref, mine_ref, theirs_ref, out_ref):
    tokens, half = mine_ref.shape[0], out_ref.shape[1]
    core = core_of(place_ref)
    out_ref[block(core, tokens), :] = mine_ref[:, block(core, half)]
    out_ref[block(1 - core, tokens), :] = theirs_ref[:, block(core, half)]


def take_half_call(place, mine, theirs):
    tokens, hidden = mine.shape
    out = jax.ShapeDtypeStruct((2 * tokens, hidden // 2), jnp.bfloat16)
    return call(take_half_kernel, place, [mine, theirs], out, 8, LITTLE)


def lay_out_kernel(chips, place_ref, *refs):
    blocks, (pre_ref, act_ref) = refs[:chips], refs[chips:]
    tokens = blocks[0].shape[0]
    rows = 64 if tokens % 64 == 0 else tokens
    for i, ref in enumerate(blocks):
        owner = lax.rem(lax.div(place_ref[1], 2) - i + chips, chips)
        pre_ref[block(owner, tokens), :] = ref[...]
        for first in range(0, tokens, rows):
            here = pl.ds(pl.multiple_of(owner * tokens + first, rows), rows)
            act_ref[here, :] = gelu(ref[pl.ds(first, rows), :]).astype(jnp.bfloat16)


def lay_out_call(place, blocks):
    tokens, half = blocks[0].shape
    out = jax.ShapeDtypeStruct((tokens * len(blocks), half), jnp.bfloat16)
    kernel = functools.partial(lay_out_kernel, len(blocks))
    return call(kernel, place, blocks, [out, out], 12, 2 * MUCH)


def hidden_kernel(place_ref, cot_ref, down_ref, own_ref, other_ref):
    half = own_ref.shape[1]
    tile = tile_of(half)
    for first in range(0, half, tile):
        here = pl.ds(first, tile)
        for core, out_ref in ((1 - core_of(place_ref), other_ref), (core_of(place_ref), own_ref)):
            rows = pl.ds(pl.multiple_of(core * half + first, tile), tile)
            part = dot(cot_ref[...], down_ref[rows, :], LAST)
            out_ref[:, here] = part.astype(out_ref.dtype)


def hidden_call(place, cot, down_weight):
    shape = (cot.shape[0], down_weight.shape[0] // 2)
    outs = [jax.ShapeDtypeStruct(shape, jnp.float32), jax.ShapeDtypeStruct(shape, jnp.bfloat16)]
    return call(hidden_kernel, place, [cot, down_weight], outs, 10, LITTLE)


def pre_grad_kernel(step, cols, place_ref, pre_ref, part_ref, *refs):
    out_ref = refs[-1]
    tokens, half = part_ref.shape
    rows = 64 if tokens % 64 == 0 else tokens
    start = block_at(place_ref, step, cols) * tokens
    for first in range(0, tokens, rows):
        here = pl.ds(first, rows)
        total = part_ref[here, :]
        for other in refs[:-1]:
            total = total + other[here, :].astype(jnp.float32)
        v = pre_ref[pl.ds(pl.multiple_of(start + first, rows), rows), :]
        out_ref[here, :] = (total * gelu_slope(v)).astype(jnp.bfloat16)


def pre_grad_call(place, step, cols, pre_all, part, others):
    out = jax.ShapeDtypeStruct(part.shape, jnp.bfloat16)
    kernel = functools.partial(pre_grad_kernel, step, cols)
    return call(kernel, place, [pre_all, part, *others], out, 8, SOME)


def share_kernel(place_ref, mine_ref, theirs_ref, up_ref, out_ref, *sent_refs):
    features, half = up_ref.shape[0], mine_ref.shape[1]
    tile = tile_of(features)
    left, right = block(core_of(place_ref), half), block(1 - core_of(place_ref), half)
    for first in range(0, features, tile):
        here = pl.ds(first, tile)
        total = dot(mine_ref[...], up_ref[here, left], LAST)
        total = total + dot(theirs_ref[...], up_ref[here, right], LAST)
        out_ref[:, here] = total
        for sent in sent_refs:
            sent[:, here] = total.astype(jnp.bfloat16)


def share_call(place, mine, theirs, up_weight, first):
    shape = (mine.shape[0], up_weight.shape[0])
    outs = [jax.ShapeDtypeStruct(shape, jnp.float32)]
    outs += [jax.ShapeDtypeStruct(shape, jnp.bfloat16)] * first
    return call(share_kernel, place, [mine, theirs, up_weight], outs, 12, LITTLE)


def add_kernel(place_ref, part_ref, *refs):
    out_ref = refs[-1]
    rows = 64 if part_ref.shape[0] % 64 == 0 else part_ref.shape[0]
    for first in range(0, part_ref.shape[0], rows):
        here = pl.ds(first, rows)
        total = part_ref[here, :].astype(jnp.float32)
        for arrived in refs[:-1]:
            total = total + arrived[here, :].astype(jnp.float32)
        out_ref[here, :] = total.astype(out_ref.dtype)


def add_call(place, part, arrived, dtype, cost):
    out = jax.ShapeDtypeStruct(part.shape, dtype)
    return call(add_kernel, place, [part, *arrived], out, 4, cost)


def grad_down_kernel(blocks, scale, place_ref, mine_ref, theirs_ref, *refs):
    cot_refs, out_ref, cots = refs[:blocks], refs[-2], refs[-1]
    tokens, tile = cot_refs[0].shape[0], out_ref.shape[0]
    i, steps = pl.program_id(0), mine_ref.shape[1] // tile

    @pl.when(i == 0)
    def _():
        for s in range(blocks):
            cots[block(block_at(place_ref, s, blocks), tokens), :] = cot_refs[s][...]

    def product(act_ref, at):
        out_ref[...] = dot(act_ref[:, block(at, tile)], cots[...], FIRST) * scale

    pl.when(i < steps)(lambda: product(mine_ref, i))
    pl.when(i >= steps)(lambda: product(theirs_ref, i - steps))


def grad_down_call(place, act_mine, act_theirs, cots, scale):
    (total, half), features = act_mine.shape, cots[0].shape[1]
    tile = tile_of(half)
    steps = half // tile

    def rows(i, place):
        core = lax.rem(place[1], 2)
        return jnp.where(i < steps, core * steps + i, (1 - core) * steps + i - steps), 0

    return call(
        functools.partial(grad_down_kernel, len(cots), scale),
        place,
        [act_mine, act_theirs, *cots],
        jax.ShapeDtypeStruct((2 * half, features), jnp.float32),
        14,
        SOME,
        grid=(2 * steps,),
        out_specs=pl.BlockSpec((tile, features), rows),
        scratch=[pltpu.VMEM((total, features), jnp.bfloat16)],
    )


def join_kernel(place_ref, *refs):
    tokens = refs[0].shape[0]
    for s, ref in enumerate(refs[:-1]):
        refs[-1][pl.ds(s * tokens, tokens), :] = ref[...]


def join_call(place, blocks):
    tokens, features = blocks[0].shape
    out = jax.ShapeDtypeStruct((tokens * len(blocks), features), blocks[0].dtype)
    return call(join_kernel, place, blocks, out, 8, MOST)


def grad_up_kernel(blocks, scale, place_ref, *refs):
    ins, refs = refs[: -2 * blocks - 3], refs[-2 * blocks - 3 :]
    mine, pair = refs[:blocks], refs[blocks : 2 * blocks]
    out_ref, inputs, grads = refs[2 * blocks :]
    tokens, half = mine[0].shape
    tile = out_ref.shape[0]

    @pl.when(pl.program_id(0) == 0)
    def _():
        left, right = block(core_of(place_ref), half), block(1 - core_of(place_ref), half)
        first = 0
        for ref in ins:
            inputs[pl.ds(first, ref.shape[0]), :] = ref[...]
            first += ref.shape[0]
        for s in range(blocks):
            here = pl.ds(s * tokens, tokens)
            grads[here, left] = mine[s][...]
            grads[here, right] = pair[s][...]

    out_ref[...] = dot(inputs[:, block(pl.program_id(0), tile)], grads[...], FIRST) * scale


def grad_up_call(place, ins, mine, pair, scale):
    total, features = sum(x.shape[0] for x in ins), ins[0].shape[1]
    hidden = 2 * mine[0].shape[1]
    tile = tile_of(features, 256)
    return call(
        functools.partial(grad_up_kernel, len(mine), scale),
        place,
        [*ins, *mine, *pair],
        jax.ShapeDtypeStruct((features, hidden), jnp.float32),
        18,
        MUCH,
        grid=(features // tile,),
        out_specs=pl.BlockSpec((tile, hidden), lambda i, place: (i, 0)),
        scratch=[
            pltpu.VMEM((total, features), jnp.bfloat16),
            pltpu.VMEM((total, hidden), jnp.bfloat16),
        ],
    )


def per_device(inputs, cotangent, preactivation, up_weight, down_weight):
    cols, rows = lax.axis_size("col"), lax.axis_size("row")
    place = jnp.stack([lax.axis_index("col"), lax.axis_index("row")]).astype(jnp.int32)
    cotangent, preactivation = after(cotangent, place), after(preactivation, place)
    ring = [(i, (i + 1) % cols) for i in range(cols)]
    pair = [(i, i ^ 1) for i in range(rows)]
    over_x = [[(i, (i + shift) % rows) for i in range(rows)] for shift in range(2, rows, 2)]
    scale = 1.0 / math.sqrt(cotangent.shape[0] * cols)
    last = cols - 1

    pre = take_half_call(place, preactivation, lax.ppermute(preactivation, "row", pair))
    pres = [pre] + [lax.ppermute(pre, "row", to) for to in over_x]
    parts, sent, others, mine, theirs = ([None] * cols for _ in range(5))

    def hidden_part(s, *first):
        own, other = hidden_call(after(place, *first), cots[s], down_weight)
        arrived = lax.ppermute(other, "row", pair)
        sent[s] = add_call(place, own, [arrived], jnp.bfloat16, LITTLE)
        parts[s] = own, arrived

    def exchange(s, *first):
        values = after(sent[s], *first)
        others[s] = [lax.ppermute(values, "row", to) for to in over_x]

    def pre_grad(s, *first):
        own, arrived = parts[s]
        total = add_call(after(place, *first), own, [arrived, *others[s]], jnp.float32, ADD_COST.get(s, MUCH))
        mine[s] = pre_grad_call(place, s, cols, pre_all, total, [])
        theirs[s] = lax.ppermute(mine[s], "row", pair)

    def share(s, *first):
        return share_call(after(place, *first), mine[s], theirs[s], up_weight, s == 1)

    cots = [cotangent]
    hidden_part(0)
    ins = [inputs, lax.ppermute(after(inputs, place), "col", ring)]
    near = join_call(place, ins)
    for s in range(1, cols):
        arriving = lax.ppermute(cots[s - 1], "col", ring)
        cots.append(after(arriving, sent[s - 1]) if s > 1 else after(arriving, pre, parts[0][0]))
        if s < last:
            hidden_part(s, *([near] if s == 2 else []))
            exchange(s)
    ins.append(lax.ppermute(after(ins[1], near, cots[last - 1]), "col", ring))
    pre_all, act = lay_out_call(place, pres)
    act_theirs = lax.ppermute(act, "row", pair)

    pre_grad(1, pre_all)
    sums = share(1)[1]
    cots[last] = after(cots[last], sums)
    hidden_part(last, sums)
    exchange(last)
    exchange(0, sent[last])
    for s in range(2, cols):
        arrived = lax.ppermute(sums, "col", ring)
        pre_grad(s, *([late] if s > 2 else []))
        if s > 2:
            ins.append(lax.ppermute(after(ins[-1], sums), "col", ring))
        first = []
        if s == last:
            grad_down = grad_down_call(
                after(place, mine[s]), act, act_theirs, cots, scale
            )
            pre_grad(0, grad_down, ins[s])
            first = [grad_down]
        if s == 2:
            arrived = add_call(place, arrived, [], jnp.float32, MOST)
        part = share(s, *first)[0]
        sums = late = add_call(place, part, [arrived], jnp.bfloat16, LITTLE)
    arrived = lax.ppermute(sums, "col", ring)
    part = share(0, sums)[0]
    grad_up = grad_up_call(after(place, part), [near, *ins[2:]], mine, theirs, scale)
    sums = add_call(after(place, grad_up), part, [arrived], jnp.bfloat16, LITTLE)
    return (sums, grad_up, grad_down)


def solution(mesh):
    placed = (
        P(("groups", "col"), "row"),
        P(("groups", "col"), "row"),
        P(("groups", "row"), "col"),
        P("row", "col"),
        P("col", "row"),
    )
    return jax.shard_map(
        per_device,
        mesh=mesh,
        in_specs=placed,
        out_specs=(
            P(("groups", "col"), "row"),
            P(("groups", "row"), "col"),
            P(("groups", "col"), "row"),
        ),
        check_vma=False,
    )
```

```python
import functools
import math

import jax
import jax.numpy as jnp
from jax import lax
from jax.experimental import pallas as pl
from jax.experimental.pallas import tpu as pltpu
from jax.sharding import PartitionSpec as P

LAST = (((1,), (1,)), ((), ()))
FIRST = (((0,), (0,)), ((), ()))
MIB = 1024 * 1024
LITTLE, SOME, MORE, MUCH, MOST = 10**7, 10**8, 10**9, 3 * 10**9, 8 * 10**9


def gelu_parts(values):
    v = values.astype(jnp.float32)
    tanh_val = jnp.tanh(0.7978845608 * (v + 0.044715 * v * v * v))
    return v, tanh_val


def gelu(values):
    v, tanh_val = gelu_parts(values)
    return 0.5 * v * (1.0 + tanh_val)


def gelu_slope(values):
    v, tanh_val = gelu_parts(values)
    return 0.5 * (1.0 + tanh_val) + 0.5 * v * (1.0 - tanh_val * tanh_val) * 0.7978845608 * (
        1.0 + 3.0 * 0.044715 * v * v
    )


def dot(a, b, dims):
    return lax.dot_general(a, b, dims, preferred_element_type=jnp.float32)


def after(value, *first):
    return lax.optimization_barrier((value, *first))[0] if first else value


def tile_of(extent, most=512):
    return next(t for t in (most, 256, 128, extent) if extent % t == 0)


def in_vmem():
    return pl.BlockSpec(memory_space=pltpu.VMEM)


def block(index, size, first=0):
    return pl.ds(pl.multiple_of(index * size + first, math.gcd(size, first)), size - first)


def ring_order(cols):
    return [*range(0, cols, 2), *reversed(range(1, cols, 2))]


def block_at(place_ref, step, cols):
    z = place_ref[0]
    turn = jnp.where(lax.rem(z, 2) == 0, lax.div(z, 2), cols - lax.div(z + 1, 2))
    turn = lax.rem(turn - step + cols, cols)
    return jnp.where(2 * turn < cols, 2 * turn, 2 * (cols - turn) - 1)


def core_of(place_ref):
    return lax.rem(place_ref[1], 2)


ADD_COST = {1: MUCH, 2: MOST}


def call(kernel, place, operands, outs, mib, cost, grid=(1,), in_specs=None, out_specs=None, scratch=()):
    return pl.pallas_call(
        kernel,
        out_shape=outs,
        grid_spec=pltpu.PrefetchScalarGridSpec(
            num_scalar_prefetch=1,
            grid=grid,
            in_specs=in_specs or [in_vmem() for _ in operands],
            out_specs=out_specs or jax.tree.map(lambda _: in_vmem(), outs),
            scratch_shapes=scratch,
        ),
        compiler_params=pltpu.CompilerParams(vmem_limit_bytes=mib * MIB),
        cost_estimate=pl.CostEstimate(flops=cost, bytes_accessed=1024, transcendentals=0),
    )(place, *operands)


def take_half_kernel(place_ref, mine_ref, theirs_ref, out_ref):
    tokens, half = mine_ref.shape[0], out_ref.shape[1]
    core = core_of(place_ref)
    out_ref[block(core, tokens), :] = mine_ref[:, block(core, half)]
    out_ref[block(1 - core, tokens), :] = theirs_ref[:, block(core, half)]


def take_half_call(place, mine, theirs):
    tokens, hidden = mine.shape
    out = jax.ShapeDtypeStruct((2 * tokens, hidden // 2), jnp.bfloat16)
    return call(take_half_kernel, place, [mine, theirs], out, 8, LITTLE)


def lay_out_kernel(chips, place_ref, *refs):
    blocks, (pre_ref, act_ref) = refs[:chips], refs[chips:]
    tokens = blocks[0].shape[0]
    rows = 64 if tokens % 64 == 0 else tokens
    for i, ref in enumerate(blocks):
        owner = lax.rem(lax.div(place_ref[1], 2) - i + chips, chips)
        pre_ref[block(owner, tokens), :] = ref[...]
        for first in range(0, tokens, rows):
            here = pl.ds(pl.multiple_of(owner * tokens + first, rows), rows)
            act_ref[here, :] = gelu(ref[pl.ds(first, rows), :]).astype(jnp.bfloat16)


def lay_out_call(place, blocks):
    tokens, half = blocks[0].shape
    out = jax.ShapeDtypeStruct((tokens * len(blocks), half), jnp.bfloat16)
    kernel = functools.partial(lay_out_kernel, len(blocks))
    return call(kernel, place, blocks, [out, out], 12, 2 * MUCH)


def hidden_kernel(place_ref, cot_ref, down_ref, own_ref, other_ref):
    half = own_ref.shape[1]
    tile = tile_of(half)
    for first in range(0, half, tile):
        here = pl.ds(first, tile)
        for core, out_ref in ((1 - core_of(place_ref), other_ref), (core_of(place_ref), own_ref)):
            rows = pl.ds(pl.multiple_of(core * half + first, tile), tile)
            part = dot(cot_ref[...], down_ref[rows, :], LAST)
            out_ref[:, here] = part.astype(out_ref.dtype)


def hidden_call(place, cot, down_weight):
    shape = (cot.shape[0], down_weight.shape[0] // 2)
    outs = [jax.ShapeDtypeStruct(shape, jnp.float32), jax.ShapeDtypeStruct(shape, jnp.bfloat16)]
    return call(hidden_kernel, place, [cot, down_weight], outs, 10, LITTLE)


def pre_grad_kernel(step, cols, place_ref, pre_ref, part_ref, *refs):
    out_ref = refs[-1]
    tokens, half = part_ref.shape
    rows = 64 if tokens % 64 == 0 else tokens
    start = block_at(place_ref, step, cols) * tokens
    for first in range(0, tokens, rows):
        here = pl.ds(first, rows)
        total = part_ref[here, :]
        for other in refs[:-1]:
            total = total + other[here, :].astype(jnp.float32)
        v = pre_ref[pl.ds(pl.multiple_of(start + first, rows), rows), :]
        out_ref[here, :] = (total * gelu_slope(v)).astype(jnp.bfloat16)


def pre_grad_call(place, step, cols, pre_all, part, others):
    out = jax.ShapeDtypeStruct(part.shape, jnp.bfloat16)
    kernel = functools.partial(pre_grad_kernel, step, cols)
    return call(kernel, place, [pre_all, part, *others], out, 8, SOME)


def share_kernel(place_ref, mine_ref, theirs_ref, up_ref, out_ref, *sent_refs):
    features, half = up_ref.shape[0], mine_ref.shape[1]
    tile = tile_of(features)
    left, right = block(core_of(place_ref), half), block(1 - core_of(place_ref), half)
    for first in range(0, features, tile):
        here = pl.ds(first, tile)
        total = dot(mine_ref[...], up_ref[here, left], LAST)
        total = total + dot(theirs_ref[...], up_ref[here, right], LAST)
        out_ref[:, here] = total
        for sent in sent_refs:
            sent[:, here] = total.astype(jnp.bfloat16)


def share_call(place, mine, theirs, up_weight, first):
    shape = (mine.shape[0], up_weight.shape[0])
    outs = [jax.ShapeDtypeStruct(shape, jnp.float32)]
    outs += [jax.ShapeDtypeStruct(shape, jnp.bfloat16)] * first
    return call(share_kernel, place, [mine, theirs, up_weight], outs, 12, LITTLE)


def add_kernel(place_ref, part_ref, *refs):
    out_ref = refs[-1]
    rows = 64 if part_ref.shape[0] % 64 == 0 else part_ref.shape[0]
    for first in range(0, part_ref.shape[0], rows):
        here = pl.ds(first, rows)
        total = part_ref[here, :].astype(jnp.float32)
        for arrived in refs[:-1]:
            total = total + arrived[here, :].astype(jnp.float32)
        out_ref[here, :] = total.astype(out_ref.dtype)


def add_call(place, part, arrived, dtype, cost):
    out = jax.ShapeDtypeStruct(part.shape, dtype)
    return call(add_kernel, place, [part, *arrived], out, 4, cost)


def grad_down_kernel(blocks, scale, place_ref, mine_ref, theirs_ref, *refs):
    cot_refs, out_ref, cots = refs[:blocks], refs[-2], refs[-1]
    tokens, tile = cot_refs[0].shape[0], out_ref.shape[0]
    i, steps = pl.program_id(0), mine_ref.shape[1] // tile

    @pl.when(i == 0)
    def _():
        for s in range(blocks):
            cots[block(block_at(place_ref, s, blocks), tokens), :] = cot_refs[s][...]

    def product(act_ref, at):
        out_ref[...] = dot(act_ref[:, block(at, tile)], cots[...], FIRST) * scale

    pl.when(i < steps)(lambda: product(mine_ref, i))
    pl.when(i >= steps)(lambda: product(theirs_ref, i - steps))


def grad_down_call(place, act_mine, act_theirs, cots, scale):
    (total, half), features = act_mine.shape, cots[0].shape[1]
    tile = tile_of(half)
    steps = half // tile

    def rows(i, place):
        core = lax.rem(place[1], 2)
        return jnp.where(i < steps, core * steps + i, (1 - core) * steps + i - steps), 0

    return call(
        functools.partial(grad_down_kernel, len(cots), scale),
        place,
        [act_mine, act_theirs, *cots],
        jax.ShapeDtypeStruct((2 * half, features), jnp.float32),
        14,
        SOME,
        grid=(2 * steps,),
        out_specs=pl.BlockSpec((tile, features), rows),
        scratch=[pltpu.VMEM((total, features), jnp.bfloat16)],
    )


def join_kernel(place_ref, *refs):
    tokens = refs[0].shape[0]
    for s, ref in enumerate(refs[:-1]):
        refs[-1][pl.ds(s * tokens, tokens), :] = ref[...]


def join_call(place, blocks):
    tokens, features = blocks[0].shape
    out = jax.ShapeDtypeStruct((tokens * len(blocks), features), blocks[0].dtype)
    return call(join_kernel, place, blocks, out, 8, MOST)


def grad_up_kernel(blocks, scale, place_ref, *refs):
    ins, refs = refs[: -2 * blocks - 3], refs[-2 * blocks - 3 :]
    mine, pair = refs[:blocks], refs[blocks : 2 * blocks]
    out_ref, inputs, grads = refs[2 * blocks :]
    tokens, half = mine[0].shape
    tile = out_ref.shape[0]

    @pl.when(pl.program_id(0) == 0)
    def _():
        left, right = block(core_of(place_ref), half), block(1 - core_of(place_ref), half)
        first = 0
        for ref in ins:
            inputs[pl.ds(first, ref.shape[0]), :] = ref[...]
            first += ref.shape[0]
        for s in range(blocks):
            here = pl.ds(s * tokens, tokens)
            grads[here, left] = mine[s][...]
            grads[here, right] = pair[s][...]

    out_ref[...] = dot(inputs[:, block(pl.program_id(0), tile)], grads[...], FIRST) * scale


def grad_up_call(place, ins, mine, pair, scale):
    total, features = sum(x.shape[0] for x in ins), ins[0].shape[1]
    hidden = 2 * mine[0].shape[1]
    tile = tile_of(features, 256)
    return call(
        functools.partial(grad_up_kernel, len(mine), scale),
        place,
        [*ins, *mine, *pair],
        jax.ShapeDtypeStruct((features, hidden), jnp.float32),
        18,
        MUCH,
        grid=(features // tile,),
        out_specs=pl.BlockSpec((tile, hidden), lambda i, place: (i, 0)),
        scratch=[
            pltpu.VMEM((total, features), jnp.bfloat16),
            pltpu.VMEM((total, hidden), jnp.bfloat16),
        ],
    )


def per_device(inputs, cotangent, preactivation, up_weight, down_weight):
    cols, rows = lax.axis_size("col"), lax.axis_size("row")
    place = jnp.stack([lax.axis_index("col"), lax.axis_index("row")]).astype(jnp.int32)
    cotangent, preactivation = after(cotangent, place), after(preactivation, place)
    stops = ring_order(cols)
    ring = [(z, stops[(i + 1) % cols]) for i, z in enumerate(stops)]
    pair = [(i, i ^ 1) for i in range(rows)]
    over_x = [[(i, (i + shift) % rows) for i in range(rows)] for shift in range(2, rows, 2)]
    scale = 1.0 / math.sqrt(cotangent.shape[0] * cols)
    last = cols - 1

    pre = take_half_call(place, preactivation, lax.ppermute(preactivation, "row", pair))
    pres = [pre] + [lax.ppermute(pre, "row", to) for to in over_x]
    parts, sent, others, mine, theirs = ([None] * cols for _ in range(5))

    def hidden_part(s, *first):
        own, other = hidden_call(after(place, *first), cots[s], down_weight)
        arrived = lax.ppermute(other, "row", pair)
        sent[s] = add_call(place, own, [arrived], jnp.bfloat16, LITTLE)
        parts[s] = own, arrived

    def exchange(s, *first):
        values = after(sent[s], *first)
        others[s] = [lax.ppermute(values, "row", to) for to in over_x]

    def pre_grad(s, *first):
        own, arrived = parts[s]
        total = add_call(after(place, *first), own, [arrived, *others[s]], jnp.float32, ADD_COST.get(s, MUCH))
        mine[s] = pre_grad_call(place, s, cols, pre_all, total, [])
        theirs[s] = lax.ppermute(mine[s], "row", pair)

    def share(s, *first):
        return share_call(after(place, *first), mine[s], theirs[s], up_weight, s == 1)

    cots = [cotangent]
    hidden_part(0)
    ins = [inputs, lax.ppermute(after(inputs, place), "col", ring)]
    near = join_call(place, ins)
    for s in range(1, cols):
        arriving = lax.ppermute(cots[s - 1], "col", ring)
        cots.append(after(arriving, sent[s - 1]) if s > 1 else after(arriving, pre, parts[0][0]))
        if s < last:
            hidden_part(s, *([near] if s == 2 else []))
            exchange(s)
    ins.append(lax.ppermute(after(ins[1], near, cots[last - 1]), "col", ring))
    pre_all, act = lay_out_call(place, pres)
    act_theirs = lax.ppermute(act, "row", pair)

    pre_grad(1, pre_all)
    sums = share(1)[1]
    cots[last] = after(cots[last], sums)
    hidden_part(last, sums)
    exchange(last)
    exchange(0, sent[last])
    for s in range(2, cols):
        arrived = lax.ppermute(sums, "col", ring)
        pre_grad(s, *([late] if s > 2 else []))
        if s > 2:
            ins.append(lax.ppermute(after(ins[-1], sums), "col", ring))
        first = []
        if s == last:
            grad_down = grad_down_call(
                after(place, mine[s]), act, act_theirs, cots, scale
            )
            pre_grad(0, grad_down, ins[s])
            first = [grad_down]
        if s == 2:
            arrived = add_call(place, arrived, [], jnp.float32, MOST)
        part = share(s, *first)[0]
        sums = late = add_call(place, part, [arrived], jnp.bfloat16, LITTLE)
    arrived = lax.ppermute(sums, "col", ring)
    part = share(0, sums)[0]
    grad_up = grad_up_call(after(place, part), [near, *ins[2:]], mine, theirs, scale)
    sums = add_call(after(place, grad_up), part, [arrived], jnp.bfloat16, LITTLE)
    return (sums, grad_up, grad_down)


def solution(mesh):
    placed = (
        P(("groups", "col"), "row"),
        P(("groups", "col"), "row"),
        P(("groups", "row"), "col"),
        P("row", "col"),
        P("col", "row"),
    )
    return jax.shard_map(
        per_device,
        mesh=mesh,
        in_specs=placed,
        out_specs=(
            P(("groups", "col"), "row"),
            P(("groups", "row"), "col"),
            P(("groups", "col"), "row"),
        ),
        check_vma=False,
    )
```

```python
import functools
import math

import jax
import jax.numpy as jnp
from jax import lax
from jax.experimental import pallas as pl
from jax.experimental.pallas import tpu as pltpu
from jax.sharding import PartitionSpec as P

LAST = (((1,), (1,)), ((), ()))
FIRST = (((0,), (0,)), ((), ()))
MIB = 1024 * 1024
LITTLE, SOME, MORE, MUCH, MOST = 10**7, 10**8, 10**9, 3 * 10**9, 8 * 10**9


def gelu_parts(values):
    v = values.astype(jnp.float32)
    tanh_val = jnp.tanh(0.7978845608 * (v + 0.044715 * v * v * v))
    return v, tanh_val


def gelu(values):
    v, tanh_val = gelu_parts(values)
    return 0.5 * v * (1.0 + tanh_val)


def gelu_slope(values):
    v, tanh_val = gelu_parts(values)
    return 0.5 * (1.0 + tanh_val) + 0.5 * v * (1.0 - tanh_val * tanh_val) * 0.7978845608 * (
        1.0 + 3.0 * 0.044715 * v * v
    )


def dot(a, b, dims):
    return lax.dot_general(a, b, dims, preferred_element_type=jnp.float32)


def after(value, *first):
    return lax.optimization_barrier((value, *first))[0] if first else value


def tile_of(extent, most=512):
    return next(t for t in (most, 256, 128, extent) if extent % t == 0)


def in_vmem():
    return pl.BlockSpec(memory_space=pltpu.VMEM)


def block(index, size, first=0):
    return pl.ds(pl.multiple_of(index * size + first, math.gcd(size, first)), size - first)


def ring_order(cols):
    return [*range(0, cols, 2), *reversed(range(1, cols, 2))]


def block_at(place_ref, step, cols):
    z = place_ref[0]
    turn = jnp.where(lax.rem(z, 2) == 0, lax.div(z, 2), cols - lax.div(z + 1, 2))
    turn = lax.rem(turn - step + cols, cols)
    return jnp.where(2 * turn < cols, 2 * turn, 2 * (cols - turn) - 1)


def core_of(place_ref):
    return lax.rem(place_ref[1], 2)


ADD_COST = {0: 3000000000, 1: 3000000000, 2: 8000000000, 3: 3000000000}


def call(kernel, place, operands, outs, mib, cost, grid=(1,), in_specs=None, out_specs=None, scratch=()):
    return pl.pallas_call(
        kernel,
        out_shape=outs,
        grid_spec=pltpu.PrefetchScalarGridSpec(
            num_scalar_prefetch=1,
            grid=grid,
            in_specs=in_specs or [in_vmem() for _ in operands],
            out_specs=out_specs or jax.tree.map(lambda _: in_vmem(), outs),
            scratch_shapes=scratch,
        ),
        compiler_params=pltpu.CompilerParams(vmem_limit_bytes=mib * MIB),
        cost_estimate=pl.CostEstimate(flops=cost, bytes_accessed=1024, transcendentals=0),
    )(place, *operands)


def take_half_kernel(place_ref, mine_ref, theirs_ref, out_ref):
    tokens, half = mine_ref.shape[0], out_ref.shape[1]
    core = core_of(place_ref)
    out_ref[block(core, tokens), :] = mine_ref[:, block(core, half)]
    out_ref[block(1 - core, tokens), :] = theirs_ref[:, block(core, half)]


def take_half_call(place, mine, theirs):
    tokens, hidden = mine.shape
    out = jax.ShapeDtypeStruct((2 * tokens, hidden // 2), jnp.bfloat16)
    return call(take_half_kernel, place, [mine, theirs], out, 8, LITTLE)


def lay_out_kernel(chips, place_ref, *refs):
    blocks, (pre_ref, act_ref) = refs[:chips], refs[chips:]
    tokens = blocks[0].shape[0]
    rows = 64 if tokens % 64 == 0 else tokens
    for i, ref in enumerate(blocks):
        owner = lax.rem(lax.div(place_ref[1], 2) - i + chips, chips)
        pre_ref[block(owner, tokens), :] = ref[...]
        for first in range(0, tokens, rows):
            here = pl.ds(pl.multiple_of(owner * tokens + first, rows), rows)
            act_ref[here, :] = gelu(ref[pl.ds(first, rows), :]).astype(jnp.bfloat16)


def lay_out_call(place, blocks):
    tokens, half = blocks[0].shape
    out = jax.ShapeDtypeStruct((tokens * len(blocks), half), jnp.bfloat16)
    kernel = functools.partial(lay_out_kernel, len(blocks))
    return call(kernel, place, blocks, [out, out], 12, 6000000000)


def hidden_kernel(place_ref, cot_ref, down_ref, own_ref, other_ref):
    half = own_ref.shape[1]
    tile = tile_of(half)
    for first in range(0, half, tile):
        here = pl.ds(first, tile)
        for core, out_ref in ((1 - core_of(place_ref), other_ref), (core_of(place_ref), own_ref)):
            rows = pl.ds(pl.multiple_of(core * half + first, tile), tile)
            part = dot(cot_ref[...], down_ref[rows, :], LAST)
            out_ref[:, here] = part.astype(out_ref.dtype)


def hidden_call(place, cot, down_weight):
    shape = (cot.shape[0], down_weight.shape[0] // 2)
    outs = [jax.ShapeDtypeStruct(shape, jnp.float32), jax.ShapeDtypeStruct(shape, jnp.bfloat16)]
    return call(hidden_kernel, place, [cot, down_weight], outs, 10, 10000000)


def pre_grad_kernel(step, cols, place_ref, pre_ref, part_ref, *refs):
    out_ref = refs[-1]
    tokens, half = part_ref.shape
    rows = 64 if tokens % 64 == 0 else tokens
    start = block_at(place_ref, step, cols) * tokens
    for first in range(0, tokens, rows):
        here = pl.ds(first, rows)
        total = part_ref[here, :]
        for other in refs[:-1]:
            total = total + other[here, :].astype(jnp.float32)
        v = pre_ref[pl.ds(pl.multiple_of(start + first, rows), rows), :]
        out_ref[here, :] = (total * gelu_slope(v)).astype(jnp.bfloat16)


def pre_grad_call(place, step, cols, pre_all, part, others):
    out = jax.ShapeDtypeStruct(part.shape, jnp.bfloat16)
    kernel = functools.partial(pre_grad_kernel, step, cols)
    return call(kernel, place, [pre_all, part, *others], out, 8, 100000000)


def share_kernel(place_ref, mine_ref, theirs_ref, up_ref, out_ref, *sent_refs):
    features, half = up_ref.shape[0], mine_ref.shape[1]
    tile = tile_of(features)
    left, right = block(core_of(place_ref), half), block(1 - core_of(place_ref), half)
    for first in range(0, features, tile):
        here = pl.ds(first, tile)
        total = dot(mine_ref[...], up_ref[here, left], LAST)
        total = total + dot(theirs_ref[...], up_ref[here, right], LAST)
        out_ref[:, here] = total
        for sent in sent_refs:
            sent[:, here] = total.astype(jnp.bfloat16)


def share_call(place, mine, theirs, up_weight, first):
    shape = (mine.shape[0], up_weight.shape[0])
    outs = [jax.ShapeDtypeStruct(shape, jnp.float32)]
    outs += [jax.ShapeDtypeStruct(shape, jnp.bfloat16)] * first
    return call(share_kernel, place, [mine, theirs, up_weight], outs, 12, 10000000)


def add_kernel(place_ref, part_ref, *refs):
    out_ref = refs[-1]
    rows = 64 if part_ref.shape[0] % 64 == 0 else part_ref.shape[0]
    for first in range(0, part_ref.shape[0], rows):
        here = pl.ds(first, rows)
        total = part_ref[here, :].astype(jnp.float32)
        for arrived in refs[:-1]:
            total = total + arrived[here, :].astype(jnp.float32)
        out_ref[here, :] = total.astype(out_ref.dtype)


def add_call(place, part, arrived, dtype, cost):
    out = jax.ShapeDtypeStruct(part.shape, dtype)
    return call(add_kernel, place, [part, *arrived], out, 4, cost)


def grad_down_kernel(blocks, scale, place_ref, mine_ref, theirs_ref, *refs):
    cot_refs, out_ref, cots = refs[:blocks], refs[-2], refs[-1]
    tokens, tile = cot_refs[0].shape[0], out_ref.shape[0]
    i, steps = pl.program_id(0), mine_ref.shape[1] // tile

    @pl.when(i == 0)
    def _():
        for s in range(blocks):
            cots[block(block_at(place_ref, s, blocks), tokens), :] = cot_refs[s][...]

    def product(act_ref, at):
        out_ref[...] = dot(act_ref[:, block(at, tile)], cots[...], FIRST) * scale

    pl.when(i < steps)(lambda: product(mine_ref, i))
    pl.when(i >= steps)(lambda: product(theirs_ref, i - steps))


def grad_down_call(place, act_mine, act_theirs, cots, scale):
    (total, half), features = act_mine.shape, cots[0].shape[1]
    tile = tile_of(half)
    steps = half // tile

    def rows(i, place):
        core = lax.rem(place[1], 2)
        return jnp.where(i < steps, core * steps + i, (1 - core) * steps + i - steps), 0

    return call(
        functools.partial(grad_down_kernel, len(cots), scale),
        place,
        [act_mine, act_theirs, *cots],
        jax.ShapeDtypeStruct((2 * half, features), jnp.float32),
        14,
        100000000,
        grid=(2 * steps,),
        out_specs=pl.BlockSpec((tile, features), rows),
        scratch=[pltpu.VMEM((total, features), jnp.bfloat16)],
    )


def join_kernel(place_ref, *refs):
    tokens = refs[0].shape[0]
    for s, ref in enumerate(refs[:-1]):
        refs[-1][pl.ds(s * tokens, tokens), :] = ref[...]


def join_call(place, blocks):
    tokens, features = blocks[0].shape
    out = jax.ShapeDtypeStruct((tokens * len(blocks), features), blocks[0].dtype)
    return call(join_kernel, place, blocks, out, 8, 8000000000)


def grad_up_kernel(blocks, scale, place_ref, *refs):
    ins, refs = refs[: -2 * blocks - 3], refs[-2 * blocks - 3 :]
    mine, pair = refs[:blocks], refs[blocks : 2 * blocks]
    out_ref, inputs, grads = refs[2 * blocks :]
    tokens, half = mine[0].shape
    tile = out_ref.shape[0]

    @pl.when(pl.program_id(0) == 0)
    def _():
        left, right = block(core_of(place_ref), half), block(1 - core_of(place_ref), half)
        first = 0
        for ref in ins:
            inputs[pl.ds(first, ref.shape[0]), :] = ref[...]
            first += ref.shape[0]
        for s in range(blocks):
            here = pl.ds(s * tokens, tokens)
            grads[here, left] = mine[s][...]
            grads[here, right] = pair[s][...]

    out_ref[...] = dot(inputs[:, block(pl.program_id(0), tile)], grads[...], FIRST) * scale


def grad_up_call(place, ins, mine, pair, scale):
    total, features = sum(x.shape[0] for x in ins), ins[0].shape[1]
    hidden = 2 * mine[0].shape[1]
    tile = tile_of(features, 256)
    return call(
        functools.partial(grad_up_kernel, len(mine), scale),
        place,
        [*ins, *mine, *pair],
        jax.ShapeDtypeStruct((features, hidden), jnp.float32),
        18,
        3000000000,
        grid=(features // tile,),
        out_specs=pl.BlockSpec((tile, hidden), lambda i, place: (i, 0)),
        scratch=[
            pltpu.VMEM((total, features), jnp.bfloat16),
            pltpu.VMEM((total, hidden), jnp.bfloat16),
        ],
    )


def per_device(inputs, cotangent, preactivation, up_weight, down_weight):
    cols, rows = lax.axis_size("col"), lax.axis_size("row")
    place = jnp.stack([lax.axis_index("col"), lax.axis_index("row")]).astype(jnp.int32)
    cotangent, preactivation = after(cotangent, place), after(preactivation, place)
    stops = ring_order(cols)
    ring = [(z, stops[(i + 1) % cols]) for i, z in enumerate(stops)]
    pair = [(i, i ^ 1) for i in range(rows)]
    over_x = [[(i, (i + shift) % rows) for i in range(rows)] for shift in range(2, rows, 2)]
    scale = 1.0 / math.sqrt(cotangent.shape[0] * cols)
    last = cols - 1

    pre = take_half_call(place, preactivation, lax.ppermute(preactivation, "row", pair))
    pres = [pre] + [lax.ppermute(pre, "row", to) for to in over_x]
    parts, sent, others, mine, theirs = ([None] * cols for _ in range(5))

    def hidden_part(s, *first):
        own, other = hidden_call(after(place, *first), cots[s], down_weight)
        arrived = lax.ppermute(other, "row", pair)
        sent[s] = add_call(place, own, [arrived], jnp.bfloat16, 10000000)
        parts[s] = own, arrived

    def exchange(s, *first):
        values = after(sent[s], *first)
        others[s] = [lax.ppermute(values, "row", to) for to in over_x]

    def pre_grad(s, *first):
        own, arrived = parts[s]
        total = add_call(after(place, *first), own, [arrived, *others[s]], jnp.float32, ADD_COST.get(s, MUCH))
        mine[s] = pre_grad_call(place, s, cols, pre_all, total, [])
        theirs[s] = lax.ppermute(mine[s], "row", pair)

    def share(s, *first):
        return share_call(after(place, *first), mine[s], theirs[s], up_weight, s == 1)

    cots = [cotangent]
    hidden_part(0)
    ins = [inputs, lax.ppermute(after(inputs, place), "col", ring)]
    near = join_call(place, ins)
    for s in range(1, cols):
        arriving = lax.ppermute(cots[s - 1], "col", ring)
        cots.append(after(arriving, sent[s - 1]) if s > 1 else after(arriving, pre, parts[0][0]))
        if s < last:
            hidden_part(s, *([near] if s == 2 else []))
            exchange(s)
    ins.append(lax.ppermute(after(ins[1], near), "col", ring))
    second = join_call(place, ins[2:])
    pre_all, act = lay_out_call(place, pres)
    act_theirs = lax.ppermute(act, "row", pair)

    pre_grad(1, pre_all)
    sums = share(1)[1]
    cots[last] = after(cots[last], sums)
    hidden_part(last, sums)
    exchange(last)
    exchange(0, sent[last])
    for s in range(2, cols):
        arrived = lax.ppermute(sums, "col", ring)
        pre_grad(s, *([late] if s > 2 else []))
        if s > 2:
            ins.append(lax.ppermute(after(ins[-1], sums), "col", ring))
        first = []
        if s == last:
            grad_down = grad_down_call(
                after(place, mine[s]), act, act_theirs, cots, scale
            )
            pre_grad(0, grad_down, ins[s])
            first = [grad_down]
        part = share(s, *first, *([second] if s == 2 else []))[0]
        sums = late = add_call(place, part, [arrived], jnp.bfloat16, LITTLE)
    arrived = lax.ppermute(sums, "col", ring)
    part = share(0, sums)[0]
    grad_up = grad_up_call(after(place, part), [near, second, *ins[3:]], mine, theirs, scale)
    sums = add_call(after(place, grad_up), part, [arrived], jnp.bfloat16, LITTLE)
    return (sums, grad_up, grad_down)


def solution(mesh):
    placed = (
        P(("groups", "col"), "row"),
        P(("groups", "col"), "row"),
        P(("groups", "row"), "col"),
        P("row", "col"),
        P("col", "row"),
    )
    return jax.shard_map(
        per_device,
        mesh=mesh,
        in_specs=placed,
        out_specs=(
            P(("groups", "col"), "row"),
            P(("groups", "row"), "col"),
            P(("groups", "col"), "row"),
        ),
        check_vma=False,
    )
```

```python
import functools
import math

import jax
import jax.numpy as jnp
from jax import lax
from jax.experimental import pallas as pl
from jax.experimental.pallas import tpu as pltpu
from jax.sharding import PartitionSpec as P

LAST = (((1,), (1,)), ((), ()))
FIRST = (((0,), (0,)), ((), ()))
MIB = 1024 * 1024
LITTLE, SOME, MORE, MUCH, MOST = 10**7, 10**8, 10**9, 3 * 10**9, 8 * 10**9


def gelu_parts(values):
    v = values.astype(jnp.float32)
    tanh_val = jnp.tanh(0.7978845608 * (v + 0.044715 * v * v * v))
    return v, tanh_val


def gelu(values):
    v, tanh_val = gelu_parts(values)
    return 0.5 * v * (1.0 + tanh_val)


def gelu_slope(values):
    v, tanh_val = gelu_parts(values)
    return 0.5 * (1.0 + tanh_val) + 0.5 * v * (1.0 - tanh_val * tanh_val) * 0.7978845608 * (
        1.0 + 3.0 * 0.044715 * v * v
    )


def dot(a, b, dims):
    return lax.dot_general(a, b, dims, preferred_element_type=jnp.float32)


def after(value, *first):
    return lax.optimization_barrier((value, *first))[0] if first else value


def tile_of(extent, most=512):
    return next(t for t in (most, 256, 128, extent) if extent % t == 0)


def in_vmem():
    return pl.BlockSpec(memory_space=pltpu.VMEM)


def block(index, size, first=0):
    return pl.ds(pl.multiple_of(index * size + first, math.gcd(size, first)), size - first)


def ring_order(cols):
    return [*range(0, cols, 2), *reversed(range(1, cols, 2))]


def block_at(place_ref, step, cols):
    z = place_ref[0]
    turn = jnp.where(lax.rem(z, 2) == 0, lax.div(z, 2), cols - lax.div(z + 1, 2))
    turn = lax.rem(turn - step + cols, cols)
    return jnp.where(2 * turn < cols, 2 * turn, 2 * (cols - turn) - 1)


def core_of(place_ref):
    return lax.rem(place_ref[1], 2)


ADD_COST = {0: 3000000000, 1: 3000000000, 2: 8000000000, 3: 3000000000}


def call(kernel, place, operands, outs, mib, cost, grid=(1,), in_specs=None, out_specs=None, scratch=()):
    return pl.pallas_call(
        kernel,
        out_shape=outs,
        grid_spec=pltpu.PrefetchScalarGridSpec(
            num_scalar_prefetch=1,
            grid=grid,
            in_specs=in_specs or [in_vmem() for _ in operands],
            out_specs=out_specs or jax.tree.map(lambda _: in_vmem(), outs),
            scratch_shapes=scratch,
        ),
        compiler_params=pltpu.CompilerParams(vmem_limit_bytes=mib * MIB),
        cost_estimate=pl.CostEstimate(flops=cost, bytes_accessed=1024, transcendentals=0),
    )(place, *operands)


def take_half_kernel(place_ref, mine_ref, theirs_ref, out_ref):
    tokens, half = mine_ref.shape[0], out_ref.shape[1]
    core = core_of(place_ref)
    out_ref[block(core, tokens), :] = mine_ref[:, block(core, half)]
    out_ref[block(1 - core, tokens), :] = theirs_ref[:, block(core, half)]


def take_half_call(place, mine, theirs):
    tokens, hidden = mine.shape
    out = jax.ShapeDtypeStruct((2 * tokens, hidden // 2), jnp.bfloat16)
    return call(take_half_kernel, place, [mine, theirs], out, 8, LITTLE)


def lay_out_kernel(chips, place_ref, *refs):
    blocks, (pre_ref, act_ref) = refs[:chips], refs[chips:]
    tokens = blocks[0].shape[0]
    rows = 64 if tokens % 64 == 0 else tokens
    for i, ref in enumerate(blocks):
        owner = lax.rem(lax.div(place_ref[1], 2) - i + chips, chips)
        pre_ref[block(owner, tokens), :] = ref[...]
        for first in range(0, tokens, rows):
            here = pl.ds(pl.multiple_of(owner * tokens + first, rows), rows)
            act_ref[here, :] = gelu(ref[pl.ds(first, rows), :]).astype(jnp.bfloat16)


def lay_out_call(place, blocks):
    tokens, half = blocks[0].shape
    out = jax.ShapeDtypeStruct((tokens * len(blocks), half), jnp.bfloat16)
    kernel = functools.partial(lay_out_kernel, len(blocks))
    return call(kernel, place, blocks, [out, out], 12, 6000000000)


def hidden_kernel(place_ref, cot_ref, down_ref, own_ref, other_ref):
    half = own_ref.shape[1]
    tile = tile_of(half)
    for first in range(0, half, tile):
        here = pl.ds(first, tile)
        for core, out_ref in ((1 - core_of(place_ref), other_ref), (core_of(place_ref), own_ref)):
            rows = pl.ds(pl.multiple_of(core * half + first, tile), tile)
            part = dot(cot_ref[...], down_ref[rows, :], LAST)
            out_ref[:, here] = part.astype(out_ref.dtype)


def hidden_call(place, cot, down_weight):
    shape = (cot.shape[0], down_weight.shape[0] // 2)
    outs = [jax.ShapeDtypeStruct(shape, jnp.float32), jax.ShapeDtypeStruct(shape, jnp.bfloat16)]
    return call(hidden_kernel, place, [cot, down_weight], outs, 10, 10000000)


def pre_grad_kernel(step, cols, place_ref, pre_ref, part_ref, *refs):
    out_ref = refs[-1]
    tokens, half = part_ref.shape
    rows = 64 if tokens % 64 == 0 else tokens
    start = block_at(place_ref, step, cols) * tokens
    for first in range(0, tokens, rows):
        here = pl.ds(first, rows)
        total = part_ref[here, :]
        for other in refs[:-1]:
            total = total + other[here, :].astype(jnp.float32)
        v = pre_ref[pl.ds(pl.multiple_of(start + first, rows), rows), :]
        out_ref[here, :] = (total * gelu_slope(v)).astype(jnp.bfloat16)


def pre_grad_call(place, step, cols, pre_all, part, others, cost):
    out = jax.ShapeDtypeStruct(part.shape, jnp.bfloat16)
    kernel = functools.partial(pre_grad_kernel, step, cols)
    return call(kernel, place, [pre_all, part, *others], out, 8, cost)


def share_kernel(place_ref, mine_ref, theirs_ref, up_ref, out_ref):
    features, half = up_ref.shape[0], mine_ref.shape[1]
    tile = tile_of(features)
    left, right = block(core_of(place_ref), half), block(1 - core_of(place_ref), half)
    for first in range(0, features, tile):
        here = pl.ds(first, tile)
        total = dot(mine_ref[...], up_ref[here, left], LAST)
        total = total + dot(theirs_ref[...], up_ref[here, right], LAST)
        out_ref[:, here] = total.astype(out_ref.dtype)


def share_call(place, mine, theirs, up_weight, dtype):
    out = jax.ShapeDtypeStruct((mine.shape[0], up_weight.shape[0]), dtype)
    return call(share_kernel, place, [mine, theirs, up_weight], out, 12, 10000000)


def add_kernel(place_ref, part_ref, *refs):
    out_ref = refs[-1]
    rows = 64 if part_ref.shape[0] % 64 == 0 else part_ref.shape[0]
    for first in range(0, part_ref.shape[0], rows):
        here = pl.ds(first, rows)
        total = part_ref[here, :].astype(jnp.float32)
        for arrived in refs[:-1]:
            total = total + arrived[here, :].astype(jnp.float32)
        out_ref[here, :] = total.astype(out_ref.dtype)


def add_call(place, part, arrived, dtype, cost):
    out = jax.ShapeDtypeStruct(part.shape, dtype)
    return call(add_kernel, place, [part, *arrived], out, 4, cost)


def grad_down_kernel(blocks, scale, place_ref, mine_ref, theirs_ref, *refs):
    cot_refs, out_ref, cots = refs[:blocks], refs[-2], refs[-1]
    tokens, tile = cot_refs[0].shape[0], out_ref.shape[0]
    i, steps = pl.program_id(0), mine_ref.shape[1] // tile

    @pl.when(i == 0)
    def _():
        for s in range(blocks):
            cots[block(block_at(place_ref, s, blocks), tokens), :] = cot_refs[s][...]

    def product(act_ref, at):
        out_ref[...] = dot(act_ref[:, block(at, tile)], cots[...], FIRST) * scale

    pl.when(i < steps)(lambda: product(mine_ref, i))
    pl.when(i >= steps)(lambda: product(theirs_ref, i - steps))


def grad_down_call(place, act_mine, act_theirs, cots, scale):
    (total, half), features = act_mine.shape, cots[0].shape[1]
    tile = tile_of(half)
    steps = half // tile

    def rows(i, place):
        core = lax.rem(place[1], 2)
        return jnp.where(i < steps, core * steps + i, (1 - core) * steps + i - steps), 0

    return call(
        functools.partial(grad_down_kernel, len(cots), scale),
        place,
        [act_mine, act_theirs, *cots],
        jax.ShapeDtypeStruct((2 * half, features), jnp.float32),
        14,
        100000000,
        grid=(2 * steps,),
        out_specs=pl.BlockSpec((tile, features), rows),
        scratch=[pltpu.VMEM((total, features), jnp.bfloat16)],
    )


def join_kernel(place_ref, *refs):
    tokens = refs[0].shape[0]
    for s, ref in enumerate(refs[:-1]):
        refs[-1][pl.ds(s * tokens, tokens), :] = ref[...]


def join_call(place, blocks):
    tokens, features = blocks[0].shape
    out = jax.ShapeDtypeStruct((tokens * len(blocks), features), blocks[0].dtype)
    return call(join_kernel, place, blocks, out, 8, 8000000000)


def grad_up_kernel(blocks, scale, place_ref, *refs):
    ins, refs = refs[: -2 * blocks - 3], refs[-2 * blocks - 3 :]
    mine, pair = refs[:blocks], refs[blocks : 2 * blocks]
    out_ref, inputs, grads = refs[2 * blocks :]
    tokens, half = mine[0].shape
    tile = out_ref.shape[0]

    @pl.when(pl.program_id(0) == 0)
    def _():
        left, right = block(core_of(place_ref), half), block(1 - core_of(place_ref), half)
        first = 0
        for ref in ins:
            inputs[pl.ds(first, ref.shape[0]), :] = ref[...]
            first += ref.shape[0]
        for s in range(blocks):
            here = pl.ds(s * tokens, tokens)
            grads[here, left] = mine[s][...]
            grads[here, right] = pair[s][...]

    out_ref[...] = dot(inputs[:, block(pl.program_id(0), tile)], grads[...], FIRST) * scale


def grad_up_call(place, ins, mine, pair, scale):
    total, features = sum(x.shape[0] for x in ins), ins[0].shape[1]
    hidden = 2 * mine[0].shape[1]
    tile = tile_of(features, 256)
    return call(
        functools.partial(grad_up_kernel, len(mine), scale),
        place,
        [*ins, *mine, *pair],
        jax.ShapeDtypeStruct((features, hidden), jnp.float32),
        18,
        3000000000,
        grid=(features // tile,),
        out_specs=pl.BlockSpec((tile, hidden), lambda i, place: (i, 0)),
        scratch=[
            pltpu.VMEM((total, features), jnp.bfloat16),
            pltpu.VMEM((total, hidden), jnp.bfloat16),
        ],
    )


def per_device(inputs, cotangent, preactivation, up_weight, down_weight):
    cols, rows = lax.axis_size("col"), lax.axis_size("row")
    place = jnp.stack([lax.axis_index("col"), lax.axis_index("row")]).astype(jnp.int32)
    cotangent, preactivation = after(cotangent, place), after(preactivation, place)
    stops = ring_order(cols)
    ring = [(z, stops[(i + 1) % cols]) for i, z in enumerate(stops)]
    pair = [(i, i ^ 1) for i in range(rows)]
    over_x = [[(i, (i + shift) % rows) for i in range(rows)] for shift in range(2, rows, 2)]
    scale = 1.0 / math.sqrt(cotangent.shape[0] * cols)
    last = cols - 1

    pre = take_half_call(place, preactivation, lax.ppermute(preactivation, "row", pair))
    pres = [pre] + [lax.ppermute(pre, "row", to) for to in over_x]
    parts, sent, others, mine, theirs = ([None] * cols for _ in range(5))

    def hidden_part(s, *first):
        own, other = hidden_call(after(place, *first), cots[s], down_weight)
        arrived = lax.ppermute(other, "row", pair)
        sent[s] = add_call(place, own, [arrived], jnp.bfloat16, 10000000)
        parts[s] = own, arrived

    def exchange(s, *first):
        values = after(sent[s], *first)
        others[s] = [lax.ppermute(values, "row", to) for to in over_x]

    def pre_grad(s, *first):
        own, arrived = parts[s]
        here, terms = after(place, *first), [arrived, *others[s]]
        mine[s] = pre_grad_call(here, s, cols, pre_all, own, terms, ADD_COST[min(s, 3)])
        theirs[s] = lax.ppermute(mine[s], "row", pair)

    def share(s, *first):
        return share_call(after(place, *first), mine[s], theirs[s], up_weight, jnp.bfloat16 if s == 1 else jnp.float32)

    cots = [cotangent]
    hidden_part(0)
    ins = [inputs, lax.ppermute(after(inputs, place), "col", ring)]
    near = join_call(place, ins)
    for s in range(1, cols):
        arriving = lax.ppermute(cots[s - 1], "col", ring)
        cots.append(after(arriving, sent[s - 1]) if s > 1 else after(arriving, pre, parts[0][0]))
        if s < last:
            hidden_part(s, *([near] if s == 2 else []))
            exchange(s)
    ins.append(lax.ppermute(after(ins[1], near), "col", ring))
    second = join_call(place, ins[2:])
    pre_all, act = lay_out_call(place, pres)
    act_theirs = lax.ppermute(act, "row", pair)

    pre_grad(1, pre_all)
    sums = share(1)
    cots[last] = after(cots[last], sums)
    hidden_part(last, sums)
    exchange(last)
    exchange(0, sent[last])
    for s in range(2, cols):
        arrived = lax.ppermute(sums, "col", ring)
        pre_grad(s, *([late] if s > 2 else []))
        if s > 2:
            ins.append(lax.ppermute(after(ins[-1], sums), "col", ring))
        first = []
        if s == last:
            grad_down = grad_down_call(
                after(place, mine[s]), act, act_theirs, cots, scale
            )
            pre_grad(0, grad_down, ins[s])
            first = [grad_down]
        part = share(s, *first, *([second] if s == 2 else []))
        sums = late = add_call(place, part, [arrived], jnp.bfloat16, LITTLE)
    arrived = lax.ppermute(sums, "col", ring)
    part = share(0, sums)
    grad_up = grad_up_call(after(place, part), [near, second, *ins[3:]], mine, theirs, scale)
    sums = add_call(after(place, grad_up), part, [arrived], jnp.bfloat16, LITTLE)
    return (sums, grad_up, grad_down)


def solution(mesh):
    placed = (
        P(("groups", "col"), "row"),
        P(("groups", "col"), "row"),
        P(("groups", "row"), "col"),
        P("row", "col"),
        P("col", "row"),
    )
    return jax.shard_map(
        per_device,
        mesh=mesh,
        in_specs=placed,
        out_specs=(
            P(("groups", "col"), "row"),
            P(("groups", "row"), "col"),
            P(("groups", "col"), "row"),
        ),
        check_vma=False,
    )
```

```python
import functools
import math

import jax
import jax.numpy as jnp
from jax import lax
from jax.experimental import pallas as pl
from jax.experimental.pallas import tpu as pltpu
from jax.sharding import PartitionSpec as P

LAST = (((1,), (1,)), ((), ()))
FIRST = (((0,), (0,)), ((), ()))
MIB = 1024 * 1024
LITTLE, SOME, MORE, MUCH, MOST = 10**7, 10**8, 10**9, 3 * 10**9, 8 * 10**9


def gelu_parts(values):
    v = values.astype(jnp.float32)
    tanh_val = jnp.tanh(0.7978845608 * (v + 0.044715 * v * v * v))
    return v, tanh_val


def gelu(values):
    v, tanh_val = gelu_parts(values)
    return 0.5 * v * (1.0 + tanh_val)


def gelu_slope(values):
    v, tanh_val = gelu_parts(values)
    return 0.5 * (1.0 + tanh_val) + 0.5 * v * (1.0 - tanh_val * tanh_val) * 0.7978845608 * (
        1.0 + 3.0 * 0.044715 * v * v
    )


def dot(a, b, dims):
    return lax.dot_general(a, b, dims, preferred_element_type=jnp.float32)


def after(value, *first):
    return lax.optimization_barrier((value, *first))[0] if first else value


def tile_of(extent, most=512):
    return next(t for t in (most, 256, 128, extent) if extent % t == 0)


def in_vmem():
    return pl.BlockSpec(memory_space=pltpu.VMEM)


def block(index, size, first=0):
    return pl.ds(pl.multiple_of(index * size + first, math.gcd(size, first)), size - first)


def ring_order(cols):
    return [*range(0, cols, 2), *reversed(range(1, cols, 2))]


def block_at(place_ref, step, cols):
    z = place_ref[0]
    turn = jnp.where(lax.rem(z, 2) == 0, lax.div(z, 2), cols - lax.div(z + 1, 2))
    turn = lax.rem(turn - step + cols, cols)
    return jnp.where(2 * turn < cols, 2 * turn, 2 * (cols - turn) - 1)


def core_of(place_ref):
    return lax.rem(place_ref[1], 2)


ADD_COST = {0: 3000000000, 1: 3000000000, 2: 8000000000, 3: 3000000000}


def call(kernel, place, operands, outs, mib, cost, grid=(1,), in_specs=None, out_specs=None, scratch=()):
    return pl.pallas_call(
        kernel,
        out_shape=outs,
        grid_spec=pltpu.PrefetchScalarGridSpec(
            num_scalar_prefetch=1,
            grid=grid,
            in_specs=in_specs or [in_vmem() for _ in operands],
            out_specs=out_specs or jax.tree.map(lambda _: in_vmem(), outs),
            scratch_shapes=scratch,
        ),
        compiler_params=pltpu.CompilerParams(vmem_limit_bytes=mib * MIB),
        cost_estimate=pl.CostEstimate(flops=cost, bytes_accessed=1024, transcendentals=0),
    )(place, *operands)


def take_half_kernel(place_ref, mine_ref, theirs_ref, out_ref):
    tokens, half = mine_ref.shape[0], out_ref.shape[1]
    core = core_of(place_ref)
    out_ref[block(core, tokens), :] = mine_ref[:, block(core, half)]
    out_ref[block(1 - core, tokens), :] = theirs_ref[:, block(core, half)]


def take_half_call(place, mine, theirs):
    tokens, hidden = mine.shape
    out = jax.ShapeDtypeStruct((2 * tokens, hidden // 2), jnp.bfloat16)
    return call(take_half_kernel, place, [mine, theirs], out, 8, LITTLE)


def lay_out_kernel(chips, place_ref, *refs):
    blocks, (pre_ref, act_ref) = refs[:chips], refs[chips:]
    tokens = blocks[0].shape[0]
    rows = 64 if tokens % 64 == 0 else tokens
    for i, ref in enumerate(blocks):
        owner = lax.rem(lax.div(place_ref[1], 2) - i + chips, chips)
        pre_ref[block(owner, tokens), :] = ref[...]
        for first in range(0, tokens, rows):
            here = pl.ds(pl.multiple_of(owner * tokens + first, rows), rows)
            act_ref[here, :] = gelu(ref[pl.ds(first, rows), :]).astype(jnp.bfloat16)


def lay_out_call(place, blocks):
    tokens, half = blocks[0].shape
    out = jax.ShapeDtypeStruct((tokens * len(blocks), half), jnp.bfloat16)
    kernel = functools.partial(lay_out_kernel, len(blocks))
    return call(kernel, place, blocks, [out, out], 12, 6000000000)


def hidden_kernel(place_ref, cot_ref, down_ref, own_ref, other_ref):
    half = own_ref.shape[1]
    tile = tile_of(half)
    for first in range(0, half, tile):
        here = pl.ds(first, tile)
        for core, out_ref in ((1 - core_of(place_ref), other_ref), (core_of(place_ref), own_ref)):
            rows = pl.ds(pl.multiple_of(core * half + first, tile), tile)
            part = dot(cot_ref[...], down_ref[rows, :], LAST)
            out_ref[:, here] = part.astype(out_ref.dtype)


def hidden_call(place, cot, down_weight):
    shape = (cot.shape[0], down_weight.shape[0] // 2)
    outs = [jax.ShapeDtypeStruct(shape, jnp.float32), jax.ShapeDtypeStruct(shape, jnp.bfloat16)]
    return call(hidden_kernel, place, [cot, down_weight], outs, 10, 10000000)


def pre_grad_kernel(step, cols, place_ref, pre_ref, part_ref, *refs):
    out_ref = refs[-1]
    tokens, half = part_ref.shape
    rows = 64 if tokens % 64 == 0 else tokens
    start = block_at(place_ref, step, cols) * tokens
    for first in range(0, tokens, rows):
        here = pl.ds(first, rows)
        total = part_ref[here, :]
        for other in refs[:-1]:
            total = total + other[here, :].astype(jnp.float32)
        v = pre_ref[pl.ds(pl.multiple_of(start + first, rows), rows), :]
        out_ref[here, :] = (total * gelu_slope(v)).astype(jnp.bfloat16)


def pre_grad_call(place, step, cols, pre_all, part, others, cost):
    out = jax.ShapeDtypeStruct(part.shape, jnp.bfloat16)
    kernel = functools.partial(pre_grad_kernel, step, cols)
    return call(kernel, place, [pre_all, part, *others], out, 8, cost)


def share_kernel(place_ref, mine_ref, theirs_ref, up_ref, out_ref):
    features, half = up_ref.shape[0], mine_ref.shape[1]
    tile = tile_of(features)
    left, right = block(core_of(place_ref), half), block(1 - core_of(place_ref), half)
    for first in range(0, features, tile):
        here = pl.ds(first, tile)
        total = dot(mine_ref[...], up_ref[here, left], LAST)
        total = total + dot(theirs_ref[...], up_ref[here, right], LAST)
        out_ref[:, here] = total.astype(out_ref.dtype)


def share_call(place, mine, theirs, up_weight, dtype):
    out = jax.ShapeDtypeStruct((mine.shape[0], up_weight.shape[0]), dtype)
    return call(share_kernel, place, [mine, theirs, up_weight], out, 12, 10000000)


def add_kernel(place_ref, part_ref, *refs):
    out_ref = refs[-1]
    rows = 64 if part_ref.shape[0] % 64 == 0 else part_ref.shape[0]
    for first in range(0, part_ref.shape[0], rows):
        here = pl.ds(first, rows)
        total = part_ref[here, :].astype(jnp.float32)
        for arrived in refs[:-1]:
            total = total + arrived[here, :].astype(jnp.float32)
        out_ref[here, :] = total.astype(out_ref.dtype)


def add_call(place, part, arrived, dtype, cost):
    out = jax.ShapeDtypeStruct(part.shape, dtype)
    return call(add_kernel, place, [part, *arrived], out, 4, cost)


def grad_down_kernel(blocks, scale, place_ref, mine_ref, theirs_ref, *refs):
    cot_refs, out_ref, cots = refs[:blocks], refs[-2], refs[-1]
    tokens, tile = cot_refs[0].shape[0], out_ref.shape[0]
    i, steps = pl.program_id(0), mine_ref.shape[1] // tile

    @pl.when(i == 0)
    def _():
        for s in range(blocks):
            cots[block(block_at(place_ref, s, blocks), tokens), :] = cot_refs[s][...]

    def product(act_ref, at):
        out_ref[...] = dot(act_ref[:, block(at, tile)], cots[...], FIRST) * scale

    pl.when(i < steps)(lambda: product(mine_ref, i))
    pl.when(i >= steps)(lambda: product(theirs_ref, i - steps))


def grad_down_call(place, act_mine, act_theirs, cots, scale):
    (total, half), features = act_mine.shape, cots[0].shape[1]
    tile = tile_of(half)
    steps = half // tile

    def rows(i, place):
        core = lax.rem(place[1], 2)
        return jnp.where(i < steps, core * steps + i, (1 - core) * steps + i - steps), 0

    return call(
        functools.partial(grad_down_kernel, len(cots), scale),
        place,
        [act_mine, act_theirs, *cots],
        jax.ShapeDtypeStruct((2 * half, features), jnp.float32),
        14,
        100000000,
        grid=(2 * steps,),
        out_specs=pl.BlockSpec((tile, features), rows),
        scratch=[pltpu.VMEM((total, features), jnp.bfloat16)],
    )


def join_kernel(place_ref, *refs):
    tokens = refs[0].shape[0]
    for s, ref in enumerate(refs[:-1]):
        refs[-1][pl.ds(s * tokens, tokens), :] = ref[...]


def join_call(place, blocks):
    tokens, features = blocks[0].shape
    out = jax.ShapeDtypeStruct((tokens * len(blocks), features), blocks[0].dtype)
    return call(join_kernel, place, blocks, out, 8, 8000000000)


def grad_up_kernel(blocks, scale, place_ref, *refs):
    ins, refs = refs[: -2 * blocks - 3], refs[-2 * blocks - 3 :]
    mine, pair = refs[:blocks], refs[blocks : 2 * blocks]
    out_ref, inputs, grads = refs[2 * blocks :]
    tokens, half = mine[0].shape
    tile = out_ref.shape[0]

    @pl.when(pl.program_id(0) == 0)
    def _():
        left, right = block(core_of(place_ref), half), block(1 - core_of(place_ref), half)
        first = 0
        for ref in ins:
            inputs[pl.ds(first, ref.shape[0]), :] = ref[...]
            first += ref.shape[0]
        for s in range(blocks):
            here = pl.ds(s * tokens, tokens)
            grads[here, left] = mine[s][...]
            grads[here, right] = pair[s][...]

    out_ref[...] = dot(inputs[:, block(pl.program_id(0), tile)], grads[...], FIRST) * scale


def grad_up_call(place, ins, mine, pair, scale):
    total, features = sum(x.shape[0] for x in ins), ins[0].shape[1]
    hidden = 2 * mine[0].shape[1]
    tile = tile_of(features, 256)
    return call(
        functools.partial(grad_up_kernel, len(mine), scale),
        place,
        [*ins, *mine, *pair],
        jax.ShapeDtypeStruct((features, hidden), jnp.float32),
        18,
        3000000000,
        grid=(features // tile,),
        out_specs=pl.BlockSpec((tile, hidden), lambda i, place: (i, 0)),
        scratch=[
            pltpu.VMEM((total, features), jnp.bfloat16),
            pltpu.VMEM((total, hidden), jnp.bfloat16),
        ],
    )


def per_device(inputs, cotangent, preactivation, up_weight, down_weight):
    cols, rows = lax.axis_size("col"), lax.axis_size("row")
    place = jnp.stack([lax.axis_index("col"), lax.axis_index("row")]).astype(jnp.int32)
    cotangent, preactivation = after(cotangent, place), after(preactivation, place)
    stops = ring_order(cols)
    ring = [(z, stops[(i + 1) % cols]) for i, z in enumerate(stops)]
    pair = [(i, i ^ 1) for i in range(rows)]
    over_x = [[(i, (i + shift) % rows) for i in range(rows)] for shift in range(2, rows, 2)]
    scale = 1.0 / math.sqrt(cotangent.shape[0] * cols)
    last = cols - 1

    pre = take_half_call(place, preactivation, lax.ppermute(preactivation, "row", pair))
    pres = [pre] + [lax.ppermute(pre, "row", to) for to in over_x]
    parts, sent, others, mine, theirs = ([None] * cols for _ in range(5))

    def hidden_part(s, *first):
        own, other = hidden_call(after(place, *first), cots[s], down_weight)
        arrived = lax.ppermute(other, "row", pair)
        sent[s] = add_call(place, own, [arrived], jnp.bfloat16, 10000000)
        parts[s] = own, arrived

    def exchange(s, *first):
        values = after(sent[s], *first)
        others[s] = [lax.ppermute(values, "row", to) for to in over_x]

    def pre_grad(s, *first):
        own, arrived = parts[s]
        here, terms = after(place, *first), [arrived, *others[s]]
        mine[s] = pre_grad_call(here, s, cols, pre_all, own, terms, ADD_COST[min(s, 3)])
        theirs[s] = lax.ppermute(mine[s], "row", pair)

    def share(s, *first):
        return share_call(after(place, *first), mine[s], theirs[s], up_weight, jnp.bfloat16 if s == 1 else jnp.float32)

    cots = [cotangent]
    hidden_part(0)
    ins = [inputs, lax.ppermute(after(inputs, place), "col", ring)]
    near = join_call(place, ins)
    for s in range(1, cols):
        arriving = lax.ppermute(cots[s - 1], "col", ring)
        cots.append(after(arriving, sent[s - 1]) if s > 1 else after(arriving, pre, parts[0][0]))
        if s < last:
            hidden_part(s, *([near] if s == 2 else []))
            exchange(s)
    ins.append(lax.ppermute(after(ins[1], near), "col", ring))
    second = join_call(place, ins[2:])
    pre_all, act = lay_out_call(place, pres)
    act_theirs = lax.ppermute(act, "row", pair)

    pre_grad(1, pre_all)
    sums = share(1)
    cots[last] = after(cots[last], sums)
    hidden_part(last, sums)
    exchange(last)
    exchange(0, sent[last])
    for s in range(2, cols):
        arrived = lax.ppermute(sums, "col", ring)
        pre_grad(s, *([late] if s > 2 else []))
        if s > 2:
            ins.append(lax.ppermute(after(ins[-1], part), "col", ring))
        first = []
        if s == last:
            grad_down = grad_down_call(
                after(place, mine[s]), act, act_theirs, cots, scale
            )
            pre_grad(0, grad_down, ins[s])
            first = [grad_down]
        part = share(s, *first, *([second] if s == 2 else []))
        sums = late = add_call(place, part, [arrived], jnp.bfloat16, LITTLE)
    arrived = lax.ppermute(sums, "col", ring)
    part = share(0, sums)
    grad_up = grad_up_call(after(place, part), [near, second, *ins[3:]], mine, theirs, scale)
    sums = add_call(after(place, grad_up), part, [arrived], jnp.bfloat16, LITTLE)
    return (sums, grad_up, grad_down)


def solution(mesh):
    placed = (
        P(("groups", "col"), "row"),
        P(("groups", "col"), "row"),
        P(("groups", "row"), "col"),
        P("row", "col"),
        P("col", "row"),
    )
    return jax.shard_map(
        per_device,
        mesh=mesh,
        in_specs=placed,
        out_specs=(
            P(("groups", "col"), "row"),
            P(("groups", "row"), "col"),
            P(("groups", "col"), "row"),
        ),
        check_vma=False,
    )
```

```python
import functools
import math

import jax
import jax.numpy as jnp
from jax import lax
from jax.experimental import pallas as pl
from jax.experimental.pallas import tpu as pltpu
from jax.sharding import PartitionSpec as P

LAST = (((1,), (1,)), ((), ()))
FIRST = (((0,), (0,)), ((), ()))
MIB = 1024 * 1024
LITTLE, SOME, MORE, MUCH, MOST = 10**7, 10**8, 10**9, 3 * 10**9, 8 * 10**9


def gelu_parts(values):
    v = values.astype(jnp.float32)
    tanh_val = jnp.tanh(0.7978845608 * (v + 0.044715 * v * v * v))
    return v, tanh_val


def gelu(values):
    v, tanh_val = gelu_parts(values)
    return 0.5 * v * (1.0 + tanh_val)


def gelu_slope(values):
    v, tanh_val = gelu_parts(values)
    return 0.5 * (1.0 + tanh_val) + 0.5 * v * (1.0 - tanh_val * tanh_val) * 0.7978845608 * (
        1.0 + 3.0 * 0.044715 * v * v
    )


def dot(a, b, dims):
    return lax.dot_general(a, b, dims, preferred_element_type=jnp.float32)


def after(value, *first):
    return lax.optimization_barrier((value, *first))[0] if first else value


def tile_of(extent, most=512):
    return next(t for t in (most, 256, 128, extent) if extent % t == 0)


def in_vmem():
    return pl.BlockSpec(memory_space=pltpu.VMEM)


def block(index, size, first=0):
    return pl.ds(pl.multiple_of(index * size + first, math.gcd(size, first)), size - first)


def ring_order(cols):
    return [*range(0, cols, 2), *reversed(range(1, cols, 2))]


def block_at(place_ref, step, cols):
    z = place_ref[0]
    turn = jnp.where(lax.rem(z, 2) == 0, lax.div(z, 2), cols - lax.div(z + 1, 2))
    turn = lax.rem(turn - step + cols, cols)
    return jnp.where(2 * turn < cols, 2 * turn, 2 * (cols - turn) - 1)


def core_of(place_ref):
    return lax.rem(place_ref[1], 2)


ADD_COST = {0: 3000000000, 1: 3000000000, 2: 8000000000, 3: 3000000000}


def call(kernel, place, operands, outs, mib, cost, grid=(1,), in_specs=None, out_specs=None, scratch=()):
    return pl.pallas_call(
        kernel,
        out_shape=outs,
        grid_spec=pltpu.PrefetchScalarGridSpec(
            num_scalar_prefetch=1,
            grid=grid,
            in_specs=in_specs or [in_vmem() for _ in operands],
            out_specs=out_specs or jax.tree.map(lambda _: in_vmem(), outs),
            scratch_shapes=scratch,
        ),
        compiler_params=pltpu.CompilerParams(vmem_limit_bytes=mib * MIB),
        cost_estimate=pl.CostEstimate(flops=cost, bytes_accessed=1024, transcendentals=0),
    )(place, *operands)


def take_half_kernel(place_ref, mine_ref, theirs_ref, out_ref):
    tokens, half = mine_ref.shape[0], out_ref.shape[1]
    core = core_of(place_ref)
    out_ref[block(core, tokens), :] = mine_ref[:, block(core, half)]
    out_ref[block(1 - core, tokens), :] = theirs_ref[:, block(core, half)]


def take_half_call(place, mine, theirs):
    tokens, hidden = mine.shape
    out = jax.ShapeDtypeStruct((2 * tokens, hidden // 2), jnp.bfloat16)
    return call(take_half_kernel, place, [mine, theirs], out, 8, LITTLE)


def lay_out_kernel(chips, place_ref, *refs):
    blocks, (pre_ref, act_ref) = refs[:chips], refs[chips:]
    tokens = blocks[0].shape[0]
    rows = 64 if tokens % 64 == 0 else tokens
    for i, ref in enumerate(blocks):
        owner = lax.rem(lax.div(place_ref[1], 2) - i + chips, chips)
        pre_ref[block(owner, tokens), :] = ref[...]
        for first in range(0, tokens, rows):
            here = pl.ds(pl.multiple_of(owner * tokens + first, rows), rows)
            act_ref[here, :] = gelu(ref[pl.ds(first, rows), :]).astype(jnp.bfloat16)


def lay_out_call(place, blocks):
    tokens, half = blocks[0].shape
    out = jax.ShapeDtypeStruct((tokens * len(blocks), half), jnp.bfloat16)
    kernel = functools.partial(lay_out_kernel, len(blocks))
    return call(kernel, place, blocks, [out, out], 12, 6000000000)


def hidden_kernel(place_ref, cot_ref, down_ref, own_ref, other_ref):
    half = own_ref.shape[1]
    tile = tile_of(half)
    for first in range(0, half, tile):
        here = pl.ds(first, tile)
        for core, out_ref in ((1 - core_of(place_ref), other_ref), (core_of(place_ref), own_ref)):
            rows = pl.ds(pl.multiple_of(core * half + first, tile), tile)
            part = dot(cot_ref[...], down_ref[rows, :], LAST)
            out_ref[:, here] = part.astype(out_ref.dtype)


def hidden_call(place, cot, down_weight):
    shape = (cot.shape[0], down_weight.shape[0] // 2)
    outs = [jax.ShapeDtypeStruct(shape, jnp.float32), jax.ShapeDtypeStruct(shape, jnp.bfloat16)]
    return call(hidden_kernel, place, [cot, down_weight], outs, 10, 10000000)


def pre_grad_kernel(step, cols, place_ref, pre_ref, part_ref, *refs):
    out_ref = refs[-1]
    tokens, half = part_ref.shape
    rows = 64 if tokens % 64 == 0 else tokens
    start = block_at(place_ref, step, cols) * tokens
    for first in range(0, tokens, rows):
        here = pl.ds(first, rows)
        total = part_ref[here, :]
        for other in refs[:-1]:
            total = total + other[here, :].astype(jnp.float32)
        v = pre_ref[pl.ds(pl.multiple_of(start + first, rows), rows), :]
        out_ref[here, :] = (total * gelu_slope(v)).astype(jnp.bfloat16)


def pre_grad_call(place, step, cols, pre_all, part, others, cost):
    out = jax.ShapeDtypeStruct(part.shape, jnp.bfloat16)
    kernel = functools.partial(pre_grad_kernel, step, cols)
    return call(kernel, place, [pre_all, part, *others], out, 8, cost)


def share_kernel(place_ref, mine_ref, theirs_ref, up_ref, out_ref):
    features, half = up_ref.shape[0], mine_ref.shape[1]
    tile = tile_of(features)
    left, right = block(core_of(place_ref), half), block(1 - core_of(place_ref), half)
    for first in range(0, features, tile):
        here = pl.ds(first, tile)
        total = dot(mine_ref[...], up_ref[here, left], LAST)
        total = total + dot(theirs_ref[...], up_ref[here, right], LAST)
        out_ref[:, here] = total.astype(out_ref.dtype)


def share_call(place, mine, theirs, up_weight, dtype):
    out = jax.ShapeDtypeStruct((mine.shape[0], up_weight.shape[0]), dtype)
    return call(share_kernel, place, [mine, theirs, up_weight], out, 12, 10000000)


def add_kernel(place_ref, part_ref, *refs):
    out_ref = refs[-1]
    rows = 64 if part_ref.shape[0] % 64 == 0 else part_ref.shape[0]
    for first in range(0, part_ref.shape[0], rows):
        here = pl.ds(first, rows)
        total = part_ref[here, :].astype(jnp.float32)
        for arrived in refs[:-1]:
            total = total + arrived[here, :].astype(jnp.float32)
        out_ref[here, :] = total.astype(out_ref.dtype)


def add_call(place, part, arrived, dtype, cost):
    out = jax.ShapeDtypeStruct(part.shape, dtype)
    return call(add_kernel, place, [part, *arrived], out, 4, cost)


def grad_down_kernel(blocks, scale, place_ref, mine_ref, theirs_ref, *refs):
    cot_refs, out_ref, cots = refs[:blocks], refs[-2], refs[-1]
    tokens, tile = cot_refs[0].shape[0], out_ref.shape[0]
    i, steps = pl.program_id(0), mine_ref.shape[1] // tile

    @pl.when(i == 0)
    def _():
        for s in range(blocks):
            cots[block(block_at(place_ref, s, blocks), tokens), :] = cot_refs[s][...]

    def product(act_ref, at):
        out_ref[...] = dot(act_ref[:, block(at, tile)], cots[...], FIRST) * scale

    pl.when(i < steps)(lambda: product(mine_ref, i))
    pl.when(i >= steps)(lambda: product(theirs_ref, i - steps))


def grad_down_call(place, act_mine, act_theirs, cots, scale):
    (total, half), features = act_mine.shape, cots[0].shape[1]
    tile = tile_of(half)
    steps = half // tile

    def rows(i, place):
        core = lax.rem(place[1], 2)
        return jnp.where(i < steps, core * steps + i, (1 - core) * steps + i - steps), 0

    return call(
        functools.partial(grad_down_kernel, len(cots), scale),
        place,
        [act_mine, act_theirs, *cots],
        jax.ShapeDtypeStruct((2 * half, features), jnp.float32),
        14,
        100000000,
        grid=(2 * steps,),
        out_specs=pl.BlockSpec((tile, features), rows),
        scratch=[pltpu.VMEM((total, features), jnp.bfloat16)],
    )


def join_kernel(place_ref, *refs):
    tokens = refs[0].shape[0]
    for s, ref in enumerate(refs[:-1]):
        refs[-1][pl.ds(s * tokens, tokens), :] = ref[...]


def join_call(place, blocks):
    tokens, features = blocks[0].shape
    out = jax.ShapeDtypeStruct((tokens * len(blocks), features), blocks[0].dtype)
    return call(join_kernel, place, blocks, out, 8, 8000000000)


def grad_up_kernel(blocks, scale, place_ref, *refs):
    ins, refs = refs[: -2 * blocks - 3], refs[-2 * blocks - 3 :]
    mine, pair = refs[:blocks], refs[blocks : 2 * blocks]
    out_ref, inputs, grads = refs[2 * blocks :]
    tokens, half = mine[0].shape
    tile = out_ref.shape[0]

    @pl.when(pl.program_id(0) == 0)
    def _():
        left, right = block(core_of(place_ref), half), block(1 - core_of(place_ref), half)
        first = 0
        for ref in ins:
            inputs[pl.ds(first, ref.shape[0]), :] = ref[...]
            first += ref.shape[0]
        for s in range(blocks):
            here = pl.ds(s * tokens, tokens)
            grads[here, left] = mine[s][...]
            grads[here, right] = pair[s][...]

    out_ref[...] = dot(inputs[:, block(pl.program_id(0), tile)], grads[...], FIRST) * scale


def grad_up_call(place, ins, mine, pair, scale):
    total, features = sum(x.shape[0] for x in ins), ins[0].shape[1]
    hidden = 2 * mine[0].shape[1]
    tile = tile_of(features)
    return call(
        functools.partial(grad_up_kernel, len(mine), scale),
        place,
        [*ins, *mine, *pair],
        jax.ShapeDtypeStruct((features, hidden), jnp.float32),
        18,
        3000000000,
        grid=(features // tile,),
        out_specs=pl.BlockSpec((tile, hidden), lambda i, place: (i, 0)),
        scratch=[
            pltpu.VMEM((total, features), jnp.bfloat16),
            pltpu.VMEM((total, hidden), jnp.bfloat16),
        ],
    )


def per_device(inputs, cotangent, preactivation, up_weight, down_weight):
    cols, rows = lax.axis_size("col"), lax.axis_size("row")
    place = jnp.stack([lax.axis_index("col"), lax.axis_index("row")]).astype(jnp.int32)
    cotangent, preactivation = after(cotangent, place), after(preactivation, place)
    stops = ring_order(cols)
    ring = [(z, stops[(i + 1) % cols]) for i, z in enumerate(stops)]
    pair = [(i, i ^ 1) for i in range(rows)]
    over_x = [[(i, (i + shift) % rows) for i in range(rows)] for shift in range(2, rows, 2)]
    scale = 1.0 / math.sqrt(cotangent.shape[0] * cols)
    last = cols - 1

    pre = take_half_call(place, preactivation, lax.ppermute(preactivation, "row", pair))
    pres = [pre] + [lax.ppermute(pre, "row", to) for to in over_x]
    parts, sent, others, mine, theirs = ([None] * cols for _ in range(5))

    def hidden_part(s, *first):
        own, other = hidden_call(after(place, *first), cots[s], down_weight)
        arrived = lax.ppermute(other, "row", pair)
        sent[s] = add_call(place, own, [arrived], jnp.bfloat16, 10000000)
        parts[s] = own, arrived

    def exchange(s, *first):
        values = after(sent[s], *first)
        others[s] = [lax.ppermute(values, "row", to) for to in over_x]

    def pre_grad(s, *first):
        own, arrived = parts[s]
        here, terms = after(place, *first), [arrived, *others[s]]
        mine[s] = pre_grad_call(here, s, cols, pre_all, own, terms, ADD_COST[min(s, 3)])
        theirs[s] = lax.ppermute(mine[s], "row", pair)

    def share(s, *first):
        return share_call(after(place, *first), mine[s], theirs[s], up_weight, jnp.bfloat16 if s == 1 else jnp.float32)

    cots = [cotangent]
    hidden_part(0)
    ins = [inputs, lax.ppermute(after(inputs, place), "col", ring)]
    near = join_call(place, ins)
    for s in range(1, cols):
        arriving = lax.ppermute(cots[s - 1], "col", ring)
        cots.append(after(arriving, sent[s - 1]) if s > 1 else after(arriving, pre, parts[0][0]))
        if s < last:
            hidden_part(s, *([near] if s == 2 else []))
            exchange(s)
    ins.append(lax.ppermute(after(ins[1], near), "col", ring))
    second = join_call(place, ins[2:])
    pre_all, act = lay_out_call(place, pres)
    act_theirs = lax.ppermute(act, "row", pair)

    pre_grad(1, pre_all)
    sums = share(1)
    cots[last] = after(cots[last], sums)
    hidden_part(last, sums)
    exchange(last)
    exchange(0, sent[last])
    for s in range(2, cols):
        arrived = lax.ppermute(sums, "col", ring)
        pre_grad(s, *([late] if s > 2 else []))
        if s > 2:
            ins.append(lax.ppermute(after(ins[-1], part), "col", ring))
        first = []
        if s == last:
            grad_down = grad_down_call(
                after(place, mine[s]), act, act_theirs, cots, scale
            )
            pre_grad(0, grad_down, ins[s])
            first = [grad_down]
        part = share(s, *first, *([second] if s == 2 else []))
        sums = late = add_call(place, part, [arrived], jnp.bfloat16, LITTLE)
    arrived = lax.ppermute(sums, "col", ring)
    part = share(0, sums)
    grad_up = grad_up_call(after(place, part), [near, second, *ins[3:]], mine, theirs, scale)
    sums = add_call(after(place, grad_up), part, [arrived], jnp.bfloat16, LITTLE)
    return (sums, grad_up, grad_down)


def solution(mesh):
    placed = (
        P(("groups", "col"), "row"),
        P(("groups", "col"), "row"),
        P(("groups", "row"), "col"),
        P("row", "col"),
        P("col", "row"),
    )
    return jax.shard_map(
        per_device,
        mesh=mesh,
        in_specs=placed,
        out_specs=(
            P(("groups", "col"), "row"),
            P(("groups", "row"), "col"),
            P(("groups", "col"), "row"),
        ),
        check_vma=False,
    )
```
